128 devices in a mesh: dp: 32 (over x, y, core), mp: 4 (over z).
Axes of the slice: x: 4, y: 4, z: 4, core: 2. Of those that a mesh axis runs over, the one named last changes fastest.
Arguments:
- context: bfloat16 [8192, 5120], P('dp', 'mp'), may hold values from -6 to 6
- residual: bfloat16 [8192, 5120], P('dp', 'mp'), may hold values from -36 to 36
- cotangent: bfloat16 [8192, 5120], P('dp', 'mp'), may hold values from -6 to 6
- out_proj: bfloat16 [5120, 5120], P(None, 'mp'), may hold values from -0.078125 to 0.078125
- norm_gain: float32 [5120], P('mp'), may hold values from 0.1 to 1.9
- rewards: float32 [128], P('dp'), may hold values from -4.2 to 10.2
- group_ids: int32 [128], P('dp'), may hold values from 0 to 7, as said below
- lengths: int32 [128], P('dp'), may hold values from 32 to 64
- destinations: int32 [2048, 1], P('dp'), may hold values from 0 to 31; in each aligned block of 64 rows (0 to 63, 64 to 127, ...) at most 3 rows name the same one
Outputs:
- d_context: bfloat16 [12288, 5120], P('dp', 'mp')
- d_residual: bfloat16 [12288, 5120], P('dp', 'mp')
- d_out_proj: float32 [5120, 5120], P('dp', 'mp')
The draws below stay inside these ranges and needn't reach their ends.
Inputs may be any that keep to these rules, and one draw needn't show every extreme that they name: `group_ids`: each prompt id is held by exactly 16 responses. `destinations`: among the 64 blocks of one owner no learner is named more than 3 times, a bound that some block reaches.
All inputs are finite; a program needn't handle non-finite values.
Results may differ from the reference program's by a relative error of at most 0.015.
Values may be sent and summed in bfloat16 or wider, within the bound.
No kernel may reach another device: no remote copies, remote signals or barrier semaphores. Data moves between devices by JAX's collectives and lax.ppermute only.
A program may use at most 128 MiB of HBM per device.

```python
import math
import jax
import jax.numpy as jnp
import numpy as np
from jax import lax

D = 5120
SEQ_DEV = 4
LMAX = 64
GROUP = 16
PAIR = 3
HQD = 5120
SEQS = 128
GROUPS = 8
ROWS = 8192
NB_DEV = 64
BLOCKS = 2048
N_DP = 32


def draw_residual(key, part):
    key = jax.random.fold_in(key, 11)
    row_key, col_key, base_key = jax.random.split(key, 3)
    row_scale = jnp.exp(jax.random.uniform(row_key, (ROWS, 1), jnp.float32, 0.0, math.log(10.0)))
    col_scale = jnp.exp(jax.random.uniform(col_key, (1, D), jnp.float32, math.log(0.3), math.log(3.0)))
    base = jnp.clip(jax.random.normal(base_key, (ROWS, D), jnp.float32), -4.0, 4.0)
    return (0.3 * base * row_scale * col_scale).astype(jnp.bfloat16)


def draw_rewards(key, part):
    key = jax.random.fold_in(key, 23)
    owners = SEQS // SEQ_DEV
    owner = (jnp.arange(SEQS) // SEQ_DEV).astype(jnp.float32)
    ramp = 1.0 + 2.0 * owner / max(owners - 1, 1)
    base = 1.0 + 0.8 * jnp.clip(jax.random.normal(key, (SEQS,), jnp.float32), -3.0, 3.0)
    return (ramp * base).astype(jnp.float32)


def draw_group_ids(key, part):
    key = jax.random.fold_in(key, 37)
    order = jax.random.permutation(key, SEQS)
    return (order // GROUP).astype(jnp.int32)


def plant(values, stream_key, least, largest):
    place = [jax.random.randint(jax.random.fold_in(stream_key, axis), (), 0, length) for axis, length in enumerate(values.shape)]
    main_axis = values.shape.index(max(values.shape))
    next_to = place[:main_axis] + [(place[main_axis] + 1) % values.shape[main_axis]] + place[main_axis + 1:]
    return values.at[tuple(place)].set(least).at[tuple(next_to)].set(largest)


def shard_levels(own_key, dims, pieces, low, largest):
    loudness = 1.0
    for dim, parts in pieces:
        draws = jax.random.uniform(jax.random.fold_in(jax.random.fold_in(own_key, 6), dim), (parts,), jnp.float32, low / len(pieces), largest / len(pieces))
        loudness = loudness * jnp.repeat(jnp.exp(draws), dims[dim] // parts).reshape((-1,) + (1,) * (len(dims) - 1 - dim))
    return loudness


def shared_out(key, own, number, rows, number_of, top, limit, lean):
    order = jax.random.permutation(key, number_of)
    crowded, common = portions_of(number_of, rows * top, limit, lean, True), portions_of(number_of, rows * top, limit, lean, False)
    places = jnp.arange(number_of)

    def named(sizes, turn):
        used = int((sizes > 0).sum())
        fixed = max(1, used // 4)
        shifted = fixed + (places - fixed + turn * (used - fixed)) % max(1, number_of - fixed)
        return jnp.zeros((number_of,), jnp.int32).at[order[jnp.where(places < fixed, places, shifted)]].set(jnp.asarray(sizes, jnp.int32))

    sizes = jnp.where(number % 4 == 0, named(crowded, number // 4), named(common, number - number // 4 - 1))
    mixed = jax.random.permutation(jax.random.fold_in(own, 3), number_of)
    donor, receiver = mixed[0:number_of // 2 * 2:2], mixed[1:number_of // 2 * 2:2]
    slack = jnp.minimum(sizes[donor] - 1, limit - sizes[receiver]) // 2
    slack = jnp.where((donor == order[0]) | (receiver == order[0]) | (sizes[receiver] == 0), 0, jnp.maximum(slack, 0))
    shifted = jax.random.randint(jax.random.fold_in(own, 4), (number_of // 2,), 0, 1 << 20) % (slack + 1)
    sizes = sizes.at[donor].add(-shifted).at[receiver].add(shifted)
    items = jnp.searchsorted(jnp.cumsum(sizes), jnp.arange(rows * top), side="right").astype(jnp.int32)
    listing = items.reshape(top, rows).T
    listing = listing[jax.random.permutation(jax.random.fold_in(own, 1), rows)]
    turn = jax.random.randint(jax.random.fold_in(own, 2), (rows, 1), 0, top)
    return jnp.take_along_axis(listing, (jnp.arange(top)[None, :] + turn) % top, axis=1)


def portions_of(number_of, total, bound, lean, full):
    portions = [(1 << 20) // math.isqrt(grade ** lean) + 1 for grade in range(1, number_of + 1)]
    largest = bound if full else min(bound, max(-(-total // number_of), total * portions[0] // sum(portions)))
    least = 1 if total - largest >= number_of - 1 else 0
    counts, spare = [largest] + [least] * (number_of - 1), total - largest - least * (number_of - 1)
    while spare > 0:
        candidates = [i for i in range(1, number_of) if counts[i] < largest] or [i for i in range(1, number_of) if counts[i] < bound]
        pool, budget = sum([portions[i] for i in candidates]), spare
        for i in candidates:
            more = min(bound - counts[i], max(1, budget * portions[i] // pool), spare)
            counts[i] = counts[i] + more
            spare = spare - more
    return np.array(counts)


def bell_draw(rng, shape, deviation, most, cuts=(), dtype=jnp.bfloat16):
    gain = shard_levels(rng, shape, cuts, -0.22, 0.18) if cuts else 1.0
    drawn = jax.random.normal(rng, shape, jnp.float32) * deviation * gain
    return jnp.minimum(jnp.maximum(drawn, -most), most).astype(dtype)


def setup_inputs(seed: int = 0) -> dict:
    key_of = jax.random.split(jax.random.key(seed), 10)
    context = bell_draw(key_of[0], (ROWS, HQD), 1.0, 6.0, ((0, 32), (1, 4)))
    residual = draw_residual(jax.random.fold_in(key_of[9], 71), 0)
    cotangent = bell_draw(key_of[2], (ROWS, D), 1.0, 6.0, ((0, 32), (1, 4)))
    out_proj = bell_draw(key_of[3], (D, HQD), HQD ** -0.5, 0.078125, ((1, 4),))
    norm_gain = jnp.clip(1.0 + 0.18 * jax.random.normal(key_of[4], (D,), jnp.float32), 0.1, 1.9)
    rewards = draw_rewards(jax.random.fold_in(key_of[9], 71), 0)
    group_ids = draw_group_ids(jax.random.fold_in(key_of[9], 71), 0)
    lengths = plant(jax.random.randint(key_of[7], (SEQS,), LMAX // 2, LMAX + 1), jax.random.fold_in(key_of[7], 1), LMAX // 2, LMAX).astype(jnp.int32)
    destinations_keys = jax.random.split(jax.random.fold_in(key_of[8], 1), BLOCKS // NB_DEV)
    destinations_turns = jax.random.permutation(jax.random.fold_in(key_of[8], 3), BLOCKS // NB_DEV)
    destinations = jax.vmap(lambda own, number: shared_out(jax.random.fold_in(key_of[8], 2), own, number, NB_DEV, N_DP, 1, PAIR, 1))(destinations_keys, destinations_turns).reshape((BLOCKS, 1))
    return {"context": context, "residual": residual, "cotangent": cotangent, "out_proj": out_proj, "norm_gain": norm_gain, "rewards": rewards, "group_ids": group_ids, "lengths": lengths, "destinations": destinations}


EPSILON = 1e-06

def slot_sources(owner_dest, slots):
    count = owner_dest.shape[0]
    same = owner_dest[:, None] == owner_dest[None, :]
    earlier = jnp.arange(count)[None, :] < jnp.arange(count)[:, None]
    rank = lax.optimization_barrier(jnp.sum((same & earlier).astype(jnp.int32), axis=1))
    target = owner_dest.astype(jnp.int32) * PAIR + rank.astype(jnp.int32)
    match = target[:, None] == jnp.arange(slots).astype(jnp.int32)[None, :]
    source = lax.optimization_barrier(jnp.sum(jnp.where(match, jnp.arange(count).astype(jnp.int32)[:, None], 0), axis=0))
    filled = jnp.any(match, axis=0)
    return (source.astype(jnp.int32), filled)

def arrange(values, source, filled, count):
    blocks = values.reshape((count, values.shape[0] // count) + values.shape[1:])
    taken = jnp.take(blocks, source, axis=0)
    shaped = filled.reshape((-1,) + (1,) * (taken.ndim - 1))
    taken = jnp.where(shaped, taken, jnp.zeros_like(taken))
    return taken.reshape((-1,) + values.shape[1:])

def learner_layout(values, destinations):
    owners = N_DP
    per_owner = values.shape[0] // owners
    blocks_dev = destinations.shape[0] // owners

    def one_owner(owner_values, owner_dest):
        source, filled = slot_sources(owner_dest, owners * PAIR)
        return arrange(owner_values, source, filled, blocks_dev)
    sent = jax.vmap(one_owner)(values.reshape((owners, per_owner) + values.shape[1:]), destinations[:, 0].reshape(owners, blocks_dev))
    sent = sent.reshape((owners, owners, -1) + values.shape[1:])
    return jnp.swapaxes(sent, 0, 1).reshape((-1,) + values.shape[1:])

def reference(context, residual, cotangent, out_proj, norm_gain, rewards, group_ids, lengths, destinations):
    member = (group_ids[:, None] == jnp.arange(GROUPS)[None, :]).astype(jnp.float32)
    group_total = lax.optimization_barrier(jnp.sum(member * rewards[:, None], axis=0))
    advantage = rewards - lax.optimization_barrier(jnp.sum(member * group_total[None, :], axis=1)) / GROUP
    scale = advantage * LMAX / (2.0 * lengths.astype(jnp.float32))
    live = jnp.arange(LMAX)[None, :] < lengths[:, None]
    row_weights = jnp.where(live, scale[:, None], jnp.float32(0.0)).reshape(-1).astype(jnp.bfloat16)
    attn = jnp.dot(context, out_proj.T, preferred_element_type=jnp.float32)
    hidden = residual.astype(jnp.float32) + attn
    upstream = norm_gain[None, :] * (row_weights.astype(jnp.float32)[:, None] * cotangent.astype(jnp.float32))
    inv_rms = lax.rsqrt(lax.optimization_barrier(jnp.sum(hidden * hidden, axis=1)) / D + EPSILON)
    coupling = lax.optimization_barrier(jnp.sum(upstream * hidden, axis=1))
    grad = (inv_rms[:, None] * upstream - hidden * (inv_rms ** 3 * coupling / D)[:, None]).astype(jnp.bfloat16)
    context_grad = jnp.dot(grad, out_proj, preferred_element_type=jnp.float32).astype(jnp.bfloat16)
    d_out_proj = jnp.dot(grad.T, context, preferred_element_type=jnp.float32) / N_DP
    d_context = learner_layout(context_grad, destinations)
    d_residual = learner_layout(grad, destinations)
    return (d_context, d_residual, d_out_proj)
```

```python
import jax
import jax.numpy as jnp
from jax import lax
from jax.sharding import Mesh
from jax.sharding import PartitionSpec as P

LMAX = 64
GROUP = 16
PAIR = 3
EPSILON = 1e-06
NX, NY, NC, NZ = 4, 4, 2, 4
DP = ("x", "y", "c")
HALF = 80
F32 = jnp.float32
BF16 = jnp.bfloat16


def shift(value, axis, step):
    size = lax.axis_size(axis)
    return lax.ppermute(value, axis, [(i, (i + step) % size) for i in range(size)])


def pick(values, index):
    return lax.dynamic_index_in_dim(values, index, 0, keepdims=False)


def group_sum(value):
    for axis, steps in (("c", (1,)), ("x", (1, 2)), ("y", (1, 2))):
        for step in steps:
            value = value + shift(value, axis, step)
    return value


def slot_matrix(owner_dest, slots, rows):
    count = owner_dest.shape[0]
    per_block = rows // count
    same = owner_dest[:, None] == owner_dest[None, :]
    earlier = jnp.arange(count)[None, :] < jnp.arange(count)[:, None]
    rank = jnp.sum((same & earlier).astype(jnp.int32), axis=1)
    target = owner_dest * PAIR + rank
    row_target = jnp.repeat(target * per_block, per_block) + jnp.tile(jnp.arange(per_block), count)
    return (jnp.arange(slots * per_block)[:, None] == row_target[None, :]).astype(BF16)


def exchange(packed, lanes):
    blocks = packed.reshape((lanes, packed.shape[0] // lanes, packed.shape[1]))
    return lax.all_to_all(blocks, DP, split_axis=0, concat_axis=0, tiled=True).reshape(packed.shape)


def per_device(
    context, residual, cotangent, out_proj, norm_gain, rewards, group_ids, lengths, destinations
):
    lanes = NX * NY * NC
    rows, width = residual.shape
    full = width * NZ
    x, y, c, z = (lax.axis_index(axis) for axis in ("x", "y", "c", "z"))

    groups = rewards.shape[0] * lanes // GROUP
    member = (group_ids[:, None] == jnp.arange(groups)[None, :]).astype(F32)
    group_total = group_sum(jnp.sum(member * rewards[:, None], axis=0))
    advantage = rewards - jnp.sum(member * group_total[None, :], axis=1) / GROUP
    scale = advantage * LMAX / (2.0 * lengths.astype(F32))
    live = jnp.arange(LMAX)[None, :] < lengths[:, None]
    row_weights = jnp.where(live, scale[:, None], F32(0.0)).reshape(-1).astype(BF16)

    proj = out_proj.reshape(NZ, width, width)

    def part(step):
        return lax.dot_general(
            pick(proj, (z + step) % NZ), context, (((1,), (1,)), ((), ())), preferred_element_type=F32
        )

    top = width // 2
    far = part(2).astype(BF16)
    far_left = shift(far[:top], "z", 1)
    far_right = shift(far[top:], "z", 3)
    near, back, own = part(1), part(3), part(0)
    near = jnp.concatenate([near[:top] + far_left.astype(F32), near[top:]], axis=0).astype(BF16)
    back = jnp.concatenate([back[:top], back[top:] + far_right.astype(F32)], axis=0).astype(BF16)
    attn_t = own + shift(near, "z", 1).astype(F32) + shift(back, "z", 3).astype(F32)

    context_x = jnp.concatenate([context] + [shift(context, "x", k) for k in (1, 2, 3)], axis=0)
    context_y = jnp.concatenate([context] + [shift(context, "y", k) for k in (1, 2, 3)], axis=0)

    hidden_t = residual.T.astype(F32) + attn_t
    upstream_t = norm_gain[:, None] * (row_weights.astype(F32)[None, :] * cotangent.T.astype(F32))
    stats = jnp.stack(
        [jnp.sum(hidden_t * hidden_t, axis=0), jnp.sum(upstream_t * hidden_t, axis=0)]
    )
    stats = stats + shift(stats, "z", 1) + shift(stats, "z", 2) + shift(stats, "z", 3)
    inv_rms = lax.rsqrt(stats[0] / full + EPSILON)
    grad_t = (
        inv_rms[None, :] * upstream_t - hidden_t * (inv_rms**3 * stats[1] / full)[None, :]
    ).astype(BF16)

    from_left, from_right = shift(grad_t, "z", 1), shift(grad_t, "z", 3)
    far_grad = jnp.concatenate(
        [shift(from_left[:top], "z", 1), shift(from_right[top:], "z", 3)], axis=0
    )
    chunks = [grad_t, from_right, far_grad, from_left]

    slots = slot_matrix(destinations[:, 0], lanes * PAIR, rows)
    d_residual = exchange(
        lax.dot_general(slots, grad_t, (((1,), (1,)), ((), ())), preferred_element_type=F32).astype(BF16),
        lanes,
    )

    grad_full = jnp.stack(chunks).reshape(NZ, NY, NC, 2, HALF, rows)
    along_x = [
        shift(pick(grad_full[:, :, :, 0], (x + k - z) % NZ).reshape(-1, rows), "x", k) if k
        else pick(grad_full[:, :, :, 0], (x - z) % NZ).reshape(-1, rows)
        for k in range(NX)
    ]
    halves_y = jnp.moveaxis(grad_full[:, :, :, 1], 1, 0)
    along_y = [
        shift(pick(halves_y, (y + k) % NY).reshape(-1, rows), "y", k) if k
        else pick(halves_y, y).reshape(-1, rows)
        for k in range(NY)
    ]
    part_x = jnp.dot(jnp.concatenate(along_x, axis=1), context_x, preferred_element_type=F32)
    part_y = jnp.dot(jnp.concatenate(along_y, axis=1), context_y, preferred_element_type=F32)

    def core_sum(value):
        value = jnp.moveaxis(value.reshape(4, NC, HALF, width), 1, 0)
        other = shift(pick(value, 1 - c).astype(BF16), "c", 1)
        return pick(value, c) + other.astype(F32)

    part_x, part_y = core_sum(part_x), core_sum(part_y)
    total_x, total_y = pick(part_x, y), pick(part_y, (x - z) % NZ)
    for k in (1, 2, 3):
        total_x = total_x + shift(pick(part_x, (y + k) % NY).astype(BF16), "y", k).astype(F32)
        total_y = total_y + shift(pick(part_y, (x + k - z) % NZ).astype(BF16), "x", k).astype(F32)
    d_out_proj = jnp.concatenate([total_x, total_y], axis=0) / lanes

    context_grad = sum(
        lax.dot_general(
            chunk, pick(proj, (z + j) % NZ), (((0,), (0,)), ((), ())), preferred_element_type=F32
        )
        for j, chunk in enumerate(chunks)
    ).astype(BF16)
    d_context = exchange(jnp.dot(slots, context_grad, preferred_element_type=F32).astype(BF16), lanes)
    return (d_context, d_residual, d_out_proj)


def solution(mesh):
    wide = Mesh(mesh.devices.reshape(NX, NY, NC, NZ), DP + ("z",))
    placed = (
        P(DP, "z"),
        P(DP, "z"),
        P(DP, "z"),
        P(None, "z"),
        P("z"),
        P(DP),
        P(DP),
        P(DP),
        P(DP, None),
    )
    return jax.shard_map(
        per_device,
        mesh=wide,
        in_specs=placed,
        out_specs=(P(DP, "z"), P(DP, "z"), P(DP, "z")),
        check_vma=False,
    )
```

```python
import jax
import jax.numpy as jnp
from jax import lax
from jax.experimental import pallas as pl
from jax.experimental.pallas import tpu as pltpu
from jax.sharding import Mesh
from jax.sharding import PartitionSpec as P

LMAX = 64
GROUP = 16
PAIR = 3
EPSILON = 1e-06
NX, NY, NC, NZ = 4, 4, 2, 4
DP = ("x", "y", "c")
HALF = 80
F32 = jnp.float32
BF16 = jnp.bfloat16


def shift(value, axis, step):
    size = lax.axis_size(axis)
    return lax.ppermute(value, axis, [(i, (i + step) % size) for i in range(size)])


def pick(values, index):
    return lax.dynamic_index_in_dim(values, index, 0, keepdims=False)


def group_sum(value):
    for axis, steps in (("c", (1,)), ("x", (1, 2)), ("y", (1, 2))):
        for step in steps:
            value = value + shift(value, axis, step)
    return value


def slot_matrix(owner_dest, slots, rows):
    count = owner_dest.shape[0]
    per_block = rows // count
    same = owner_dest[:, None] == owner_dest[None, :]
    earlier = jnp.arange(count)[None, :] < jnp.arange(count)[:, None]
    rank = jnp.sum((same & earlier).astype(jnp.int32), axis=1)
    target = owner_dest * PAIR + rank
    row_target = jnp.repeat(target * per_block, per_block) + jnp.tile(jnp.arange(per_block), count)
    return (jnp.arange(slots * per_block)[:, None] == row_target[None, :]).astype(BF16)


def exchange(packed, lanes):
    blocks = packed.reshape((lanes, packed.shape[0] // lanes, packed.shape[1]))
    return lax.all_to_all(blocks, DP, split_axis=0, concat_axis=0, tiled=True).reshape(packed.shape)


def chunk_product(out_proj, context, chunk, dtype):
    rows, width = context.shape
    tile = 256

    def body(which, proj_ref, context_ref, out_ref):
        out_ref[...] = lax.dot_general(
            proj_ref[...], context_ref[...], (((1,), (1,)), ((), ())), preferred_element_type=F32
        ).astype(dtype)

    tiles = width // tile
    return pl.pallas_call(
        body,
        out_shape=jax.ShapeDtypeStruct((width, rows), dtype),
        grid_spec=pltpu.PrefetchScalarGridSpec(
            num_scalar_prefetch=1,
            grid=(tiles,),
            in_specs=[
                pl.BlockSpec((tile, width), lambda i, which: (which[0] * tiles + i, 0)),
                pl.BlockSpec((rows, width), lambda i, which: (0, 0)),
            ],
            out_specs=pl.BlockSpec((tile, rows), lambda i, which: (i, 0)),
        ),
        cost_estimate=pl.CostEstimate(
            flops=2 * rows * width * width, bytes_accessed=2 * width * width, transcendentals=0
        ),
        name="forward_part",
    )(chunk.reshape(1), out_proj, context)


def per_device(
    context, residual, cotangent, out_proj, norm_gain, rewards, group_ids, lengths, destinations
):
    lanes = NX * NY * NC
    rows, width = residual.shape
    full = width * NZ
    x, y, c, z = (lax.axis_index(axis) for axis in ("x", "y", "c", "z"))

    groups = rewards.shape[0] * lanes // GROUP
    member = (group_ids[:, None] == jnp.arange(groups)[None, :]).astype(F32)
    group_total = group_sum(jnp.sum(member * rewards[:, None], axis=0))
    advantage = rewards - jnp.sum(member * group_total[None, :], axis=1) / GROUP
    scale = advantage * LMAX / (2.0 * lengths.astype(F32))
    live = jnp.arange(LMAX)[None, :] < lengths[:, None]
    row_weights = jnp.where(live, scale[:, None], F32(0.0)).reshape(-1).astype(BF16)

    proj = out_proj.reshape(NZ, width, width)

    def part(step, dtype=F32):
        return chunk_product(out_proj, context, (z + step) % NZ, dtype)

    top = width // 2
    far = part(2, BF16)
    far_left = shift(far[:top], "z", 1)
    far_right = shift(far[top:], "z", 3)
    near, back, own = part(1), part(3), part(0)
    near = jnp.concatenate([near[:top] + far_left.astype(F32), near[top:]], axis=0).astype(BF16)
    back = jnp.concatenate([back[:top], back[top:] + far_right.astype(F32)], axis=0).astype(BF16)
    attn_t = own + shift(near, "z", 1).astype(F32) + shift(back, "z", 3).astype(F32)

    context_x, context_y = (
        jnp.concatenate([pick(gathered, (place - k) % 4) for k in range(4)], axis=0)
        for gathered, place in (
            (lax.all_gather(context, "x", axis=0), x),
            (lax.all_gather(context, "y", axis=0), y),
        )
    )

    hidden_t = residual.T.astype(F32) + attn_t
    upstream_t = norm_gain[:, None] * (row_weights.astype(F32)[None, :] * cotangent.T.astype(F32))
    stats = jnp.stack(
        [jnp.sum(hidden_t * hidden_t, axis=0), jnp.sum(upstream_t * hidden_t, axis=0)]
    )
    stats = stats + shift(stats, "z", 1) + shift(stats, "z", 2) + shift(stats, "z", 3)
    inv_rms = lax.rsqrt(stats[0] / full + EPSILON)
    grad_t = (
        inv_rms[None, :] * upstream_t - hidden_t * (inv_rms**3 * stats[1] / full)[None, :]
    ).astype(BF16)

    from_left, from_right = shift(grad_t, "z", 1), shift(grad_t, "z", 3)
    far_grad = jnp.concatenate(
        [shift(from_left[:top], "z", 1), shift(from_right[top:], "z", 3)], axis=0
    )
    chunks = [grad_t, from_right, far_grad, from_left]

    slots = slot_matrix(destinations[:, 0], lanes * PAIR, rows)
    d_residual = exchange(
        lax.dot_general(slots, grad_t, (((1,), (1,)), ((), ())), preferred_element_type=F32).astype(BF16),
        lanes,
    )

    grad_full = jnp.stack(chunks).reshape(NZ, NY, NC, 2, HALF, rows)
    along_x = [
        shift(pick(grad_full[:, :, :, 0], (x + k - z) % NZ).reshape(-1, rows), "x", k) if k
        else pick(grad_full[:, :, :, 0], (x - z) % NZ).reshape(-1, rows)
        for k in range(NX)
    ]
    halves_y = jnp.moveaxis(grad_full[:, :, :, 1], 1, 0)
    along_y = [
        shift(pick(halves_y, (y + k) % NY).reshape(-1, rows), "y", k) if k
        else pick(halves_y, y).reshape(-1, rows)
        for k in range(NY)
    ]
    part_x = jnp.dot(jnp.concatenate(along_x, axis=1), context_x, preferred_element_type=F32)
    part_y = jnp.dot(jnp.concatenate(along_y, axis=1), context_y, preferred_element_type=F32)

    def core_sum(value):
        value = jnp.moveaxis(value.reshape(4, NC, HALF, width), 1, 0)
        other = shift(pick(value, 1 - c).astype(BF16), "c", 1)
        return pick(value, c) + other.astype(F32)

    part_x, part_y = core_sum(part_x), core_sum(part_y)
    total_x, total_y = pick(part_x, y), pick(part_y, (x - z) % NZ)
    for k in (1, 2, 3):
        total_x = total_x + shift(pick(part_x, (y + k) % NY).astype(BF16), "y", k).astype(F32)
        total_y = total_y + shift(pick(part_y, (x + k - z) % NZ).astype(BF16), "x", k).astype(F32)
    d_out_proj = jnp.concatenate([total_x, total_y], axis=0) / lanes

    context_grad = sum(
        lax.dot_general(
            chunk, pick(proj, (z + j) % NZ), (((0,), (0,)), ((), ())), preferred_element_type=F32
        )
        for j, chunk in enumerate(chunks)
    ).astype(BF16)
    d_context = exchange(jnp.dot(slots, context_grad, preferred_element_type=F32).astype(BF16), lanes)
    return (d_context, d_residual, d_out_proj)


def solution(mesh):
    wide = Mesh(mesh.devices.reshape(NX, NY, NC, NZ), DP + ("z",))
    placed = (
        P(DP, "z"),
        P(DP, "z"),
        P(DP, "z"),
        P(None, "z"),
        P("z"),
        P(DP),
        P(DP),
        P(DP),
        P(DP, None),
    )
    return jax.shard_map(
        per_device,
        mesh=wide,
        in_specs=placed,
        out_specs=(P(DP, "z"), P(DP, "z"), P(DP, "z")),
        check_vma=False,
    )
```

```python
import jax
import jax.numpy as jnp
from jax import lax
from jax.sharding import Mesh
from jax.sharding import PartitionSpec as P

LMAX = 64
GROUP = 16
PAIR = 3
EPSILON = 1e-06
NX, NY, NC, NZ = 4, 4, 2, 4
DP = ("x", "y", "c")
F32 = jnp.float32
BF16 = jnp.bfloat16


def shift(value, axis, step):
    size = lax.axis_size(axis)
    return lax.ppermute(value, axis, [(i, (i + step) % size) for i in range(size)])


def pick(values, index):
    return lax.dynamic_index_in_dim(values, index, 0, keepdims=False)


def cross(value, step, first):
    pairs = []
    for x in range(NX):
        for y in range(NY):
            for c in range(NC):
                along_y = (c == 0) == first
                to = (x, (y + step) % NY, c) if along_y else ((x + step) % NX, y, c)
                pairs.append(((x * NY + y) * NC + c, (to[0] * NY + to[1]) * NC + to[2]))
    return lax.ppermute(value, DP, pairs)


def group_sum(value):
    copies = jnp.broadcast_to(value, (NX * NY * NC,) + value.shape)
    return jnp.sum(lax.all_to_all(copies, DP, split_axis=0, concat_axis=0, tiled=True), axis=0)


def slot_matrix(owner_dest, slots, rows):
    count = owner_dest.shape[0]
    per_block = rows // count
    same = owner_dest[:, None] == owner_dest[None, :]
    earlier = jnp.arange(count)[None, :] < jnp.arange(count)[:, None]
    rank = jnp.sum((same & earlier).astype(jnp.int32), axis=1)
    target = owner_dest * PAIR + rank
    row_target = jnp.repeat(target * per_block, per_block) + jnp.tile(jnp.arange(per_block), count)
    return (jnp.arange(slots * per_block)[:, None] == row_target[None, :]).astype(BF16)


def exchange(packed, lanes):
    blocks = packed.reshape((lanes, packed.shape[0] // lanes, packed.shape[1]))
    return lax.all_to_all(blocks, DP, split_axis=0, concat_axis=0, tiled=True).reshape(packed.shape)


def per_device(
    context, residual, cotangent, out_proj, norm_gain, rewards, group_ids, lengths, destinations
):
    lanes = NX * NY * NC
    rows, width = residual.shape
    full = width * NZ
    x, y, c, z = (lax.axis_index(axis) for axis in ("x", "y", "c", "z"))

    groups = rewards.shape[0] * lanes // GROUP
    member = (group_ids[:, None] == jnp.arange(groups)[None, :]).astype(F32)
    group_total = group_sum(jnp.sum(member * rewards[:, None], axis=0))
    advantage = rewards - jnp.sum(member * group_total[None, :], axis=1) / GROUP
    scale = advantage * LMAX / (2.0 * lengths.astype(F32))
    live = jnp.arange(LMAX)[None, :] < lengths[:, None]
    row_weights = jnp.where(live, scale[:, None], F32(0.0)).reshape(-1).astype(BF16)

    proj = out_proj.reshape(NZ, width, width)

    def part(step):
        return lax.dot_general(
            pick(proj, (z + step) % NZ), context, (((1,), (1,)), ((), ())), preferred_element_type=F32
        )

    top = width // 2
    far = part(2).astype(BF16)
    far_left = shift(far[:top], "z", 1)
    far_right = shift(far[top:], "z", 3)
    near, back, own = part(1), part(3), part(0)
    near = jnp.concatenate([near[:top] + far_left.astype(F32), near[top:]], axis=0).astype(BF16)
    back = jnp.concatenate([back[:top], back[top:] + far_right.astype(F32)], axis=0).astype(BF16)
    near, back, own = lax.optimization_barrier((near, back, own))
    attn_t = own + shift(near, "z", 1).astype(F32) + shift(back, "z", 3).astype(F32)

    early, _ = lax.optimization_barrier((context, far))
    others = [context, cross(early, 1, True), None, cross(early, 3, True)]
    selves = [context, cross(early, 1, False), None, None]
    late, _ = lax.optimization_barrier((context, near))
    others[2] = cross(late, 2, True)
    selves[2], selves[3] = cross(late, 2, False), cross(late, 3, False)

    attn_t, others[1], others[3], selves[1] = lax.optimization_barrier(
        (attn_t, others[1], others[3], selves[1])
    )
    hidden_t = residual.T.astype(F32) + attn_t
    upstream_t = norm_gain[:, None] * (row_weights.astype(F32)[None, :] * cotangent.T.astype(F32))
    stats = jnp.stack(
        [jnp.sum(hidden_t * hidden_t, axis=0), jnp.sum(upstream_t * hidden_t, axis=0)]
    )
    stats = stats + shift(stats, "z", 1) + shift(stats, "z", 2) + shift(stats, "z", 3)
    inv_rms = lax.rsqrt(stats[0] / full + EPSILON)
    grad_t = (
        inv_rms[None, :] * upstream_t - hidden_t * (inv_rms**3 * stats[1] / full)[None, :]
    ).astype(BF16)
    grad_t, others[2], selves[2], selves[3] = lax.optimization_barrier(
        (grad_t, others[2], selves[2], selves[3])
    )

    def context_part(step, chunk):
        return lax.dot_general(
            chunk, pick(proj, (z + step) % NZ), (((0,), (0,)), ((), ())), preferred_element_type=F32
        )

    slots = slot_matrix(destinations[:, 0], lanes * PAIR, rows)
    from_left, from_right = shift(grad_t, "z", 1), shift(grad_t, "z", 3)
    packed = lax.dot_general(
        slots, grad_t, (((1,), (1,)), ((), ())), preferred_element_type=F32
    ).astype(BF16)
    d_residual = exchange(packed, lanes)
    context_grad = context_part(0, grad_t)
    from_left, from_right, context_grad = lax.optimization_barrier(
        (from_left, from_right, context_grad)
    )
    far_grad = jnp.concatenate(
        [shift(from_left[:top], "z", 1), shift(from_right[top:], "z", 3)], axis=0
    )
    context_grad = context_grad + context_part(1, from_right) + context_part(3, from_left)
    far_grad, context_grad = lax.optimization_barrier((far_grad, context_grad))

    block = width // (NY * NC)
    grad_full = jnp.stack([grad_t, from_right, far_grad, from_left]).reshape(NZ, NY, NC, block, rows)

    def set_rows(step, first):
        along_x = pick(grad_full[:, :, 0], (x + step - z) % NZ)
        along_y = lax.dynamic_index_in_dim(grad_full[:, :, 1], (y + step) % NY, 1, keepdims=False)
        return jnp.where((c == 0) == first, along_y, along_x).reshape(-1, rows)

    def partial_sum(first, contexts):
        pieces = [set_rows(0, first)] + [cross(set_rows(k, first), k, first) for k in (1, 2, 3)]
        return jnp.dot(
            jnp.concatenate(pieces, axis=1),
            jnp.concatenate(contexts, axis=0),
            preferred_element_type=F32,
        )

    other = shift(partial_sum(True, others).astype(BF16), "c", 1)
    total = partial_sum(False, selves) + other.astype(F32)
    total = total.reshape(4, block, width)

    def place(step):
        return pick(total, jnp.where(c == 0, (y + step) % NY, (x + step - z) % NZ))

    d_out_proj = place(0)
    for k in (1, 2, 3):
        d_out_proj = d_out_proj + cross(place(k).astype(BF16), k, True).astype(F32)
    d_out_proj = d_out_proj / lanes

    context_grad = (context_grad + context_part(2, far_grad)).astype(BF16)
    d_context = exchange(jnp.dot(slots, context_grad, preferred_element_type=F32).astype(BF16), lanes)
    return (d_context, d_residual, d_out_proj)


def solution(mesh):
    wide = Mesh(mesh.devices.reshape(NX, NY, NC, NZ), DP + ("z",))
    placed = (
        P(DP, "z"),
        P(DP, "z"),
        P(DP, "z"),
        P(None, "z"),
        P("z"),
        P(DP),
        P(DP),
        P(DP),
        P(DP, None),
    )
    return jax.shard_map(
        per_device,
        mesh=wide,
        in_specs=placed,
        out_specs=(P(DP, "z"), P(DP, "z"), P(DP, "z")),
        check_vma=False,
    )
```

```python
import jax
import jax.numpy as jnp
from jax import lax
from jax.experimental import pallas as pl
from jax.experimental.pallas import tpu as pltpu
from jax.sharding import Mesh
from jax.sharding import PartitionSpec as P

LMAX = 64
GROUP = 16
PAIR = 3
BLOCK_ROWS = 4
EPSILON = 1e-06
NX, NY, NC, NZ = 4, 4, 2, 4
DP = ("x", "y", "c")
F32 = jnp.float32
BF16 = jnp.bfloat16


def shift(value, axis, step):
    size = lax.axis_size(axis)
    return lax.ppermute(value, axis, [(i, (i + step) % size) for i in range(size)])


def pick(values, index):
    return lax.dynamic_index_in_dim(values, index, 0, keepdims=False)


def cross(value, step, first):
    pairs = []
    for x in range(NX):
        for y in range(NY):
            for c in range(NC):
                along_y = (c == 0) == first
                to = (x, (y + step) % NY, c) if along_y else ((x + step) % NX, y, c)
                pairs.append(((x * NY + y) * NC + c, (to[0] * NY + to[1]) * NC + to[2]))
    return lax.ppermute(value, DP, pairs)


def group_sum(value):
    copies = jnp.broadcast_to(value, (NX * NY * NC,) + value.shape)
    return jnp.sum(lax.all_to_all(copies, DP, split_axis=0, concat_axis=0, tiled=True), axis=0)


def slot_matrix(owner_dest, slots, rows, padded):
    count = owner_dest.shape[0]
    per_block = rows // count
    same = owner_dest[:, None] == owner_dest[None, :]
    earlier = jnp.arange(count)[None, :] < jnp.arange(count)[:, None]
    rank = jnp.sum((same & earlier).astype(jnp.int32), axis=1)
    target = owner_dest * padded + rank * per_block
    row_target = jnp.repeat(target, per_block) + jnp.tile(jnp.arange(per_block), count)
    return (jnp.arange(slots // PAIR * padded)[:, None] == row_target[None, :]).astype(BF16)


def exchange(packed, lanes):
    blocks = packed.reshape((lanes, packed.shape[0] // lanes, packed.shape[1]))
    got = lax.all_to_all(blocks, DP, split_axis=0, concat_axis=0, tiled=True)
    kept = PAIR * BLOCK_ROWS
    return got[:, :kept].reshape(lanes * kept, packed.shape[1])


FREE = pl.CostEstimate(flops=0, bytes_accessed=0, transcendentals=0)
PARAMS = pltpu.CompilerParams(vmem_limit_bytes=48 * 1024 * 1024)


def context_product(chunks, places, out_proj, before=None, slots=None):
    width, rows = chunks[0].shape
    count, tile = len(chunks), 640
    dtype = F32 if slots is None else BF16

    def body(which, *refs):
        refs = list(refs)
        out_ref = refs.pop()
        total = sum(
            lax.dot_general(
                refs[i][...], refs[count + i][...], (((0,), (0,)), ((), ())), preferred_element_type=F32
            )
            for i in range(count)
        )
        if before is not None:
            total = total + refs[2 * count][...]
        if slots is not None:
            total = jnp.dot(refs[-1][...], total.astype(BF16), preferred_element_type=F32)
        out_ref[...] = total.astype(dtype)

    in_specs = [pl.BlockSpec((width, rows), lambda n, which: (0, 0)) for _ in chunks]
    in_specs += [
        pl.BlockSpec((width, tile), lambda n, which, i=i: (which[i], n)) for i in range(count)
    ]
    operands = list(chunks) + [out_proj] * count
    out_rows = rows
    if before is not None:
        in_specs.append(pl.BlockSpec((rows, tile), lambda n, which: (0, n)))
        operands.append(before)
    if slots is not None:
        in_specs.append(pl.BlockSpec(slots.shape, lambda n, which: (0, 0)))
        operands.append(slots)
        out_rows = slots.shape[0]
    return pl.pallas_call(
        body,
        out_shape=jax.ShapeDtypeStruct((out_rows, width), dtype),
        grid_spec=pltpu.PrefetchScalarGridSpec(
            num_scalar_prefetch=1,
            grid=(width // tile,),
            in_specs=in_specs,
            out_specs=pl.BlockSpec((out_rows, tile), lambda n, which: (0, n)),
        ),
        cost_estimate=FREE,
        compiler_params=PARAMS,
        name="context_product",
    )(jnp.stack(places), *operands)


def place_rows(slots, grad_t):
    def body(slots_ref, grad_ref, out_ref):
        out_ref[...] = lax.dot_general(
            slots_ref[...], grad_ref[...], (((1,), (1,)), ((), ())), preferred_element_type=F32
        ).astype(BF16)

    return pl.pallas_call(
        body,
        out_shape=jax.ShapeDtypeStruct((slots.shape[0], grad_t.shape[0]), BF16),
        cost_estimate=FREE,
        compiler_params=PARAMS,
        name="place_rows",
    )(slots, grad_t)


def weight_product(pieces, contexts, before=None):
    count, height, tile = len(pieces), pieces[0].shape[0], 640
    rows, width = contexts[0].shape

    def body(*refs):
        total = sum(
            jnp.dot(refs[i][...], refs[count + i][...], preferred_element_type=F32)
            for i in range(count)
        )
        if before is not None:
            total = total + refs[2 * count][...].astype(F32)
        refs[-1][...] = total.astype(BF16)

    in_specs = [pl.BlockSpec((height, rows), lambda n: (0, 0)) for _ in pieces]
    in_specs += [pl.BlockSpec((rows, tile), lambda n: (0, n)) for _ in contexts]
    operands = list(pieces) + list(contexts)
    if before is not None:
        in_specs.append(pl.BlockSpec((height, tile), lambda n: (0, n)))
        operands.append(before)
    return pl.pallas_call(
        body,
        out_shape=jax.ShapeDtypeStruct((height, width), BF16),
        grid=(width // tile,),
        in_specs=in_specs,
        out_specs=pl.BlockSpec((height, tile), lambda n: (0, n)),
        cost_estimate=FREE,
        compiler_params=PARAMS,
        name="weight_product",
    )(*operands)


def per_device(
    context, residual, cotangent, out_proj, norm_gain, rewards, group_ids, lengths, destinations
):
    lanes = NX * NY * NC
    rows, width = residual.shape
    full = width * NZ
    x, y, c, z = (lax.axis_index(axis) for axis in ("x", "y", "c", "z"))

    groups = rewards.shape[0] * lanes // GROUP
    member = (group_ids[:, None] == jnp.arange(groups)[None, :]).astype(F32)
    group_total = group_sum(jnp.sum(member * rewards[:, None], axis=0))
    advantage = rewards - jnp.sum(member * group_total[None, :], axis=1) / GROUP
    scale = advantage * LMAX / (2.0 * lengths.astype(F32))
    live = jnp.arange(LMAX)[None, :] < lengths[:, None]
    row_weights = jnp.where(live, scale[:, None], F32(0.0)).reshape(-1).astype(BF16)

    proj = out_proj.reshape(NZ, width, width)

    def part(step, rows_in):
        return lax.dot_general(
            pick(proj, (z + step) % NZ), rows_in, (((1,), (1,)), ((), ())), preferred_element_type=F32
        )

    far = part(2, context).astype(BF16)
    near = part(1, lax.optimization_barrier((context, far))[0]).astype(BF16)
    back = part(3, lax.optimization_barrier((context, near))[0]).astype(BF16)
    parts = [shift(far, "z", 2), shift(near, "z", 1), shift(back, "z", 3)]

    after, _ = lax.optimization_barrier((context, near))
    others, selves = [context] * 4, [context] * 4
    others[1], others[3] = cross(after, 1, True), cross(after, 3, True)
    after, others[1], others[3] = lax.optimization_barrier((context, others[1], others[3]))
    own = part(0, after)
    others[2], selves[1] = cross(after, 2, True), cross(after, 1, False)
    after, others[2], selves[1] = lax.optimization_barrier((context, others[2], selves[1]))
    selves[2], selves[3] = cross(after, 2, False), cross(after, 3, False)

    attn_t = own + sum(value.astype(F32) for value in parts)
    attn_t, others[2], selves[1] = lax.optimization_barrier((attn_t, others[2], selves[1]))
    hidden_t = residual.T.astype(F32) + attn_t
    upstream_t = norm_gain[:, None] * (row_weights.astype(F32)[None, :] * cotangent.T.astype(F32))
    stats = jnp.stack(
        [jnp.sum(hidden_t * hidden_t, axis=0), jnp.sum(upstream_t * hidden_t, axis=0)]
    )
    stats = stats + shift(stats, "z", 1) + shift(stats, "z", 2) + shift(stats, "z", 3)
    inv_rms = lax.rsqrt(stats[0] / full + EPSILON)
    grad_t = (
        inv_rms[None, :] * upstream_t - hidden_t * (inv_rms**3 * stats[1] / full)[None, :]
    ).astype(BF16)
    grad_t, selves[2], selves[3] = lax.optimization_barrier((grad_t, selves[2], selves[3]))

    slots = slot_matrix(destinations[:, 0], lanes * PAIR, rows, 16)
    top = width // 2
    from_left, from_right = shift(grad_t, "z", 1), shift(grad_t, "z", 3)
    d_residual = exchange(place_rows(slots, grad_t), lanes)
    context_grad = context_product([grad_t], [z], out_proj)
    from_left, from_right, context_grad = lax.optimization_barrier(
        (from_left, from_right, context_grad)
    )
    far_left, far_right = shift(from_left[:top], "z", 1), shift(from_right[top:], "z", 3)
    context_grad = context_product(
        [from_right, from_left], [(z + 1) % NZ, (z + 3) % NZ], out_proj, before=context_grad
    )
    far_left, far_right, context_grad, d_residual = lax.optimization_barrier(
        (far_left, far_right, context_grad, d_residual)
    )
    far_grad = jnp.concatenate([far_left, far_right], axis=0)

    block = width // (NY * NC)
    grad_full = jnp.stack([grad_t, from_right, far_grad, from_left]).reshape(NZ, NY, NC, block, rows)

    def set_rows(step, first):
        along_x = pick(grad_full[:, :, 0], (x + step - z) % NZ)
        along_y = lax.dynamic_index_in_dim(grad_full[:, :, 1], (y + step) % NY, 1, keepdims=False)
        return jnp.where((c == 0) == first, along_y, along_x).reshape(-1, rows)

    def gather(first):
        return [set_rows(0, first)] + [cross(set_rows(k, first), k, first) for k in (1, 2, 3)]

    other_rows, self_rows = gather(True), gather(False)
    d_context = exchange(
        context_product([far_grad], [(z + 2) % NZ], out_proj, before=context_grad, slots=slots), lanes
    )
    other = shift(weight_product(other_rows, others), "c", 1)
    total = weight_product(self_rows, selves, before=other).reshape(4, block, width)

    def place(step):
        return pick(total, jnp.where(c == 0, (y + step) % NY, (x + step - z) % NZ))

    d_out_proj = place(0).astype(F32)
    for k in (1, 2, 3):
        d_out_proj = d_out_proj + cross(place(k), k, True).astype(F32)
    return (d_context, d_residual, d_out_proj / lanes)


def solution(mesh):
    wide = Mesh(mesh.devices.reshape(NX, NY, NC, NZ), DP + ("z",))
    placed = (
        P(DP, "z"),
        P(DP, "z"),
        P(DP, "z"),
        P(None, "z"),
        P("z"),
        P(DP),
        P(DP),
        P(DP),
        P(DP, None),
    )
    return jax.shard_map(
        per_device,
        mesh=wide,
        in_specs=placed,
        out_specs=(P(DP, "z"), P(DP, "z"), P(DP, "z")),
        check_vma=False,
    )
```

```python
import jax
import jax.numpy as jnp
from jax import lax
from jax.experimental import pallas as pl
from jax.experimental.pallas import tpu as pltpu
from jax.sharding import Mesh
from jax.sharding import PartitionSpec as P

LMAX = 64
GROUP = 16
PAIR = 3
BLOCK_ROWS = 4
EPSILON = 1e-06
NX, NY, NC, NZ = 4, 4, 2, 4
DP = ("x", "y", "c")
F32 = jnp.float32
BF16 = jnp.bfloat16


def shift(value, axis, step):
    size = lax.axis_size(axis)
    return lax.ppermute(value, axis, [(i, (i + step) % size) for i in range(size)])


def pick(values, index):
    return lax.dynamic_index_in_dim(values, index, 0, keepdims=False)


def cross(value, step, first):
    pairs = []
    for x in range(NX):
        for y in range(NY):
            for c in range(NC):
                along_x = (c == 0) == first
                to = ((x + step) % NX, y, c) if along_x else (x, (y + step) % NY, c)
                pairs.append(((x * NY + y) * NC + c, (to[0] * NY + to[1]) * NC + to[2]))
    return lax.ppermute(value, DP, pairs)


def group_sum(value):
    copies = jnp.broadcast_to(value, (NX * NY * NC,) + value.shape)
    return jnp.sum(lax.all_to_all(copies, DP, split_axis=0, concat_axis=0, tiled=True), axis=0)


def slot_matrix(owner_dest, slots, rows, padded):
    count = owner_dest.shape[0]
    per_block = rows // count
    same = owner_dest[:, None] == owner_dest[None, :]
    earlier = jnp.arange(count)[None, :] < jnp.arange(count)[:, None]
    rank = jnp.sum((same & earlier).astype(jnp.int32), axis=1)
    target = owner_dest * padded + rank * per_block
    row_target = jnp.repeat(target, per_block) + jnp.tile(jnp.arange(per_block), count)
    return (jnp.arange(slots // PAIR * padded)[:, None] == row_target[None, :]).astype(BF16)


def exchange(packed, lanes):
    blocks = packed.reshape((lanes, packed.shape[0] // lanes, packed.shape[1]))
    got = lax.all_to_all(blocks, DP, split_axis=0, concat_axis=0, tiled=True)
    kept = PAIR * BLOCK_ROWS
    return got[:, :kept].reshape(lanes * kept, packed.shape[1])


FREE = pl.CostEstimate(flops=0, bytes_accessed=0, transcendentals=0)
PARAMS = pltpu.CompilerParams(vmem_limit_bytes=48 * 1024 * 1024)


def context_product(chunks, places, out_proj, before=None, slots=None):
    width, rows = chunks[0].shape
    count, tile = len(chunks), 640
    dtype = F32 if slots is None else BF16

    def body(which, *refs):
        refs = list(refs)
        out_ref = refs.pop()
        total = sum(
            lax.dot_general(
                refs[i][...], refs[count + i][...], (((0,), (0,)), ((), ())), preferred_element_type=F32
            )
            for i in range(count)
        )
        if before is not None:
            total = total + refs[2 * count][...]
        if slots is not None:
            total = jnp.dot(refs[-1][...], total.astype(BF16), preferred_element_type=F32)
        out_ref[...] = total.astype(dtype)

    in_specs = [pl.BlockSpec((width, rows), lambda n, which: (0, 0)) for _ in chunks]
    in_specs += [
        pl.BlockSpec((width, tile), lambda n, which, i=i: (which[i], n)) for i in range(count)
    ]
    operands = list(chunks) + [out_proj] * count
    out_rows = rows
    if before is not None:
        in_specs.append(pl.BlockSpec((rows, tile), lambda n, which: (0, n)))
        operands.append(before)
    if slots is not None:
        in_specs.append(pl.BlockSpec(slots.shape, lambda n, which: (0, 0)))
        operands.append(slots)
        out_rows = slots.shape[0]
    return pl.pallas_call(
        body,
        out_shape=jax.ShapeDtypeStruct((out_rows, width), dtype),
        grid_spec=pltpu.PrefetchScalarGridSpec(
            num_scalar_prefetch=1,
            grid=(width // tile,),
            in_specs=in_specs,
            out_specs=pl.BlockSpec((out_rows, tile), lambda n, which: (0, n)),
        ),
        cost_estimate=FREE,
        compiler_params=PARAMS,
        name="context_product",
    )(jnp.stack(places), *operands)


def place_rows(slots, grad_t):
    def body(slots_ref, grad_ref, out_ref):
        out_ref[...] = lax.dot_general(
            slots_ref[...], grad_ref[...], (((1,), (1,)), ((), ())), preferred_element_type=F32
        ).astype(BF16)

    return pl.pallas_call(
        body,
        out_shape=jax.ShapeDtypeStruct((slots.shape[0], grad_t.shape[0]), BF16),
        cost_estimate=FREE,
        compiler_params=PARAMS,
        name="place_rows",
    )(slots, grad_t)


def forward_product(out_proj, context, place, split):
    rows, width = context.shape
    tile = width // 2

    def body(which, proj_ref, context_ref, *out_refs):
        value = lax.dot_general(
            proj_ref[...], context_ref[...], (((1,), (1,)), ((), ())), preferred_element_type=F32
        )
        if split:
            for half in (0, 1):

                @pl.when(pl.program_id(0) == half)
                def _(half=half):
                    out_refs[half][...] = value.astype(BF16)
        else:
            out_refs[0][...] = value

    half_spec = pl.BlockSpec((tile, rows), lambda i, which: (0, 0))
    out = pl.pallas_call(
        body,
        out_shape=[jax.ShapeDtypeStruct((tile, rows), BF16)] * 2
        if split
        else [jax.ShapeDtypeStruct((width, rows), F32)],
        grid_spec=pltpu.PrefetchScalarGridSpec(
            num_scalar_prefetch=1,
            grid=(2,),
            in_specs=[
                pl.BlockSpec((tile, width), lambda i, which: (which[0] * 2 + i, 0)),
                pl.BlockSpec((rows, width), lambda i, which: (0, 0)),
            ],
            out_specs=[half_spec] * 2
            if split
            else [pl.BlockSpec((tile, rows), lambda i, which: (i, 0))],
        ),
        cost_estimate=FREE,
        compiler_params=PARAMS,
        name="forward_product",
    )(place.reshape(1), out_proj, context)
    return out if split else out[0]


def lay_out(chunks, siblings, x, y, c, z):
    rows = chunks[0][0].shape[1]
    block = 160
    flat = [piece for group in (chunks, siblings) for pieces in group for piece in pieces]
    counts = [[len(pieces) for pieces in group] for group in (chunks, siblings)]

    def body(where, *refs):
        ins, outs, sems = refs[: len(flat)], refs[len(flat) : len(flat) + 4], refs[-1]
        here = [where[i] for i in range(4)]
        wx, wy, wc, wz = here
        position = 0
        for owner, group in enumerate(counts):
            pitch = 2 * block if owner == 0 else block
            shift_rows = wc * block if owner == 0 else 0
            for j, count in enumerate(group):
                pieces = ins[position : position + count]
                position += count
                per_piece = 4 // count

                def source(piece, slot, pitch=pitch, shift_rows=shift_rows):
                    start = pl.multiple_of(slot * pitch + shift_rows, 32)
                    return piece.at[pl.ds(start, block), :]

                for k in range(4):
                    target = outs[k]

                    def send(src, slot, target=target, k=k, owner=owner):
                        dst = target.at[pl.ds((owner * 4 + slot) * block, block), :]
                        pltpu.make_async_copy(src, dst, sems.at[k]).start()

                    @pl.when((wc == 0) & (lax.rem(j + wz - wx + 4, 4) == k))
                    def _(pieces=pieces, per_piece=per_piece, send=send, source=source):
                        for slot in range(4):
                            send(source(pieces[slot // per_piece], slot % per_piece), slot)

                    wanted = lax.rem(wy + k, 4)
                    for number, piece in enumerate(pieces):

                        @pl.when((wc == 1) & (wanted // per_piece == number))
                        def _(piece=piece, number=number, per_piece=per_piece, send=send,
                              source=source, wanted=wanted, j=j):
                            send(source(piece, wanted - number * per_piece), j)

        for k in range(4):
            pltpu.make_async_copy(outs[k], outs[k], sems.at[k]).wait()

    return pl.pallas_call(
        body,
        out_shape=[jax.ShapeDtypeStruct((8 * block, rows), BF16)] * 4,
        grid_spec=pltpu.PrefetchScalarGridSpec(
            num_scalar_prefetch=1,
            grid=(1,),
            in_specs=[pl.BlockSpec(memory_space=pl.ANY)] * len(flat),
            out_specs=[pl.BlockSpec(memory_space=pl.ANY)] * 4,
            scratch_shapes=[pltpu.SemaphoreType.DMA((4,))],
        ),
        cost_estimate=FREE,
        compiler_params=PARAMS,
        name="lay_out",
    )(jnp.stack([x, y, c, z]).astype(jnp.int32), *flat)


def weight_product(pieces, contexts):
    count, tile = len(pieces), 640
    height, rows = pieces[0].shape[0] // 2, pieces[0].shape[1]
    width = contexts[0].shape[1]

    def body(*refs):
        total = sum(
            jnp.dot(
                refs[i][core * height : (core + 1) * height, :],
                refs[count + i][core * rows : (core + 1) * rows, :],
                preferred_element_type=F32,
            )
            for i in range(count)
            for core in (0, 1)
        )
        refs[-1][...] = total.astype(BF16)

    return pl.pallas_call(
        body,
        out_shape=jax.ShapeDtypeStruct((height, width), BF16),
        grid=(width // tile,),
        in_specs=[pl.BlockSpec((2 * height, rows), lambda n: (0, 0)) for _ in pieces]
        + [pl.BlockSpec((2 * rows, tile), lambda n: (0, n)) for _ in contexts],
        out_specs=pl.BlockSpec((height, tile), lambda n: (0, n)),
        cost_estimate=FREE,
        compiler_params=PARAMS,
        name="weight_product",
    )(*pieces, *contexts)


def per_device(
    context, residual, cotangent, out_proj, norm_gain, rewards, group_ids, lengths, destinations
):
    lanes = NX * NY * NC
    rows, width = residual.shape
    full = width * NZ
    x, y, c, z = (lax.axis_index(axis) for axis in ("x", "y", "c", "z"))

    groups = rewards.shape[0] * lanes // GROUP
    member = (group_ids[:, None] == jnp.arange(groups)[None, :]).astype(F32)
    group_total = group_sum(jnp.sum(member * rewards[:, None], axis=0))
    advantage = rewards - jnp.sum(member * group_total[None, :], axis=1) / GROUP
    scale = advantage * LMAX / (2.0 * lengths.astype(F32))
    live = jnp.arange(LMAX)[None, :] < lengths[:, None]
    row_weights = jnp.where(live, scale[:, None], F32(0.0)).reshape(-1).astype(BF16)

    top = width // 2
    far_top, far_bottom = forward_product(out_proj, context, (z + 2) % NZ, True)
    far_top, far_bottom = shift(far_top, "z", 1), shift(far_bottom, "z", 3)
    near = forward_product(out_proj, context, (z + 1) % NZ, False)
    back = forward_product(out_proj, context, (z + 3) % NZ, False)
    near = jnp.concatenate([near[:top] + far_top.astype(F32), near[top:]], axis=0).astype(BF16)
    back = jnp.concatenate([back[:top], back[top:] + far_bottom.astype(F32)], axis=0).astype(BF16)

    pair = jnp.concatenate([context, shift(context, "c", 1)], axis=0)
    contexts = [pair, cross(pair, 1, True), None, cross(pair, 3, True)]
    after, contexts[1], contexts[3] = lax.optimization_barrier((context, contexts[1], contexts[3]))
    own = forward_product(out_proj, after, z, False)
    again, _ = lax.optimization_barrier((pair, own))
    contexts[2] = cross(again, 2, True)

    attn_t = own + shift(near, "z", 1).astype(F32) + shift(back, "z", 3).astype(F32)
    hidden_t = residual.T.astype(F32) + attn_t
    upstream_t = norm_gain[:, None] * (row_weights.astype(F32)[None, :] * cotangent.T.astype(F32))
    stats = jnp.stack(
        [jnp.sum(hidden_t * hidden_t, axis=0), jnp.sum(upstream_t * hidden_t, axis=0)]
    )
    stats = stats + shift(stats, "z", 1) + shift(stats, "z", 2) + shift(stats, "z", 3)
    inv_rms = lax.rsqrt(stats[0] / full + EPSILON)
    grad_t = (
        inv_rms[None, :] * upstream_t - hidden_t * (inv_rms**3 * stats[1] / full)[None, :]
    ).astype(BF16)

    block = width // (NY * NC)

    def swap(value):
        parted = value.reshape(-1, NC, block, rows)
        return shift(
            lax.dynamic_index_in_dim(parted, 1 - c, 1, keepdims=False).reshape(-1, rows), "c", 1
        )

    slots = slot_matrix(destinations[:, 0], lanes * PAIR, rows, 16)
    from_left, from_right = shift(grad_t, "z", 1), shift(grad_t, "z", 3)
    swapped = swap(grad_t)
    d_residual = exchange(place_rows(slots, grad_t), lanes)
    context_grad = context_product([grad_t], [z], out_proj)
    from_left, from_right, context_grad, swapped, contexts[2] = lax.optimization_barrier(
        (from_left, from_right, context_grad, swapped, contexts[2])
    )
    far_left, far_right = shift(from_left[:top], "z", 1), shift(from_right[top:], "z", 3)
    swapped_left, swapped_right = swap(from_left), swap(from_right)
    context_grad = context_product(
        [from_right, from_left], [(z + 1) % NZ, (z + 3) % NZ], out_proj, before=context_grad
    )
    far_left, far_right, context_grad, swapped_left, swapped_right, d_residual = (
        lax.optimization_barrier(
            (far_left, far_right, context_grad, swapped_left, swapped_right, d_residual)
        )
    )
    far_grad = jnp.concatenate([far_left, far_right], axis=0)

    sends = lay_out(
        [[grad_t], [from_right], [far_left, far_right], [from_left]],
        [[swapped], [swapped_right], [swap(far_grad)], [swapped_left]],
        x, y, c, z,
    )
    pieces = [sends[0]] + [cross(sends[k], k, True) for k in (1, 2, 3)]
    d_context = exchange(
        context_product([far_grad], [(z + 2) % NZ], out_proj, before=context_grad, slots=slots), lanes
    )
    total = weight_product(pieces, contexts).reshape(4, block, width)

    def place(step):
        return pick(total, jnp.where(c == 0, (y + step) % NY, (x + step - z) % NZ))

    d_out_proj = place(0).astype(F32)
    for k in (1, 2, 3):
        d_out_proj = d_out_proj + cross(place(k), k, False).astype(F32)
    return (d_context, d_residual, d_out_proj / lanes)


def solution(mesh):
    wide = Mesh(mesh.devices.reshape(NX, NY, NC, NZ), DP + ("z",))
    placed = (
        P(DP, "z"),
        P(DP, "z"),
        P(DP, "z"),
        P(None, "z"),
        P("z"),
        P(DP),
        P(DP),
        P(DP),
        P(DP, None),
    )
    return jax.shard_map(
        per_device,
        mesh=wide,
        in_specs=placed,
        out_specs=(P(DP, "z"), P(DP, "z"), P(DP, "z")),
        check_vma=False,
    )
```

```python
import jax
import jax.numpy as jnp
from jax import lax
from jax.experimental import pallas as pl
from jax.experimental.pallas import tpu as pltpu
from jax.sharding import Mesh
from jax.sharding import PartitionSpec as P

LMAX = 64
GROUP = 16
PAIR = 3
BLOCK_ROWS = 4
EPSILON = 1e-06
NX, NY, NC, NZ = 4, 4, 2, 4
DP = ("x", "y", "c")
F32 = jnp.float32
BF16 = jnp.bfloat16


def shift(value, axis, step):
    size = lax.axis_size(axis)
    return lax.ppermute(value, axis, [(i, (i + step) % size) for i in range(size)])


def pick(values, index):
    return lax.dynamic_index_in_dim(values, index, 0, keepdims=False)


def cross(value, step, first):
    pairs = []
    for x in range(NX):
        for y in range(NY):
            for c in range(NC):
                along_x = (c == 0) == first
                to = ((x + step) % NX, y, c) if along_x else (x, (y + step) % NY, c)
                pairs.append(((x * NY + y) * NC + c, (to[0] * NY + to[1]) * NC + to[2]))
    return lax.ppermute(value, DP, pairs)


def group_sum(value):
    copies = jnp.broadcast_to(value, (NX * NY * NC,) + value.shape)
    return jnp.sum(lax.all_to_all(copies, DP, split_axis=0, concat_axis=0, tiled=True), axis=0)


def slot_matrix(owner_dest, slots, rows, padded):
    count = owner_dest.shape[0]
    per_block = rows // count
    same = owner_dest[:, None] == owner_dest[None, :]
    earlier = jnp.arange(count)[None, :] < jnp.arange(count)[:, None]
    rank = jnp.sum((same & earlier).astype(jnp.int32), axis=1)
    target = owner_dest * padded + rank * per_block
    row_target = jnp.repeat(target, per_block) + jnp.tile(jnp.arange(per_block), count)
    return (jnp.arange(slots // PAIR * padded)[:, None] == row_target[None, :]).astype(BF16)


def exchange(packed, lanes):
    blocks = packed.reshape((lanes, packed.shape[0] // lanes, packed.shape[1]))
    got = lax.all_to_all(blocks, DP, split_axis=0, concat_axis=0, tiled=True)
    kept = PAIR * BLOCK_ROWS
    return got[:, :kept].reshape(lanes * kept, packed.shape[1])


FREE = pl.CostEstimate(flops=0, bytes_accessed=0, transcendentals=0)
PARAMS = pltpu.CompilerParams(vmem_limit_bytes=20 * 1024 * 1024)


def context_product(chunks, places, out_proj, before=None, slots=None):
    width, rows = out_proj.shape[1], chunks[0].shape[1]
    count, tile = len(chunks), 640
    dtype = F32 if slots is None else BF16

    def body(which, *refs):
        refs = list(refs)
        out_ref = refs.pop()
        total = sum(
            lax.dot_general(
                refs[i][...], refs[count + i][...], (((0,), (0,)), ((), ())), preferred_element_type=F32
            )
            for i in range(count)
        )
        if before is not None:
            total = total + refs[2 * count][...]
        if slots is not None:
            total = jnp.dot(refs[-1][...], total.astype(BF16), preferred_element_type=F32)
        out_ref[...] = total.astype(dtype)

    in_specs = [pl.BlockSpec(chunk.shape, lambda n, which: (0, 0)) for chunk in chunks]
    in_specs += [
        pl.BlockSpec((chunk.shape[0], tile), lambda n, which, i=i: (which[i], n))
        for i, chunk in enumerate(chunks)
    ]
    operands = list(chunks) + [out_proj] * count
    out_rows = rows
    if before is not None:
        in_specs.append(pl.BlockSpec((rows, tile), lambda n, which: (0, n)))
        operands.append(before)
    if slots is not None:
        in_specs.append(pl.BlockSpec(slots.shape, lambda n, which: (0, 0)))
        operands.append(slots)
        out_rows = slots.shape[0]
    return pl.pallas_call(
        body,
        out_shape=jax.ShapeDtypeStruct((out_rows, width), dtype),
        grid_spec=pltpu.PrefetchScalarGridSpec(
            num_scalar_prefetch=1,
            grid=(width // tile,),
            in_specs=in_specs,
            out_specs=pl.BlockSpec((out_rows, tile), lambda n, which: (0, n)),
        ),
        cost_estimate=FREE,
        compiler_params=PARAMS,
        name="context_product",
    )(jnp.stack(places), *operands)


def place_rows(slots, grad_t):
    def body(slots_ref, grad_ref, out_ref):
        out_ref[...] = lax.dot_general(
            slots_ref[...], grad_ref[...], (((1,), (1,)), ((), ())), preferred_element_type=F32
        ).astype(BF16)

    return pl.pallas_call(
        body,
        out_shape=jax.ShapeDtypeStruct((slots.shape[0], grad_t.shape[0]), BF16),
        cost_estimate=FREE,
        compiler_params=PARAMS,
        name="place_rows",
    )(slots, grad_t)


def forward_product(out_proj, context, place, split):
    rows, width = context.shape
    tile = width // 2

    def body(which, proj_ref, context_ref, *out_refs):
        value = lax.dot_general(
            proj_ref[...], context_ref[...], (((1,), (1,)), ((), ())), preferred_element_type=F32
        )
        if split:
            for half in (0, 1):

                @pl.when(pl.program_id(0) == half)
                def _(half=half):
                    out_refs[half][...] = value.astype(BF16)
        else:
            out_refs[0][...] = value

    half_spec = pl.BlockSpec((tile, rows), lambda i, which: (0, 0))
    out = pl.pallas_call(
        body,
        out_shape=[jax.ShapeDtypeStruct((tile, rows), BF16)] * 2
        if split
        else [jax.ShapeDtypeStruct((width, rows), F32)],
        grid_spec=pltpu.PrefetchScalarGridSpec(
            num_scalar_prefetch=1,
            grid=(2,),
            in_specs=[
                pl.BlockSpec((tile, width), lambda i, which: (which[0] * 2 + i, 0)),
                pl.BlockSpec((rows, width), lambda i, which: (0, 0)),
            ],
            out_specs=[half_spec] * 2
            if split
            else [pl.BlockSpec((tile, rows), lambda i, which: (i, 0))],
        ),
        cost_estimate=FREE,
        compiler_params=PARAMS,
        name="forward_product",
    )(place.reshape(1), out_proj, context)
    return out if split else out[0]


def lay_out(chunks, siblings, x, y, c, z):
    rows = chunks[0][0].shape[1]
    block = 160
    flat = [piece for group in (chunks, siblings) for pieces in group for piece in pieces]
    counts = [[len(pieces) for pieces in group] for group in (chunks, siblings)]

    def body(where, *refs):
        ins, outs, sems = refs[: len(flat)], refs[len(flat) : len(flat) + 4], refs[-1]
        here = [where[i] for i in range(4)]
        wx, wy, wc, wz = here
        position = 0
        for owner, group in enumerate(counts):
            pitch = 2 * block if owner == 0 else block
            shift_rows = wc * block if owner == 0 else 0
            for j, count in enumerate(group):
                pieces = ins[position : position + count]
                position += count
                per_piece = 4 // count

                def source(piece, slot, pitch=pitch, shift_rows=shift_rows):
                    start = pl.multiple_of(slot * pitch + shift_rows, 32)
                    return piece.at[pl.ds(start, block), :]

                for k in range(4):
                    target = outs[k]

                    def send(src, slot, target=target, k=k, owner=owner):
                        dst = target.at[pl.ds((owner * 4 + slot) * block, block), :]
                        pltpu.make_async_copy(src, dst, sems.at[k]).start()

                    @pl.when((wc == 0) & (lax.rem(j + wz - wx + 4, 4) == k))
                    def _(pieces=pieces, per_piece=per_piece, send=send, source=source):
                        for slot in range(4):
                            send(source(pieces[slot // per_piece], slot % per_piece), slot)

                    wanted = lax.rem(wy + k, 4)
                    for number, piece in enumerate(pieces):

                        @pl.when((wc == 1) & (wanted // per_piece == number))
                        def _(piece=piece, number=number, per_piece=per_piece, send=send,
                              source=source, wanted=wanted, j=j):
                            send(source(piece, wanted - number * per_piece), j)

        for k in range(4):
            pltpu.make_async_copy(outs[k], outs[k], sems.at[k]).wait()

    return pl.pallas_call(
        body,
        out_shape=[jax.ShapeDtypeStruct((8 * block, rows), BF16)] * 4,
        grid_spec=pltpu.PrefetchScalarGridSpec(
            num_scalar_prefetch=1,
            grid=(1,),
            in_specs=[pl.BlockSpec(memory_space=pl.ANY)] * len(flat),
            out_specs=[pl.BlockSpec((8 * block, rows), lambda i, where: (0, 0))] * 4,
            scratch_shapes=[pltpu.SemaphoreType.DMA((4,))],
        ),
        cost_estimate=FREE,
        compiler_params=PARAMS,
        name="lay_out",
    )(jnp.stack([x, y, c, z]).astype(jnp.int32), *flat)


def weight_product(pieces, contexts):
    count, tile = len(pieces), 640
    height, rows = pieces[0].shape[0] // 2, pieces[0].shape[1]
    width = contexts[0].shape[1]

    def body(*refs):
        total = sum(
            jnp.dot(
                refs[i][core * height : (core + 1) * height, :],
                refs[count + i][core * rows : (core + 1) * rows, :],
                preferred_element_type=F32,
            )
            for i in range(count)
            for core in (0, 1)
        )
        refs[-1][...] = total.astype(BF16)

    return pl.pallas_call(
        body,
        out_shape=jax.ShapeDtypeStruct((height, width), BF16),
        grid=(width // tile,),
        in_specs=[pl.BlockSpec((2 * height, rows), lambda n: (0, 0)) for _ in pieces]
        + [pl.BlockSpec((2 * rows, tile), lambda n: (0, n)) for _ in contexts],
        out_specs=pl.BlockSpec((height, tile), lambda n: (0, n)),
        cost_estimate=FREE,
        compiler_params=PARAMS,
        name="weight_product",
    )(*pieces, *contexts)


def per_device(
    context, residual, cotangent, out_proj, norm_gain, rewards, group_ids, lengths, destinations
):
    lanes = NX * NY * NC
    rows, width = residual.shape
    full = width * NZ
    x, y, c, z = (lax.axis_index(axis) for axis in ("x", "y", "c", "z"))

    top = width // 2
    far_top, far_bottom = forward_product(out_proj, context, (z + 2) % NZ, True)
    pair = jnp.concatenate(
        [context, shift(lax.optimization_barrier((context, far_top))[0], "c", 1)], axis=0
    )
    far_top, far_bottom = shift(far_top, "z", 1), shift(far_bottom, "z", 3)
    ready, pair = lax.optimization_barrier((context, pair))
    near = forward_product(out_proj, ready, (z + 1) % NZ, False)
    back = forward_product(out_proj, ready, (z + 3) % NZ, False)
    near = jnp.concatenate([near[:top] + far_top.astype(F32), near[top:]], axis=0).astype(BF16)
    back = jnp.concatenate([back[:top], back[top:] + far_bottom.astype(F32)], axis=0).astype(BF16)

    groups = rewards.shape[0] * lanes // GROUP
    member = (group_ids[:, None] == jnp.arange(groups)[None, :]).astype(F32)
    share, _ = lax.optimization_barrier((jnp.sum(member * rewards[:, None], axis=0), near))
    group_total = group_sum(share)
    advantage = rewards - jnp.sum(member * group_total[None, :], axis=1) / GROUP
    scale = advantage * LMAX / (2.0 * lengths.astype(F32))
    live = jnp.arange(LMAX)[None, :] < lengths[:, None]
    row_weights = jnp.where(live, scale[:, None], F32(0.0)).reshape(-1).astype(BF16)

    contexts = [pair, cross(pair, 1, True), None, cross(pair, 3, True)]
    own = forward_product(out_proj, lax.optimization_barrier((context, near))[0], z, False)
    attn_t = own + shift(near, "z", 1).astype(F32) + shift(back, "z", 3).astype(F32)
    attn_t, contexts[1], contexts[3] = lax.optimization_barrier(
        (attn_t, contexts[1], contexts[3])
    )
    contexts[2] = cross(lax.optimization_barrier((pair, contexts[1]))[0], 2, True)
    hidden_t = residual.T.astype(F32) + attn_t
    upstream_t = norm_gain[:, None] * (row_weights.astype(F32)[None, :] * cotangent.T.astype(F32))
    stats = jnp.stack(
        [jnp.sum(hidden_t * hidden_t, axis=0), jnp.sum(upstream_t * hidden_t, axis=0)]
    )
    stats = stats + shift(stats, "z", 1) + shift(stats, "z", 2) + shift(stats, "z", 3)
    inv_rms = lax.rsqrt(stats[0] / full + EPSILON)
    grad_t = (
        inv_rms[None, :] * upstream_t - hidden_t * (inv_rms**3 * stats[1] / full)[None, :]
    ).astype(BF16)

    block = width // (NY * NC)

    def swap(*values):
        parted = [value.reshape(-1, NC, block, rows) for value in values]
        asked = [lax.dynamic_index_in_dim(value, 1 - c, 1, keepdims=False) for value in parted]
        return shift(jnp.concatenate(asked, axis=0).reshape(-1, rows), "c", 1)

    slots = slot_matrix(destinations[:, 0], lanes * PAIR, rows, 16)
    from_left, from_right = shift(grad_t, "z", 1), shift(grad_t, "z", 3)
    swapped = swap(grad_t)
    grad_rows, _ = lax.optimization_barrier((grad_t, swapped))
    d_residual = exchange(place_rows(slots, grad_rows), lanes)
    context_grad = context_product([grad_t], [z], out_proj)
    from_left, from_right, context_grad, swapped, contexts[2] = lax.optimization_barrier(
        (from_left, from_right, context_grad, swapped, contexts[2])
    )
    far_left, far_right = shift(from_left[:top], "z", 1), shift(from_right[top:], "z", 3)
    swapped_left, swapped_right = swap(from_left), swap(from_right)
    context_grad = context_product(
        [from_right, from_left], [(z + 1) % NZ, (z + 3) % NZ], out_proj, before=context_grad
    )
    far_left, far_right, context_grad, swapped_left, swapped_right, d_residual = (
        lax.optimization_barrier(
            (far_left, far_right, context_grad, swapped_left, swapped_right, d_residual)
        )
    )
    sends = lay_out(
        [[grad_t], [from_right], [far_left, far_right], [from_left]],
        [[swapped], [swapped_right], [swap(far_left, far_right)], [swapped_left]],
        x, y, c, z,
    )
    pieces = [sends[0]] + [cross(sends[k], k, True) for k in (1, 2, 3)]
    far_place = (z + 2) % NZ * 2
    placed = context_product(
        [far_left, far_right], [far_place, far_place + 1], out_proj, before=context_grad, slots=slots
    )
    d_context = exchange(placed, lanes)
    total = weight_product(pieces, contexts).reshape(4, block, width)

    def place(step):
        return pick(total, jnp.where(c == 0, (y + step) % NY, (x + step - z) % NZ))

    d_out_proj = place(0).astype(F32)
    for k in (1, 2, 3):
        d_out_proj = d_out_proj + cross(place(k), k, False).astype(F32)
    return (d_context, d_residual, d_out_proj / lanes)


def solution(mesh):
    wide = Mesh(mesh.devices.reshape(NX, NY, NC, NZ), DP + ("z",))
    placed = (
        P(DP, "z"),
        P(DP, "z"),
        P(DP, "z"),
        P(None, "z"),
        P("z"),
        P(DP),
        P(DP),
        P(DP),
        P(DP, None),
    )
    return jax.shard_map(
        per_device,
        mesh=wide,
        in_specs=placed,
        out_specs=(P(DP, "z"), P(DP, "z"), P(DP, "z")),
        check_vma=False,
    )
```

```python
import jax
import jax.numpy as jnp
from jax import lax
from jax.experimental import pallas as pl
from jax.experimental.pallas import tpu as pltpu
from jax.sharding import Mesh
from jax.sharding import PartitionSpec as P

LMAX = 64
GROUP = 16
PAIR = 3
BLOCK_ROWS = 4
EPSILON = 1e-06
NX, NY, NC, NZ = 4, 4, 2, 4
DP = ("x", "y", "c")
F32 = jnp.float32
BF16 = jnp.bfloat16


def shift(value, axis, step):
    size = lax.axis_size(axis)
    return lax.ppermute(value, axis, [(i, (i + step) % size) for i in range(size)])


def pick(values, index):
    return lax.dynamic_index_in_dim(values, index, 0, keepdims=False)


def cross(value, step, first):
    pairs = []
    for x in range(NX):
        for y in range(NY):
            for c in range(NC):
                along_x = (c == 0) == first
                to = ((x + step) % NX, y, c) if along_x else (x, (y + step) % NY, c)
                pairs.append(((x * NY + y) * NC + c, (to[0] * NY + to[1]) * NC + to[2]))
    return lax.ppermute(value, DP, pairs)


def group_sum(value):
    copies = jnp.broadcast_to(value, (NX * NY * NC,) + value.shape)
    return jnp.sum(lax.all_to_all(copies, DP, split_axis=0, concat_axis=0, tiled=True), axis=0)


def slot_matrix(owner_dest, slots, rows, padded):
    count = owner_dest.shape[0]
    per_block = rows // count
    same = owner_dest[:, None] == owner_dest[None, :]
    earlier = jnp.arange(count)[None, :] < jnp.arange(count)[:, None]
    rank = jnp.sum((same & earlier).astype(jnp.int32), axis=1)
    target = owner_dest * padded + rank * per_block
    row_target = jnp.repeat(target, per_block) + jnp.tile(jnp.arange(per_block), count)
    return (jnp.arange(slots // PAIR * padded)[:, None] == row_target[None, :]).astype(BF16)


def exchange(packed, lanes):
    blocks = packed.reshape((lanes, packed.shape[0] // lanes, packed.shape[1]))
    got = lax.all_to_all(blocks, DP, split_axis=0, concat_axis=0, tiled=True)
    kept = PAIR * BLOCK_ROWS
    return got[:, :kept].reshape(lanes * kept, packed.shape[1])


FREE = pl.CostEstimate(flops=0, bytes_accessed=0, transcendentals=0)
PARAMS = pltpu.CompilerParams(vmem_limit_bytes=20 * 1024 * 1024)
WIDE = pltpu.CompilerParams(vmem_limit_bytes=56 * 1024 * 1024)


def context_product(chunks, places, out_proj, before=None, slots=None):
    width, rows = out_proj.shape[1], chunks[0].shape[1]
    count, tile = len(chunks), 640
    dtype = F32 if slots is None else BF16

    def body(which, *refs):
        refs = list(refs)
        out_ref = refs.pop()
        total = sum(
            lax.dot_general(
                refs[i][...], refs[count + i][...], (((0,), (0,)), ((), ())), preferred_element_type=F32
            )
            for i in range(count)
        )
        if before is not None:
            total = total + refs[2 * count][...]
        if slots is not None:
            total = jnp.dot(refs[-1][...], total.astype(BF16), preferred_element_type=F32)
        out_ref[...] = total.astype(dtype)

    in_specs = [pl.BlockSpec(chunk.shape, lambda n, which: (0, 0)) for chunk in chunks]
    in_specs += [
        pl.BlockSpec((chunk.shape[0], tile), lambda n, which, i=i: (which[i], n))
        for i, chunk in enumerate(chunks)
    ]
    operands = list(chunks) + [out_proj] * count
    out_rows = rows
    if before is not None:
        in_specs.append(pl.BlockSpec((rows, tile), lambda n, which: (0, n)))
        operands.append(before)
    if slots is not None:
        in_specs.append(pl.BlockSpec(slots.shape, lambda n, which: (0, 0)))
        operands.append(slots)
        out_rows = slots.shape[0]
    return pl.pallas_call(
        body,
        out_shape=jax.ShapeDtypeStruct((out_rows, width), dtype),
        grid_spec=pltpu.PrefetchScalarGridSpec(
            num_scalar_prefetch=1,
            grid=(width // tile,),
            in_specs=in_specs,
            out_specs=pl.BlockSpec((out_rows, tile), lambda n, which: (0, n)),
        ),
        cost_estimate=FREE,
        compiler_params=WIDE,
        name="context_product",
    )(jnp.stack(places), *operands)


def place_rows(slots, grad_t):
    def body(slots_ref, grad_ref, out_ref):
        out_ref[...] = lax.dot_general(
            slots_ref[...], grad_ref[...], (((1,), (1,)), ((), ())), preferred_element_type=F32
        ).astype(BF16)

    return pl.pallas_call(
        body,
        out_shape=jax.ShapeDtypeStruct((slots.shape[0], grad_t.shape[0]), BF16),
        cost_estimate=FREE,
        compiler_params=PARAMS,
        name="place_rows",
    )(slots, grad_t)


def forward_product(out_proj, context, place, split):
    rows, width = context.shape
    tile = width // 2

    def body(which, proj_ref, context_ref, *out_refs):
        value = lax.dot_general(
            proj_ref[...], context_ref[...], (((1,), (1,)), ((), ())), preferred_element_type=F32
        )
        if split:
            for half in (0, 1):

                @pl.when(pl.program_id(0) == half)
                def _(half=half):
                    out_refs[half][...] = value.astype(BF16)
        else:
            out_refs[0][...] = value

    half_spec = pl.BlockSpec((tile, rows), lambda i, which: (0, 0))
    out = pl.pallas_call(
        body,
        out_shape=[jax.ShapeDtypeStruct((tile, rows), BF16)] * 2
        if split
        else [jax.ShapeDtypeStruct((width, rows), F32)],
        grid_spec=pltpu.PrefetchScalarGridSpec(
            num_scalar_prefetch=1,
            grid=(2,),
            in_specs=[
                pl.BlockSpec((tile, width), lambda i, which: (which[0] * 2 + i, 0)),
                pl.BlockSpec((rows, width), lambda i, which: (0, 0)),
            ],
            out_specs=[half_spec] * 2
            if split
            else [pl.BlockSpec((tile, rows), lambda i, which: (i, 0))],
        ),
        cost_estimate=FREE,
        compiler_params=WIDE,
        name="forward_product",
    )(place.reshape(1), out_proj, context)
    return out if split else out[0]


def lay_out(chunks, siblings, x, y, c, z):
    rows = chunks[0][0].shape[1]
    block = 160
    flat = [piece for group in (chunks, siblings) for pieces in group for piece in pieces]
    counts = [[len(pieces) for pieces in group] for group in (chunks, siblings)]

    def body(where, *refs):
        ins, outs, sems = refs[: len(flat)], refs[len(flat) : len(flat) + 4], refs[-1]
        here = [where[i] for i in range(4)]
        wx, wy, wc, wz = here
        position = 0
        for owner, group in enumerate(counts):
            pitch = 2 * block if owner == 0 else block
            shift_rows = wc * block if owner == 0 else 0
            for j, count in enumerate(group):
                pieces = ins[position : position + count]
                position += count
                per_piece = 4 // count

                def source(piece, slot, pitch=pitch, shift_rows=shift_rows):
                    start = pl.multiple_of(slot * pitch + shift_rows, 32)
                    return piece.at[pl.ds(start, block), :]

                for k in range(4):
                    target = outs[k]

                    def send(src, slot, target=target, k=k, owner=owner):
                        dst = target.at[pl.ds((owner * 4 + slot) * block, block), :]
                        pltpu.make_async_copy(src, dst, sems.at[k]).start()

                    @pl.when((wc == 0) & (lax.rem(j + wz - wx + 4, 4) == k))
                    def _(pieces=pieces, per_piece=per_piece, send=send, source=source):
                        for slot in range(4):
                            send(source(pieces[slot // per_piece], slot % per_piece), slot)

                    wanted = lax.rem(wy + k, 4)
                    for number, piece in enumerate(pieces):

                        @pl.when((wc == 1) & (wanted // per_piece == number))
                        def _(piece=piece, number=number, per_piece=per_piece, send=send,
                              source=source, wanted=wanted, j=j):
                            send(source(piece, wanted - number * per_piece), j)

        for k in range(4):
            pltpu.make_async_copy(outs[k], outs[k], sems.at[k]).wait()

    return pl.pallas_call(
        body,
        out_shape=[jax.ShapeDtypeStruct((8 * block, rows), BF16)] * 4,
        grid_spec=pltpu.PrefetchScalarGridSpec(
            num_scalar_prefetch=1,
            grid=(1,),
            in_specs=[pl.BlockSpec(memory_space=pl.ANY)] * len(flat),
            out_specs=[pl.BlockSpec((8 * block, rows), lambda i, where: (0, 0))] * 4,
            scratch_shapes=[pltpu.SemaphoreType.DMA((4,))],
        ),
        cost_estimate=FREE,
        compiler_params=PARAMS,
        name="lay_out",
    )(jnp.stack([x, y, c, z]).astype(jnp.int32), *flat)


def weight_product(pieces, contexts):
    count, tile = len(pieces), 640
    height, rows = pieces[0].shape[0] // 2, pieces[0].shape[1]
    width = contexts[0].shape[1]

    def body(*refs):
        total = sum(
            jnp.dot(
                refs[i][core * height : (core + 1) * height, :],
                refs[count + i][core * rows : (core + 1) * rows, :],
                preferred_element_type=F32,
            )
            for i in range(count)
            for core in (0, 1)
        )
        refs[-1][...] = total.astype(BF16)

    return pl.pallas_call(
        body,
        out_shape=jax.ShapeDtypeStruct((height, width), BF16),
        grid=(width // tile,),
        in_specs=[pl.BlockSpec((2 * height, rows), lambda n: (0, 0)) for _ in pieces]
        + [pl.BlockSpec((2 * rows, tile), lambda n: (0, n)) for _ in contexts],
        out_specs=pl.BlockSpec((height, tile), lambda n: (0, n)),
        cost_estimate=FREE,
        compiler_params=WIDE,
        name="weight_product",
    )(*pieces, *contexts)


def per_device(
    context, residual, cotangent, out_proj, norm_gain, rewards, group_ids, lengths, destinations
):
    lanes = NX * NY * NC
    rows, width = residual.shape
    full = width * NZ
    x, y, c, z = (lax.axis_index(axis) for axis in ("x", "y", "c", "z"))

    top = width // 2
    far_top, far_bottom = forward_product(out_proj, context, (z + 2) % NZ, True)
    pair = jnp.concatenate(
        [context, shift(lax.optimization_barrier((context, far_top))[0], "c", 1)], axis=0
    )
    far_top, far_bottom = shift(far_top, "z", 1), shift(far_bottom, "z", 3)
    ready, pair = lax.optimization_barrier((context, pair))
    near = forward_product(out_proj, ready, (z + 1) % NZ, False)
    back = forward_product(out_proj, ready, (z + 3) % NZ, False)
    near = jnp.concatenate([near[:top] + far_top.astype(F32), near[top:]], axis=0).astype(BF16)
    back = jnp.concatenate([back[:top], back[top:] + far_bottom.astype(F32)], axis=0).astype(BF16)

    groups = rewards.shape[0] * lanes // GROUP
    member = (group_ids[:, None] == jnp.arange(groups)[None, :]).astype(F32)
    share, _ = lax.optimization_barrier((jnp.sum(member * rewards[:, None], axis=0), near))
    group_total = group_sum(share)
    advantage = rewards - jnp.sum(member * group_total[None, :], axis=1) / GROUP
    scale = advantage * LMAX / (2.0 * lengths.astype(F32))
    live = jnp.arange(LMAX)[None, :] < lengths[:, None]
    row_weights = jnp.where(live, scale[:, None], F32(0.0)).reshape(-1).astype(BF16)

    contexts = [pair, cross(pair, 1, True), None, cross(pair, 3, True)]
    own = forward_product(out_proj, lax.optimization_barrier((context, near))[0], z, False)
    attn_t = own + shift(near, "z", 1).astype(F32) + shift(back, "z", 3).astype(F32)
    attn_t, contexts[1], contexts[3] = lax.optimization_barrier(
        (attn_t, contexts[1], contexts[3])
    )
    contexts[2] = cross(lax.optimization_barrier((pair, contexts[1]))[0], 2, True)
    hidden_t = residual.T.astype(F32) + attn_t
    upstream_t = norm_gain[:, None] * (row_weights.astype(F32)[None, :] * cotangent.T.astype(F32))
    stats = jnp.stack(
        [jnp.sum(hidden_t * hidden_t, axis=0), jnp.sum(upstream_t * hidden_t, axis=0)]
    )
    stats = stats + shift(stats, "z", 1) + shift(stats, "z", 2) + shift(stats, "z", 3)
    inv_rms = lax.rsqrt(stats[0] / full + EPSILON)
    grad_t = (
        inv_rms[None, :] * upstream_t - hidden_t * (inv_rms**3 * stats[1] / full)[None, :]
    ).astype(BF16)

    block = width // (NY * NC)

    def swap(*values):
        parted = [value.reshape(-1, NC, block, rows) for value in values]
        asked = [lax.dynamic_index_in_dim(value, 1 - c, 1, keepdims=False) for value in parted]
        return shift(jnp.concatenate(asked, axis=0).reshape(-1, rows), "c", 1)

    slots = slot_matrix(destinations[:, 0], lanes * PAIR, rows, 16)
    from_left, from_right = shift(grad_t, "z", 1), shift(grad_t, "z", 3)
    swapped = swap(grad_t)
    grad_rows, _ = lax.optimization_barrier((grad_t, swapped))
    d_residual = exchange(place_rows(slots, grad_rows), lanes)
    context_grad = context_product([grad_t], [z], out_proj)
    from_left, from_right, context_grad, swapped, contexts[2] = lax.optimization_barrier(
        (from_left, from_right, context_grad, swapped, contexts[2])
    )
    far_left, far_right = shift(from_left[:top], "z", 1), shift(from_right[top:], "z", 3)
    swapped_left, swapped_right = swap(from_left), swap(from_right)
    context_grad = context_product(
        [from_right, from_left], [(z + 1) % NZ, (z + 3) % NZ], out_proj, before=context_grad
    )
    far_left, far_right, context_grad, swapped_left, swapped_right = lax.optimization_barrier(
        (far_left, far_right, context_grad, swapped_left, swapped_right)
    )
    sends = lay_out(
        [[grad_t], [from_right], [far_left, far_right], [from_left]],
        [[swapped], [swapped_right], [swap(far_left, far_right)], [swapped_left]],
        x, y, c, z,
    )
    pieces = [sends[0]] + [cross(sends[k], k, True) for k in (1, 2, 3)]
    far_place = (z + 2) % NZ * 2
    placed = context_product(
        [far_left, far_right], [far_place, far_place + 1], out_proj, before=context_grad, slots=slots
    )
    placed, d_residual = lax.optimization_barrier((placed, d_residual))
    d_context = exchange(placed, lanes)
    total = weight_product(pieces, contexts).reshape(4, block, width)

    def place(step):
        return pick(total, jnp.where(c == 0, (y + step) % NY, (x + step - z) % NZ))

    d_out_proj = place(0).astype(F32)
    for k in (1, 2, 3):
        d_out_proj = d_out_proj + cross(place(k), k, False).astype(F32)
    return (d_context, d_residual, d_out_proj / lanes)


def solution(mesh):
    wide = Mesh(mesh.devices.reshape(NX, NY, NC, NZ), DP + ("z",))
    placed = (
        P(DP, "z"),
        P(DP, "z"),
        P(DP, "z"),
        P(None, "z"),
        P("z"),
        P(DP),
        P(DP),
        P(DP),
        P(DP, None),
    )
    return jax.shard_map(
        per_device,
        mesh=wide,
        in_specs=placed,
        out_specs=(P(DP, "z"), P(DP, "z"), P(DP, "z")),
        check_vma=False,
    )
```

```python
import jax
import jax.numpy as jnp
from jax import lax
from jax.experimental import pallas as pl
from jax.experimental.pallas import tpu as pltpu
from jax.sharding import Mesh
from jax.sharding import PartitionSpec as P

LMAX = 64
GROUP = 16
PAIR = 3
EPSILON = 1e-06
NX, NY, NC, NZ = 4, 4, 2, 4
DP = ("x", "y", "c")
F32 = jnp.float32
BF16 = jnp.bfloat16


def shift(value, axis, step):
    size = lax.axis_size(axis)
    return lax.ppermute(value, axis, [(i, (i + step) % size) for i in range(size)])


def pick(values, index):
    return lax.dynamic_index_in_dim(values, index, 0, keepdims=False)


def cross(value, step, first):
    pairs = []
    for x in range(NX):
        for y in range(NY):
            for c in range(NC):
                along_x = (c == 0) == first
                to = ((x + step) % NX, y, c) if along_x else (x, (y + step) % NY, c)
                pairs.append(((x * NY + y) * NC + c, (to[0] * NY + to[1]) * NC + to[2]))
    return lax.ppermute(value, DP, pairs)


def group_sum(value):
    copies = jnp.broadcast_to(value, (NX * NY * NC,) + value.shape)
    return jnp.sum(lax.all_to_all(copies, DP, split_axis=0, concat_axis=0, tiled=True), axis=0)


def slot_matrix(owner_dest, lanes, rows):
    count = owner_dest.shape[0]
    per_block = rows // count
    kept = PAIR * per_block
    same = owner_dest[:, None] == owner_dest[None, :]
    earlier = jnp.arange(count)[None, :] < jnp.arange(count)[:, None]
    rank = jnp.sum((same & earlier).astype(jnp.int32), axis=1)
    target = owner_dest * 2 * kept + rank * per_block
    row_target = jnp.repeat(target, per_block) + jnp.tile(jnp.arange(per_block), count)
    row_target = row_target[None, None, :] + kept * jnp.arange(2)[:, None, None]
    return (jnp.arange(lanes * 2 * kept)[None, :, None] == row_target).astype(BF16)


def exchange(packed, lanes):
    height, half = packed.shape
    blocks = packed.reshape((lanes, height // lanes, half))
    got = lax.all_to_all(blocks, DP, split_axis=0, concat_axis=0, tiled=True)
    got = got.reshape((lanes, 2, height // lanes // 2, half))
    return jnp.swapaxes(got, 1, 2).reshape(height // 2, 2 * half)


FREE = pl.CostEstimate(flops=0, bytes_accessed=0, transcendentals=0)
PARAMS = pltpu.CompilerParams(vmem_limit_bytes=48 * 1024 * 1024)


def context_product(chunks, places, out_proj, before=None, slots=None):
    width, rows = out_proj.shape[1], chunks[0].shape[1]
    count, tile = len(chunks), 640
    dtype = F32 if slots is None else BF16

    def body(which, *refs):
        refs = list(refs)
        out_ref = refs.pop()
        total = sum(
            lax.dot_general(
                refs[i][...], refs[count + i][...], (((0,), (0,)), ((), ())), preferred_element_type=F32
            )
            for i in range(count)
        )
        if before is not None:
            total = total + refs[2 * count][...]
        if slots is None:
            out_ref[...] = total
            return
        total = jnp.dot(refs[-1][0], total.astype(BF16), preferred_element_type=F32)

        @pl.when(pl.program_id(0) == 0)
        def _():
            out_ref[...] = total.astype(BF16)

        @pl.when(pl.program_id(0) == 1)
        def _():
            out_ref[...] += total.astype(BF16)

    in_specs = [pl.BlockSpec(chunk.shape, lambda n, which: (0, 0)) for chunk in chunks]
    in_specs += [
        pl.BlockSpec((chunk.shape[0], tile), lambda n, which, i=i: (which[i], n))
        for i, chunk in enumerate(chunks)
    ]
    operands = list(chunks) + [out_proj] * count
    out_rows = rows
    if before is not None:
        in_specs.append(pl.BlockSpec((rows, tile), lambda n, which: (0, n)))
        operands.append(before)
    if slots is not None:
        in_specs.append(pl.BlockSpec((1,) + slots.shape[1:], lambda n, which: (n, 0, 0)))
        operands.append(slots)
        out_rows = slots.shape[1]
    return pl.pallas_call(
        body,
        out_shape=jax.ShapeDtypeStruct((out_rows, width if slots is None else tile), dtype),
        grid_spec=pltpu.PrefetchScalarGridSpec(
            num_scalar_prefetch=1,
            grid=(width // tile,),
            in_specs=in_specs,
            out_specs=pl.BlockSpec(
                (out_rows, tile), lambda n, which: (0, n if slots is None else 0)
            ),
        ),
        cost_estimate=FREE,
        compiler_params=PARAMS,
        name="context_product",
    )(jnp.stack(places), *operands)


def place_rows(slots, grad_t):
    half = grad_t.shape[0] // 2

    def body(slots_ref, grad_ref, out_ref):
        out_ref[...] = sum(
            lax.dot_general(
                slots_ref[i],
                grad_ref[i * half : (i + 1) * half, :],
                (((1,), (1,)), ((), ())),
                preferred_element_type=F32,
            )
            for i in (0, 1)
        ).astype(BF16)

    return pl.pallas_call(
        body,
        out_shape=jax.ShapeDtypeStruct((slots.shape[1], half), BF16),
        cost_estimate=FREE,
        compiler_params=PARAMS,
        name="place_rows",
    )(slots, grad_t)


def top_up(whole, part, half):
    height, rows = part.shape

    def body(whole_ref, part_ref, out_ref):
        value = whole_ref[...].astype(F32) + part_ref[...].astype(F32)
        out_ref[...] = value.astype(BF16)

    spec = pl.BlockSpec((height, rows), lambda i: (half, 0))
    return pl.pallas_call(
        body,
        out_shape=jax.ShapeDtypeStruct(whole.shape, BF16),
        grid=(1,),
        in_specs=[spec, pl.BlockSpec((height, rows), lambda i: (0, 0))],
        out_specs=spec,
        input_output_aliases={0: 0},
        cost_estimate=FREE,
        compiler_params=PARAMS,
        name="top_up",
    )(whole, part)


def forward_product(out_proj, context, place, split, dtype=F32):
    rows, width = context.shape
    tile = width // 2

    def body(which, proj_ref, context_ref, *out_refs):
        value = lax.dot_general(
            proj_ref[...], context_ref[...], (((1,), (1,)), ((), ())), preferred_element_type=F32
        )
        if split:
            for half in (0, 1):

                @pl.when(pl.program_id(0) == half)
                def _(half=half):
                    out_refs[half][...] = value.astype(BF16)
        else:
            out_refs[0][...] = value.astype(dtype)

    half_spec = pl.BlockSpec((tile, rows), lambda i, which: (0, 0))
    out = pl.pallas_call(
        body,
        out_shape=[jax.ShapeDtypeStruct((tile, rows), BF16)] * 2
        if split
        else [jax.ShapeDtypeStruct((width, rows), dtype)],
        grid_spec=pltpu.PrefetchScalarGridSpec(
            num_scalar_prefetch=1,
            grid=(2,),
            in_specs=[
                pl.BlockSpec((tile, width), lambda i, which: (which[0] * 2 + i, 0)),
                pl.BlockSpec((rows, width), lambda i, which: (0, 0)),
            ],
            out_specs=[half_spec] * 2
            if split
            else [pl.BlockSpec((tile, rows), lambda i, which: (i, 0))],
        ),
        cost_estimate=FREE,
        compiler_params=PARAMS,
        name="forward_product",
    )(place.reshape(1), out_proj, context)
    return out if split else out[0]


def lay_out(chunks, siblings, x, y, c, z):
    block, rows = chunks[0][0].shape[-2:]
    flat = [piece for group in (chunks, siblings) for pieces in group for piece in pieces]
    counts = [[len(pieces) for pieces in group] for group in (chunks, siblings)]

    def body(where, *refs):
        ins, outs, sems = refs[: len(flat)], refs[len(flat) : len(flat) + 4], refs[-1]
        wx, wy, wc, wz = (where[i] for i in range(4))

        def send(src, k, first, slots):
            pltpu.make_async_copy(src, outs[k].at[pl.ds(first, slots)], sems.at[k]).start()

        position = 0
        for owner, group in enumerate(counts):
            for j, count in enumerate(group):
                pieces = ins[position : position + count]
                position += count
                per_piece = 4 // count
                if owner == 0:
                    pieces = [piece.at[:, wc] for piece in pieces]
                for k in range(4):
                    wanted = lax.rem(wy + k, 4)

                    @pl.when((wc == 0) & (lax.rem(j + wz - wx + 4, 4) == k))
                    def _(pieces=pieces, per_piece=per_piece, k=k, owner=owner):
                        for number, piece in enumerate(pieces):
                            send(piece, k, owner * 4 + number * per_piece, per_piece)

                    for number, piece in enumerate(pieces):

                        @pl.when((wc == 1) & (wanted // per_piece == number))
                        def _(piece=piece, number=number, per_piece=per_piece, k=k, owner=owner,
                              j=j, wanted=wanted):
                            slot = wanted - number * per_piece
                            send(piece.at[pl.ds(slot, 1)], k, owner * 4 + j, 1)

        for k in range(4):
            pltpu.make_async_copy(outs[k], outs[k], sems.at[k]).wait()

    out = pl.pallas_call(
        body,
        out_shape=[jax.ShapeDtypeStruct((8, block, rows), BF16)] * 4,
        grid_spec=pltpu.PrefetchScalarGridSpec(
            num_scalar_prefetch=1,
            grid=(1,),
            in_specs=[pl.BlockSpec(memory_space=pltpu.HBM)] * len(flat),
            out_specs=[pl.BlockSpec((8, block, rows), lambda i, where: (0, 0, 0))] * 4,
            scratch_shapes=[pltpu.SemaphoreType.DMA((4,))],
        ),
        cost_estimate=FREE,
        compiler_params=PARAMS,
        name="lay_out",
    )(jnp.stack([x, y, c, z]).astype(jnp.int32), *flat)
    return [value.reshape(8 * block, rows) for value in out]


def weight_product(pieces, contexts, order, block):
    count, tile = len(pieces), 640
    height, rows = pieces[0].shape[0] // 2, pieces[0].shape[1]
    width = contexts[0].shape[1]

    def body(order_ref, *refs):
        outs, total = refs[2 * count : 2 * count + 4], refs[-1]
        total[...] = sum(
            jnp.dot(
                refs[i][core * height : (core + 1) * height, :],
                refs[count + i][core * rows : (core + 1) * rows, :],
                preferred_element_type=F32,
            )
            for i in range(count)
            for core in (0, 1)
        )
        for k in range(4):
            first = pl.multiple_of(order_ref[k] * block, block)
            outs[k][...] = total[pl.ds(first, block), :].astype(outs[k].dtype)

    return pl.pallas_call(
        body,
        out_shape=[jax.ShapeDtypeStruct((block, width), BF16 if k else F32) for k in range(4)],
        grid_spec=pltpu.PrefetchScalarGridSpec(
            num_scalar_prefetch=1,
            grid=(width // tile,),
            in_specs=[pl.BlockSpec((2 * height, rows), lambda n, order: (0, 0)) for _ in pieces]
            + [pl.BlockSpec((2 * rows, tile), lambda n, order: (0, n)) for _ in contexts],
            out_specs=[pl.BlockSpec((block, tile), lambda n, order: (0, n))] * 4,
            scratch_shapes=[pltpu.VMEM((height, tile), F32)],
        ),
        cost_estimate=FREE,
        compiler_params=PARAMS,
        name="weight_product",
    )(order, *pieces, *contexts)


def per_device(
    context, residual, cotangent, out_proj, norm_gain, rewards, group_ids, lengths, destinations
):
    lanes = NX * NY * NC
    rows, width = residual.shape
    full = width * NZ
    x, y, c, z = (lax.axis_index(axis) for axis in ("x", "y", "c", "z"))

    top = width // 2
    far_top, far_bottom = forward_product(out_proj, context, (z + 2) % NZ, True)
    sent_top, sent_bottom = shift(far_top, "z", 1), shift(far_bottom, "z", 3)
    near = forward_product(out_proj, context, (z + 1) % NZ, False, BF16)
    back = forward_product(out_proj, context, (z + 3) % NZ, False, BF16)
    sent_top, sent_bottom, near, back = lax.optimization_barrier(
        (sent_top, sent_bottom, near, back)
    )
    near, back = top_up(near, sent_top, 0), top_up(back, sent_bottom, 1)

    groups = rewards.shape[0] * lanes // GROUP
    member = (group_ids[:, None] == jnp.arange(groups)[None, :]).astype(F32)
    share, _ = lax.optimization_barrier((jnp.sum(member * rewards[:, None], axis=0), near))
    group_total = group_sum(share)
    advantage = rewards - jnp.sum(member * group_total[None, :], axis=1) / GROUP
    scale = advantage * LMAX / (2.0 * lengths.astype(F32))
    live = jnp.arange(LMAX)[None, :] < lengths[:, None]
    row_weights = jnp.where(live, scale[:, None], F32(0.0)).reshape(-1).astype(BF16)

    ready, _ = lax.optimization_barrier((context, near))
    pair = jnp.concatenate([context, shift(ready, "c", 1)], axis=0)
    contexts = [pair, cross(pair, 1, True), None, cross(pair, 3, True)]
    own = forward_product(out_proj, ready, z, False)
    attn_t = own + shift(near, "z", 1).astype(F32) + shift(back, "z", 3).astype(F32)
    attn_t, pair = lax.optimization_barrier((attn_t, pair))
    hidden_t = residual.T.astype(F32) + attn_t
    upstream_t = norm_gain[:, None] * (row_weights.astype(F32)[None, :] * cotangent.T.astype(F32))
    stats = jnp.stack(
        [jnp.sum(hidden_t * hidden_t, axis=0), jnp.sum(upstream_t * hidden_t, axis=0)]
    )
    stats = stats + shift(stats, "z", 1) + shift(stats, "z", 2) + shift(stats, "z", 3)
    inv_rms = lax.rsqrt(stats[0] / full + EPSILON)
    grad_t = (
        inv_rms[None, :] * upstream_t - hidden_t * (inv_rms**3 * stats[1] / full)[None, :]
    ).astype(BF16)

    block = width // (NY * NC)

    def swap(*values):
        parted = [value.reshape(-1, NC, block, rows) for value in values]
        asked = [lax.dynamic_index_in_dim(value, 1 - c, 1, keepdims=False) for value in parted]
        return shift(jnp.concatenate(asked, axis=0).reshape(-1, rows), "c", 1)

    slots = slot_matrix(destinations[:, 0], lanes, rows)
    from_left, from_right = shift(grad_t, "z", 1), shift(grad_t, "z", 3)
    swapped = swap(grad_t)
    grad_rows, _ = lax.optimization_barrier((grad_t, swapped))
    d_residual = exchange(place_rows(slots, grad_rows), lanes)
    context_grad = context_product([grad_t], [z], out_proj)
    from_left, from_right, context_grad, swapped, contexts[1], contexts[3] = (
        lax.optimization_barrier(
            (from_left, from_right, context_grad, swapped, contexts[1], contexts[3])
        )
    )
    contexts[2] = cross(lax.optimization_barrier((pair, contexts[1]))[0], 2, True)
    far_left, far_right = shift(from_left[:top], "z", 1), shift(from_right[top:], "z", 3)
    swapped_left, swapped_right = swap(from_left), swap(from_right)
    context_grad = context_product(
        [from_right, from_left], [(z + 1) % NZ, (z + 3) % NZ], out_proj, before=context_grad
    )
    far_left, far_right, context_grad, swapped_left, swapped_right, contexts[2] = (
        lax.optimization_barrier(
            (far_left, far_right, context_grad, swapped_left, swapped_right, contexts[2])
        )
    )
    def parted(*values):
        return [value.reshape(-1, NC, block, rows) for value in values]

    def single(value):
        return [value.reshape(-1, block, rows)]

    sends = lay_out(
        [parted(grad_t), parted(from_right), parted(far_left, far_right), parted(from_left)],
        [single(value) for value in (swapped, swapped_right, swap(far_left, far_right), swapped_left)],
        x, y, c, z,
    )
    pieces = [sends[0]] + [cross(sends[k], k, True) for k in (1, 2, 3)]
    far_place = (z + 2) % NZ * 2
    placed = context_product(
        [far_left, far_right], [far_place, far_place + 1], out_proj, before=context_grad, slots=slots
    )
    placed, d_residual = lax.optimization_barrier((placed, d_residual))
    d_context = exchange(placed, lanes)
    order = [jnp.where(c == 0, (y + k) % NY, (x + k - z) % NZ) for k in range(4)]
    d_out_proj, *parts = weight_product(pieces, contexts, jnp.stack(order), block)
    for k in (1, 2, 3):
        d_out_proj = d_out_proj + cross(parts[k - 1], k, False).astype(F32)
    return (d_context, d_residual, d_out_proj / lanes)


def solution(mesh):
    wide = Mesh(mesh.devices.reshape(NX, NY, NC, NZ), DP + ("z",))
    placed = (
        P(DP, "z"),
        P(DP, "z"),
        P(DP, "z"),
        P(None, "z"),
        P("z"),
        P(DP),
        P(DP),
        P(DP),
        P(DP, None),
    )
    return jax.shard_map(
        per_device,
        mesh=wide,
        in_specs=placed,
        out_specs=(P(DP, "z"), P(DP, "z"), P(DP, "z")),
        check_vma=False,
    )
```

```python
import jax
import jax.numpy as jnp
from jax import lax
from jax.experimental import pallas as pl
from jax.experimental.pallas import tpu as pltpu
from jax.sharding import Mesh
from jax.sharding import PartitionSpec as P

LMAX = 64
GROUP = 16
PAIR = 3
EPSILON = 1e-06
NX, NY, NC, NZ = 4, 4, 2, 4
DP = ("x", "y", "c")
F32 = jnp.float32
BF16 = jnp.bfloat16


def shift(value, axis, step):
    size = lax.axis_size(axis)
    return lax.ppermute(value, axis, [(i, (i + step) % size) for i in range(size)])


def pick(values, index):
    return lax.dynamic_index_in_dim(values, index, 0, keepdims=False)


def cross(value, step, first):
    pairs = []
    for x in range(NX):
        for y in range(NY):
            for c in range(NC):
                along_x = (c == 0) == first
                to = ((x + step) % NX, y, c) if along_x else (x, (y + step) % NY, c)
                pairs.append(((x * NY + y) * NC + c, (to[0] * NY + to[1]) * NC + to[2]))
    return lax.ppermute(value, DP, pairs)


def group_sum(value):
    copies = jnp.broadcast_to(value, (NX * NY * NC,) + value.shape)
    return jnp.sum(lax.all_to_all(copies, DP, split_axis=0, concat_axis=0, tiled=True), axis=0)


def slot_matrix(owner_dest, lanes, rows):
    count = owner_dest.shape[0]
    per_block = rows // count
    kept = PAIR * per_block
    same = owner_dest[:, None] == owner_dest[None, :]
    earlier = jnp.arange(count)[None, :] < jnp.arange(count)[:, None]
    rank = jnp.sum((same & earlier).astype(jnp.int32), axis=1)
    target = owner_dest * 2 * kept + rank * per_block
    row_target = jnp.repeat(target, per_block) + jnp.tile(jnp.arange(per_block), count)
    row_target = row_target[None, None, :] + kept * jnp.arange(2)[:, None, None]
    return (jnp.arange(lanes * 2 * kept)[None, :, None] == row_target).astype(BF16)


def exchange(packed, lanes):
    height, half = packed.shape
    blocks = packed.reshape((lanes, height // lanes, half))
    got = lax.all_to_all(blocks, DP, split_axis=0, concat_axis=0, tiled=True)
    got = got.reshape((lanes, 2, height // lanes // 2, half))
    return jnp.swapaxes(got, 1, 2).reshape(height // 2, 2 * half)


FREE = pl.CostEstimate(flops=0, bytes_accessed=0, transcendentals=0)
PARAMS = pltpu.CompilerParams(vmem_limit_bytes=48 * 1024 * 1024)


def context_product(chunks, places, out_proj, before=None, slots=None):
    width, rows = out_proj.shape[1], chunks[0].shape[1]
    count, tile = len(chunks), 640
    dtype = F32 if slots is None else BF16

    def body(which, *refs):
        refs = list(refs)
        out_ref = refs.pop()
        total = sum(
            lax.dot_general(
                refs[i][...], refs[count + i][...], (((0,), (0,)), ((), ())), preferred_element_type=F32
            )
            for i in range(count)
        )
        if before is not None:
            total = total + refs[2 * count][...]
        if slots is None:
            out_ref[...] = total
            return
        total = jnp.dot(refs[-1][0], total.astype(BF16), preferred_element_type=F32)

        @pl.when(pl.program_id(0) == 0)
        def _():
            out_ref[...] = total.astype(BF16)

        @pl.when(pl.program_id(0) == 1)
        def _():
            out_ref[...] += total.astype(BF16)

    in_specs = [pl.BlockSpec(chunk.shape, lambda n, which: (0, 0)) for chunk in chunks]
    in_specs += [
        pl.BlockSpec((chunk.shape[0], tile), lambda n, which, i=i: (which[i], n))
        for i, chunk in enumerate(chunks)
    ]
    operands = list(chunks) + [out_proj] * count
    out_rows = rows
    if before is not None:
        in_specs.append(pl.BlockSpec((rows, tile), lambda n, which: (0, n)))
        operands.append(before)
    if slots is not None:
        in_specs.append(pl.BlockSpec((1,) + slots.shape[1:], lambda n, which: (n, 0, 0)))
        operands.append(slots)
        out_rows = slots.shape[1]
    return pl.pallas_call(
        body,
        out_shape=jax.ShapeDtypeStruct((out_rows, width if slots is None else tile), dtype),
        grid_spec=pltpu.PrefetchScalarGridSpec(
            num_scalar_prefetch=1,
            grid=(width // tile,),
            in_specs=in_specs,
            out_specs=pl.BlockSpec(
                (out_rows, tile), lambda n, which: (0, n if slots is None else 0)
            ),
        ),
        cost_estimate=FREE,
        compiler_params=PARAMS,
        name="context_product",
    )(jnp.stack(places), *operands)


def place_rows(slots, grad):
    def body(slots_ref, *refs):
        refs[-1][...] = sum(
            lax.dot_general(
                slots_ref[i], refs[i][...], (((1,), (1,)), ((), ())), preferred_element_type=F32
            )
            for i in (0, 1)
        ).astype(BF16)

    return pl.pallas_call(
        body,
        out_shape=jax.ShapeDtypeStruct((slots.shape[1], grad[0].shape[0]), BF16),
        cost_estimate=FREE,
        compiler_params=PARAMS,
        name="place_rows",
    )(slots, *grad)


def top_up(whole, part, half):
    height, rows = part.shape

    def body(whole_ref, part_ref, out_ref):
        value = whole_ref[...].astype(F32) + part_ref[...].astype(F32)
        out_ref[...] = value.astype(BF16)

    spec = pl.BlockSpec((height, rows), lambda i: (half, 0))
    return pl.pallas_call(
        body,
        out_shape=jax.ShapeDtypeStruct(whole.shape, BF16),
        grid=(1,),
        in_specs=[spec, pl.BlockSpec((height, rows), lambda i: (0, 0))],
        out_specs=spec,
        input_output_aliases={0: 0},
        cost_estimate=FREE,
        compiler_params=PARAMS,
        name="top_up",
    )(whole, part)


def forward_product(out_proj, context, place, split, dtype=F32):
    rows, width = context.shape
    tile = width // 2

    def body(which, proj_ref, context_ref, *out_refs):
        value = lax.dot_general(
            proj_ref[...], context_ref[...], (((1,), (1,)), ((), ())), preferred_element_type=F32
        )
        if split:
            for half in (0, 1):

                @pl.when(pl.program_id(0) == half)
                def _(half=half):
                    out_refs[half][...] = value.astype(BF16)
        else:
            out_refs[0][...] = value.astype(dtype)

    half_spec = pl.BlockSpec((tile, rows), lambda i, which: (0, 0))
    out = pl.pallas_call(
        body,
        out_shape=[jax.ShapeDtypeStruct((tile, rows), BF16)] * 2
        if split
        else [jax.ShapeDtypeStruct((width, rows), dtype)],
        grid_spec=pltpu.PrefetchScalarGridSpec(
            num_scalar_prefetch=1,
            grid=(2,),
            in_specs=[
                pl.BlockSpec((tile, width), lambda i, which: (which[0] * 2 + i, 0)),
                pl.BlockSpec((rows, width), lambda i, which: (0, 0)),
            ],
            out_specs=[half_spec] * 2
            if split
            else [pl.BlockSpec((tile, rows), lambda i, which: (i, 0))],
        ),
        cost_estimate=FREE,
        compiler_params=PARAMS,
        name="forward_product",
    )(place.reshape(1), out_proj, context)
    return out if split else out[0]


def lay_out(chunks, siblings, x, y, c, z):
    block, rows = chunks[0][0].shape[-2:]
    flat = [piece for group in (chunks, siblings) for pieces in group for piece in pieces]
    counts = [[len(pieces) for pieces in group] for group in (chunks, siblings)]

    def body(where, *refs):
        ins, outs, sems = refs[: len(flat)], refs[len(flat) : len(flat) + 4], refs[-1]
        wx, wy, wc, wz = (where[i] for i in range(4))

        def send(src, k, first, slots):
            pltpu.make_async_copy(src, outs[k].at[pl.ds(first, slots)], sems.at[k]).start()

        position = 0
        for owner, group in enumerate(counts):
            for j, count in enumerate(group):
                pieces = ins[position : position + count]
                position += count
                per_piece = 4 // count
                if owner == 0:
                    pieces = [piece.at[:, wc] for piece in pieces]
                for k in range(4):
                    wanted = lax.rem(wy + k, 4)

                    @pl.when((wc == 0) & (lax.rem(j + wz - wx + 4, 4) == k))
                    def _(pieces=pieces, per_piece=per_piece, k=k, owner=owner):
                        for number, piece in enumerate(pieces):
                            send(piece, k, owner * 4 + number * per_piece, per_piece)

                    for number, piece in enumerate(pieces):

                        @pl.when((wc == 1) & (wanted // per_piece == number))
                        def _(piece=piece, number=number, per_piece=per_piece, k=k, owner=owner,
                              j=j, wanted=wanted):
                            slot = wanted - number * per_piece
                            send(piece.at[pl.ds(slot, 1)], k, owner * 4 + j, 1)

        for k in range(4):
            pltpu.make_async_copy(outs[k], outs[k], sems.at[k]).wait()

    out = pl.pallas_call(
        body,
        out_shape=[jax.ShapeDtypeStruct((8, block, rows), BF16)] * 4,
        grid_spec=pltpu.PrefetchScalarGridSpec(
            num_scalar_prefetch=1,
            grid=(1,),
            in_specs=[pl.BlockSpec(memory_space=pltpu.HBM)] * len(flat),
            out_specs=[pl.BlockSpec((8, block, rows), lambda i, where: (0, 0, 0))] * 4,
            scratch_shapes=[pltpu.SemaphoreType.DMA((4,))],
        ),
        cost_estimate=FREE,
        compiler_params=PARAMS,
        name="lay_out",
    )(jnp.stack([x, y, c, z]).astype(jnp.int32), *flat)
    return [value.reshape(8 * block, rows) for value in out]


def per_device(
    context, residual, cotangent, out_proj, norm_gain, rewards, group_ids, lengths, destinations
):
    lanes = NX * NY * NC
    rows, width = residual.shape
    full = width * NZ
    x, y, c, z = (lax.axis_index(axis) for axis in ("x", "y", "c", "z"))

    top = width // 2
    far_top, far_bottom = forward_product(out_proj, context, (z + 2) % NZ, True)
    ready, _ = lax.optimization_barrier((context, far_top))
    pair = jnp.concatenate([context, shift(ready, "c", 1)], axis=0)
    sent_top, sent_bottom = shift(far_top, "z", 1), shift(far_bottom, "z", 3)
    near = forward_product(out_proj, context, (z + 1) % NZ, False, BF16)
    back = forward_product(out_proj, context, (z + 3) % NZ, False, BF16)
    sent_top, sent_bottom, near, back, pair = lax.optimization_barrier(
        (sent_top, sent_bottom, near, back, pair)
    )
    near, back = top_up(near, sent_top, 0), top_up(back, sent_bottom, 1)

    contexts = [pair, cross(pair, 1, True), None, cross(pair, 3, True)]
    ready, _ = lax.optimization_barrier((context, near))
    own = forward_product(out_proj, ready, z, False)
    attn_t = own + shift(near, "z", 1).astype(F32) + shift(back, "z", 3).astype(F32)
    attn_t, contexts[1], contexts[3] = lax.optimization_barrier(
        (attn_t, contexts[1], contexts[3])
    )

    groups = rewards.shape[0] * lanes // GROUP
    member = (group_ids[:, None] == jnp.arange(groups)[None, :]).astype(F32)
    share, _ = lax.optimization_barrier((jnp.sum(member * rewards[:, None], axis=0), own))
    group_total = group_sum(share)
    advantage = rewards - jnp.sum(member * group_total[None, :], axis=1) / GROUP
    scale = advantage * LMAX / (2.0 * lengths.astype(F32))
    live = jnp.arange(LMAX)[None, :] < lengths[:, None]
    row_weights = jnp.where(live, scale[:, None], F32(0.0)).reshape(-1).astype(BF16).astype(F32)

    hidden_t = residual.T.astype(F32) + attn_t
    gained_t = norm_gain[:, None] * cotangent.T.astype(F32)
    stats = jnp.stack(
        [jnp.sum(hidden_t * hidden_t, axis=0), jnp.sum(gained_t * hidden_t, axis=0)]
    )
    stats = stats + shift(stats, "z", 1) + shift(stats, "z", 2) + shift(stats, "z", 3)
    inv_rms = lax.rsqrt(stats[0] / full + EPSILON)
    up_scale = inv_rms * row_weights
    hidden_scale = inv_rms**3 * (row_weights * stats[1]) / full
    grad = [
        (up_scale[None, :] * gained_t[rows_of] - hidden_t[rows_of] * hidden_scale[None, :]).astype(BF16)
        for rows_of in (slice(0, top), slice(top, width))
    ]

    block = width // (NY * NC)

    def swap(*values):
        parted = [value.reshape(-1, NC, block, rows) for value in values]
        asked = [lax.dynamic_index_in_dim(value, 1 - c, 1, keepdims=False) for value in parted]
        return shift(jnp.concatenate(asked, axis=0).reshape(-1, rows), "c", 1)

    def places(step):
        return [(z + step) % NZ * 2, (z + step) % NZ * 2 + 1]

    slots = slot_matrix(destinations[:, 0], lanes, rows)
    left, right = [shift(grad[0], "z", 1), None], [None, shift(grad[1], "z", 3)]
    left[1], right[0] = shift(grad[1], "z", 1), shift(grad[0], "z", 3)
    far = [shift(left[0], "z", 1), shift(right[1], "z", 3)]
    swapped = swap(*grad)
    grad_rows, late_pair, _ = lax.optimization_barrier((tuple(grad), pair, swapped))
    contexts[2] = cross(late_pair, 2, True)
    d_residual = exchange(place_rows(slots, grad_rows), lanes)
    context_grad = context_product(grad, places(0), out_proj)
    (left, right, context_grad, contexts[2]) = lax.optimization_barrier(
        (left, right, context_grad, contexts[2])
    )
    context_grad = context_product(
        right + left, places(1) + places(3), out_proj, before=context_grad
    )
    swap_left, swap_right, _ = lax.optimization_barrier((left, right, context_grad))
    swapped_near = swap(*swap_right, *swap_left)
    far, context_grad, swapped_near = lax.optimization_barrier((far, context_grad, swapped_near))

    def blocks(values):
        return [value.reshape(-1, NC, block, rows) for value in values]

    swapped_near = swapped_near.reshape(2, 4, block, rows)
    sends = lay_out(
        [blocks(grad), blocks(right), blocks(far), blocks(left)],
        [
            [swapped.reshape(4, block, rows)],
            [swapped_near[0]],
            [swap(*far).reshape(4, block, rows)],
            [swapped_near[1]],
        ],
        x, y, c, z,
    )
    sends, d_residual = lax.optimization_barrier((sends, d_residual))
    pieces = [sends[0]] + [cross(sends[k], k, True) for k in (1, 2, 3)]
    placed = context_product(far, places(2), out_proj, before=context_grad, slots=slots)
    d_context = exchange(placed, lanes)

    total = 0.0
    for k in (0, 1, 3, 2):
        for core in (0, 1):
            total = total + jnp.dot(
                pieces[k].reshape(2, -1, rows)[core],
                contexts[k].reshape(2, rows, width)[core],
                preferred_element_type=F32,
            )
    total = total.reshape(4, block, width)
    order = [jnp.where(c == 0, (y + k) % NY, (x + k - z) % NZ) for k in range(4)]
    d_out_proj = pick(total, order[0])
    for k in (1, 2, 3):
        d_out_proj = d_out_proj + cross(pick(total, order[k]).astype(BF16), k, False).astype(F32)
    return (d_context, d_residual, d_out_proj / lanes)


def solution(mesh):
    wide = Mesh(mesh.devices.reshape(NX, NY, NC, NZ), DP + ("z",))
    placed = (
        P(DP, "z"),
        P(DP, "z"),
        P(DP, "z"),
        P(None, "z"),
        P("z"),
        P(DP),
        P(DP),
        P(DP),
        P(DP, None),
    )
    return jax.shard_map(
        per_device,
        mesh=wide,
        in_specs=placed,
        out_specs=(P(DP, "z"), P(DP, "z"), P(DP, "z")),
        check_vma=False,
    )
```

```python
import jax
import jax.numpy as jnp
from jax import lax
from jax.experimental import pallas as pl
from jax.experimental.pallas import tpu as pltpu
from jax.sharding import Mesh
from jax.sharding import PartitionSpec as P

LMAX = 64
GROUP = 16
PAIR = 3
BLOCK_ROWS = 4
EPSILON = 1e-06
NX, NY, NC, NZ = 4, 4, 2, 4
DP = ("x", "y", "c")
F32 = jnp.float32
BF16 = jnp.bfloat16


def shift(value, axis, step):
    size = lax.axis_size(axis)
    return lax.ppermute(value, axis, [(i, (i + step) % size) for i in range(size)])


def pick(values, index):
    return lax.dynamic_index_in_dim(values, index, 0, keepdims=False)


def cross(value, step, first):
    pairs = []
    for x in range(NX):
        for y in range(NY):
            for c in range(NC):
                along_x = (c == 0) == first
                to = ((x + step) % NX, y, c) if along_x else (x, (y + step) % NY, c)
                pairs.append(((x * NY + y) * NC + c, (to[0] * NY + to[1]) * NC + to[2]))
    return lax.ppermute(value, DP, pairs)


def all_shares(value):
    copies = jnp.broadcast_to(value, (NX * NY * NC,) + value.shape)
    return lax.all_to_all(copies, DP, split_axis=0, concat_axis=0, tiled=True)


def slot_matrix(owner_dest, slots, rows, padded):
    count = owner_dest.shape[0]
    per_block = rows // count
    same = owner_dest[:, None] == owner_dest[None, :]
    earlier = jnp.arange(count)[None, :] < jnp.arange(count)[:, None]
    rank = jnp.sum((same & earlier).astype(jnp.int32), axis=1)
    target = owner_dest * padded + rank * per_block
    row_target = jnp.repeat(target, per_block) + jnp.tile(jnp.arange(per_block), count)
    return (jnp.arange(slots // PAIR * padded)[:, None] == row_target[None, :]).astype(BF16)


def exchange(packed, lanes):
    blocks = packed.reshape((lanes, packed.shape[0] // lanes, packed.shape[1]))
    got = lax.all_to_all(blocks, DP, split_axis=0, concat_axis=0, tiled=True)
    kept = PAIR * BLOCK_ROWS
    return got[:, :kept].reshape(lanes * kept, packed.shape[1])


FREE = pl.CostEstimate(flops=0, bytes_accessed=0, transcendentals=0)
PARAMS = pltpu.CompilerParams(vmem_limit_bytes=48 * 1024 * 1024)


def context_product(chunks, places, out_proj, before=None, slots=None):
    width, rows = out_proj.shape[1], chunks[0].shape[1]
    count, tile = len(chunks), 640
    dtype = F32 if slots is None else BF16

    def body(which, *refs):
        refs = list(refs)
        out_ref = refs.pop()
        total = sum(
            lax.dot_general(
                refs[i][...], refs[count + i][...], (((0,), (0,)), ((), ())), preferred_element_type=F32
            )
            for i in range(count)
        )
        if before is not None:
            total = total + refs[2 * count][...]
        if slots is not None:
            total = jnp.dot(refs[-1][...], total.astype(BF16), preferred_element_type=F32)
        out_ref[...] = total.astype(dtype)

    in_specs = [pl.BlockSpec(chunk.shape, lambda n, which: (0, 0)) for chunk in chunks]
    in_specs += [
        pl.BlockSpec((chunk.shape[0], tile), lambda n, which, i=i: (which[i], n))
        for i, chunk in enumerate(chunks)
    ]
    operands = list(chunks) + [out_proj] * count
    out_rows = rows
    if before is not None:
        in_specs.append(pl.BlockSpec((rows, tile), lambda n, which: (0, n)))
        operands.append(before)
    if slots is not None:
        in_specs.append(pl.BlockSpec(slots.shape, lambda n, which: (0, 0)))
        operands.append(slots)
        out_rows = slots.shape[0]
    return pl.pallas_call(
        body,
        out_shape=jax.ShapeDtypeStruct((out_rows, width), dtype),
        grid_spec=pltpu.PrefetchScalarGridSpec(
            num_scalar_prefetch=1,
            grid=(width // tile,),
            in_specs=in_specs,
            out_specs=pl.BlockSpec((out_rows, tile), lambda n, which: (0, n)),
        ),
        cost_estimate=FREE,
        compiler_params=PARAMS,
        name="context_product",
    )(jnp.stack(places), *operands)


def place_rows(slots, grad_t):
    def body(slots_ref, grad_ref, out_ref):
        out_ref[...] = lax.dot_general(
            slots_ref[...], grad_ref[...], (((1,), (1,)), ((), ())), preferred_element_type=F32
        ).astype(BF16)

    return pl.pallas_call(
        body,
        out_shape=jax.ShapeDtypeStruct((slots.shape[0], grad_t.shape[0]), BF16),
        cost_estimate=FREE,
        compiler_params=PARAMS,
        name="place_rows",
    )(slots, grad_t)


def top_up(whole, part, half):
    height, rows = part.shape

    def body(whole_ref, part_ref, out_ref):
        value = whole_ref[...].astype(F32) + part_ref[...].astype(F32)
        out_ref[...] = value.astype(BF16)

    spec = pl.BlockSpec((height, rows), lambda i: (half, 0))
    return pl.pallas_call(
        body,
        out_shape=jax.ShapeDtypeStruct(whole.shape, BF16),
        grid=(1,),
        in_specs=[spec, pl.BlockSpec((height, rows), lambda i: (0, 0))],
        out_specs=spec,
        input_output_aliases={0: 0},
        cost_estimate=FREE,
        compiler_params=PARAMS,
        name="top_up",
    )(whole, part)


def forward_product(out_proj, context, place, split, dtype=F32):
    rows, width = context.shape
    tile = width // 2

    def body(which, proj_ref, context_ref, *out_refs):
        value = lax.dot_general(
            proj_ref[...], context_ref[...], (((1,), (1,)), ((), ())), preferred_element_type=F32
        )
        if split:
            for half in (0, 1):

                @pl.when(pl.program_id(0) == half)
                def _(half=half):
                    out_refs[half][...] = value.astype(BF16)
        else:
            out_refs[0][...] = value.astype(dtype)

    half_spec = pl.BlockSpec((tile, rows), lambda i, which: (0, 0))
    out = pl.pallas_call(
        body,
        out_shape=[jax.ShapeDtypeStruct((tile, rows), BF16)] * 2
        if split
        else [jax.ShapeDtypeStruct((width, rows), dtype)],
        grid_spec=pltpu.PrefetchScalarGridSpec(
            num_scalar_prefetch=1,
            grid=(2,),
            in_specs=[
                pl.BlockSpec((tile, width), lambda i, which: (which[0] * 2 + i, 0)),
                pl.BlockSpec((rows, width), lambda i, which: (0, 0)),
            ],
            out_specs=[half_spec] * 2
            if split
            else [pl.BlockSpec((tile, rows), lambda i, which: (i, 0))],
        ),
        cost_estimate=FREE,
        compiler_params=PARAMS,
        name="forward_product",
    )(place.reshape(1), out_proj, context)
    return out if split else out[0]


def lay_out(chunks, siblings, x, y, c, z):
    block, rows = chunks[0][0].shape[-2:]
    flat = [piece for group in (chunks, siblings) for pieces in group for piece in pieces]
    counts = [[len(pieces) for pieces in group] for group in (chunks, siblings)]

    def body(where, *refs):
        ins, outs, sems = refs[: len(flat)], refs[len(flat) : len(flat) + 4], refs[-1]
        wx, wy, wc, wz = (where[i] for i in range(4))

        def send(src, k, first, slots):
            pltpu.make_async_copy(src, outs[k].at[pl.ds(first, slots)], sems.at[k]).start()

        position = 0
        for owner, group in enumerate(counts):
            for j, count in enumerate(group):
                pieces = ins[position : position + count]
                position += count
                per_piece = 4 // count
                if owner == 0:
                    pieces = [piece.at[:, wc] for piece in pieces]
                for k in range(4):
                    wanted = lax.rem(wy + k, 4)

                    @pl.when((wc == 0) & (lax.rem(j + wz - wx + 4, 4) == k))
                    def _(pieces=pieces, per_piece=per_piece, k=k, owner=owner):
                        for number, piece in enumerate(pieces):
                            send(piece, k, owner * 4 + number * per_piece, per_piece)

                    for number, piece in enumerate(pieces):

                        @pl.when((wc == 1) & (wanted // per_piece == number))
                        def _(piece=piece, number=number, per_piece=per_piece, k=k, owner=owner,
                              j=j, wanted=wanted):
                            slot = wanted - number * per_piece
                            send(piece.at[pl.ds(slot, 1)], k, owner * 4 + j, 1)

        for k in range(4):
            pltpu.make_async_copy(outs[k], outs[k], sems.at[k]).wait()

    out = pl.pallas_call(
        body,
        out_shape=[jax.ShapeDtypeStruct((8, block, rows), BF16)] * 4,
        grid_spec=pltpu.PrefetchScalarGridSpec(
            num_scalar_prefetch=1,
            grid=(1,),
            in_specs=[pl.BlockSpec(memory_space=pl.ANY)] * len(flat),
            out_specs=[pl.BlockSpec((8, block, rows), lambda i, where: (0, 0, 0))] * 4,
            scratch_shapes=[pltpu.SemaphoreType.DMA((4,))],
        ),
        cost_estimate=FREE,
        compiler_params=PARAMS,
        name="lay_out",
    )(jnp.stack([x, y, c, z]).astype(jnp.int32), *flat)
    return [value.reshape(8 * block, rows) for value in out]


def weight_product(pieces, contexts, order, block):
    count, tile = len(pieces), 640
    height, rows = pieces[0].shape[0] // 2, pieces[0].shape[1]
    width = contexts[0].shape[1]

    def body(order_ref, *refs):
        outs, total = refs[2 * count : 2 * count + 4], refs[-1]
        total[...] = sum(
            jnp.dot(
                refs[i][core * height : (core + 1) * height, :],
                refs[count + i][core * rows : (core + 1) * rows, :],
                preferred_element_type=F32,
            )
            for i in range(count)
            for core in (0, 1)
        )
        for k in range(4):
            first = pl.multiple_of(order_ref[k] * block, block)
            outs[k][...] = total[pl.ds(first, block), :].astype(outs[k].dtype)

    return pl.pallas_call(
        body,
        out_shape=[jax.ShapeDtypeStruct((block, width), BF16 if k else F32) for k in range(4)],
        grid_spec=pltpu.PrefetchScalarGridSpec(
            num_scalar_prefetch=1,
            grid=(width // tile,),
            in_specs=[pl.BlockSpec((2 * height, rows), lambda n, order: (0, 0)) for _ in pieces]
            + [pl.BlockSpec((2 * rows, tile), lambda n, order: (0, n)) for _ in contexts],
            out_specs=[pl.BlockSpec((block, tile), lambda n, order: (0, n))] * 4,
            scratch_shapes=[pltpu.VMEM((height, tile), F32)],
        ),
        cost_estimate=FREE,
        compiler_params=PARAMS,
        name="weight_product",
    )(order, *pieces, *contexts)


def per_device(
    context, residual, cotangent, out_proj, norm_gain, rewards, group_ids, lengths, destinations
):
    lanes = NX * NY * NC
    rows, width = residual.shape
    full = width * NZ
    x, y, c, z = (lax.axis_index(axis) for axis in ("x", "y", "c", "z"))

    top = width // 2
    far_top, far_bottom = forward_product(out_proj, context, (z + 2) % NZ, True)
    ready, _ = lax.optimization_barrier((context, far_top))
    pair = jnp.concatenate([context, shift(ready, "c", 1)], axis=0)
    sent_top, sent_bottom = shift(far_top, "z", 1), shift(far_bottom, "z", 3)
    near = forward_product(out_proj, context, (z + 1) % NZ, False, BF16)
    back = forward_product(out_proj, context, (z + 3) % NZ, False, BF16)
    sent_top, sent_bottom, near, back, pair = lax.optimization_barrier(
        (sent_top, sent_bottom, near, back, pair)
    )
    near, back = top_up(near, sent_top, 0), top_up(back, sent_bottom, 1)

    ready, _, _ = lax.optimization_barrier((context, near, back))
    own = forward_product(out_proj, ready, z, False)
    late_pair, _ = lax.optimization_barrier((pair, own))
    contexts = [pair] + [cross(late_pair, k, True) for k in (1, 2, 3)]
    attn_t = own + shift(near, "z", 1).astype(F32) + shift(back, "z", 3).astype(F32)

    hidden_t = residual.T.astype(F32) + attn_t
    gained_t = norm_gain[:, None] * cotangent.T.astype(F32)
    stats = jnp.stack(
        [jnp.sum(hidden_t * hidden_t, axis=0), jnp.sum(gained_t * hidden_t, axis=0)]
    )
    groups = rewards.shape[0] * lanes // GROUP
    member = (group_ids[:, None] == jnp.arange(groups)[None, :]).astype(F32)
    share, _ = lax.optimization_barrier((jnp.sum(member * rewards[:, None], axis=0), own))
    shares, _ = lax.optimization_barrier((all_shares(share), stats))
    group_total = jnp.sum(shares, axis=0)
    advantage = rewards - jnp.sum(member * group_total[None, :], axis=1) / GROUP
    scale = advantage * LMAX / (2.0 * lengths.astype(F32))
    live = jnp.arange(LMAX)[None, :] < lengths[:, None]
    row_weights = jnp.where(live, scale[:, None], F32(0.0)).reshape(-1).astype(BF16).astype(F32)

    stats = stats + shift(stats, "z", 1) + shift(stats, "z", 2) + shift(stats, "z", 3)
    inv_rms = lax.rsqrt(stats[0] / full + EPSILON)
    up_scale = inv_rms * row_weights
    hidden_scale = inv_rms**3 * (row_weights * stats[1]) / full
    grad_t = (up_scale[None, :] * gained_t - hidden_t * hidden_scale[None, :]).astype(BF16)
    grad_t, contexts[1], contexts[3] = lax.optimization_barrier((grad_t, contexts[1], contexts[3]))

    block = width // (NY * NC)

    def swap(*values):
        parted = [value.reshape(-1, NC, block, rows) for value in values]
        asked = [lax.dynamic_index_in_dim(value, 1 - c, 1, keepdims=False) for value in parted]
        return shift(jnp.concatenate(asked, axis=0).reshape(-1, rows), "c", 1)

    slots = slot_matrix(destinations[:, 0], lanes * PAIR, rows, 16)
    from_left, from_right = shift(grad_t, "z", 1), shift(grad_t, "z", 3)
    swapped = swap(grad_t)
    grad_rows, _ = lax.optimization_barrier((grad_t, swapped))
    d_residual = exchange(place_rows(slots, grad_rows), lanes)
    context_grad = context_product([grad_t], [z], out_proj)
    from_left, from_right, context_grad, swapped, contexts[2] = lax.optimization_barrier(
        (from_left, from_right, context_grad, swapped, contexts[2])
    )
    far_left, far_right = shift(from_left[:top], "z", 1), shift(from_right[top:], "z", 3)
    context_grad = context_product(
        [from_right, from_left], [(z + 1) % NZ, (z + 3) % NZ], out_proj, before=context_grad
    )
    far_left, far_right, context_grad = lax.optimization_barrier(
        (far_left, far_right, context_grad)
    )
    swapped_right, swapped_left = jnp.split(swap(from_right, from_left), 2)
    swapped_far = swap(far_left, far_right)
    def parted(*values):
        return [value.reshape(-1, NC, block, rows) for value in values]

    def single(value):
        return [value.reshape(-1, block, rows)]

    sends = lay_out(
        [parted(grad_t), parted(from_right), parted(far_left, far_right), parted(from_left)],
        [single(value) for value in (swapped, swapped_right, swapped_far, swapped_left)],
        x, y, c, z,
    )
    far_left, far_right, sends = lax.optimization_barrier((far_left, far_right, sends))
    pieces = [sends[0]] + [cross(sends[k], k, True) for k in (1, 2, 3)]
    far_place = (z + 2) % NZ * 2
    placed = context_product(
        [far_left, far_right], [far_place, far_place + 1], out_proj, before=context_grad, slots=slots
    )
    placed, d_residual = lax.optimization_barrier((placed, d_residual))
    d_context = exchange(placed, lanes)
    order = [jnp.where(c == 0, (y + k) % NY, (x + k - z) % NZ) for k in range(4)]
    d_out_proj, *parts = weight_product(pieces, contexts, jnp.stack(order), block)
    for k in (1, 2, 3):
        d_out_proj = d_out_proj + cross(parts[k - 1], k, False).astype(F32)
    return (d_context, d_residual, d_out_proj / lanes)


def solution(mesh):
    wide = Mesh(mesh.devices.reshape(NX, NY, NC, NZ), DP + ("z",))
    placed = (
        P(DP, "z"),
        P(DP, "z"),
        P(DP, "z"),
        P(None, "z"),
        P("z"),
        P(DP),
        P(DP),
        P(DP),
        P(DP, None),
    )
    return jax.shard_map(
        per_device,
        mesh=wide,
        in_specs=placed,
        out_specs=(P(DP, "z"), P(DP, "z"), P(DP, "z")),
        check_vma=False,
    )
```

```python
import jax
import jax.numpy as jnp
from jax import lax
from jax.experimental import pallas as pl
from jax.experimental.pallas import tpu as pltpu
from jax.sharding import Mesh
from jax.sharding import PartitionSpec as P

LMAX = 64
GROUP = 16
PAIR = 3
BLOCK_ROWS = 4
EPSILON = 1e-06
NX, NY, NC, NZ = 4, 4, 2, 4
DP = ("x", "y", "c")
F32 = jnp.float32
BF16 = jnp.bfloat16


def shift(value, axis, step):
    size = lax.axis_size(axis)
    return lax.ppermute(value, axis, [(i, (i + step) % size) for i in range(size)])


def pick(values, index):
    return lax.dynamic_index_in_dim(values, index, 0, keepdims=False)


def cross(value, step, first):
    pairs = []
    for x in range(NX):
        for y in range(NY):
            for c in range(NC):
                along_x = (c == 0) == first
                to = ((x + step) % NX, y, c) if along_x else (x, (y + step) % NY, c)
                pairs.append(((x * NY + y) * NC + c, (to[0] * NY + to[1]) * NC + to[2]))
    return lax.ppermute(value, DP, pairs)


def all_shares(value):
    copies = jnp.broadcast_to(value, (NX * NY * NC,) + value.shape)
    return lax.all_to_all(copies, DP, split_axis=0, concat_axis=0, tiled=True)


def slot_matrix(owner_dest, slots, rows, padded):
    count = owner_dest.shape[0]
    per_block = rows // count
    same = owner_dest[:, None] == owner_dest[None, :]
    earlier = jnp.arange(count)[None, :] < jnp.arange(count)[:, None]
    rank = jnp.sum((same & earlier).astype(jnp.int32), axis=1)
    target = owner_dest * padded + rank * per_block
    row_target = jnp.repeat(target, per_block) + jnp.tile(jnp.arange(per_block), count)
    return (jnp.arange(slots // PAIR * padded)[:, None] == row_target[None, :]).astype(BF16)


def exchange(packed, lanes):
    blocks = packed.reshape((lanes, packed.shape[0] // lanes, packed.shape[1]))
    return lax.all_to_all(blocks, DP, split_axis=0, concat_axis=0, tiled=True)


def learner_rows(got):
    kept = PAIR * BLOCK_ROWS
    return got[:, :kept].reshape(got.shape[0] * kept, got.shape[2])


FREE = pl.CostEstimate(flops=0, bytes_accessed=0, transcendentals=0)
PARAMS = pltpu.CompilerParams(vmem_limit_bytes=48 * 1024 * 1024)


def context_product(chunks, places, out_proj, before=None, slots=None):
    width, rows = out_proj.shape[1], chunks[0].shape[1]
    count, tile = len(chunks), 640
    dtype = F32 if slots is None else BF16

    def body(which, *refs):
        refs = list(refs)
        out_ref = refs.pop()
        total = sum(
            lax.dot_general(
                refs[i][...], refs[count + i][...], (((0,), (0,)), ((), ())), preferred_element_type=F32
            )
            for i in range(count)
        )
        if before is not None:
            total = total + refs[2 * count][...]
        if slots is not None:
            total = jnp.dot(refs[-1][...], total.astype(BF16), preferred_element_type=F32)
        out_ref[...] = total.astype(dtype)

    in_specs = [pl.BlockSpec(chunk.shape, lambda n, which: (0, 0)) for chunk in chunks]
    in_specs += [
        pl.BlockSpec((chunk.shape[0], tile), lambda n, which, i=i: (which[i], n))
        for i, chunk in enumerate(chunks)
    ]
    operands = list(chunks) + [out_proj] * count
    out_rows = rows
    if before is not None:
        in_specs.append(pl.BlockSpec((rows, tile), lambda n, which: (0, n)))
        operands.append(before)
    if slots is not None:
        in_specs.append(pl.BlockSpec(slots.shape, lambda n, which: (0, 0)))
        operands.append(slots)
        out_rows = slots.shape[0]
    return pl.pallas_call(
        body,
        out_shape=jax.ShapeDtypeStruct((out_rows, width), dtype),
        grid_spec=pltpu.PrefetchScalarGridSpec(
            num_scalar_prefetch=1,
            grid=(width // tile,),
            in_specs=in_specs,
            out_specs=pl.BlockSpec((out_rows, tile), lambda n, which: (0, n)),
        ),
        cost_estimate=FREE,
        compiler_params=PARAMS,
        name="context_product",
    )(jnp.stack(places), *operands)


def place_rows(slots, grad_t):
    def body(slots_ref, grad_ref, out_ref):
        out_ref[...] = lax.dot_general(
            slots_ref[...], grad_ref[...], (((1,), (1,)), ((), ())), preferred_element_type=F32
        ).astype(BF16)

    return pl.pallas_call(
        body,
        out_shape=jax.ShapeDtypeStruct((slots.shape[0], grad_t.shape[0]), BF16),
        cost_estimate=FREE,
        compiler_params=PARAMS,
        name="place_rows",
    )(slots, grad_t)


def top_up(near, near_part, back, back_part):
    height, rows = near_part.shape

    def body(*refs):
        for i in (0, 1):
            value = refs[2 * i][...].astype(F32) + refs[2 * i + 1][...].astype(F32)
            refs[4 + i][...] = value.astype(BF16)

    top = pl.BlockSpec((height, rows), lambda i: (0, 0))
    bottom = pl.BlockSpec((height, rows), lambda i: (1, 0))
    return pl.pallas_call(
        body,
        out_shape=[jax.ShapeDtypeStruct(near.shape, BF16)] * 2,
        grid=(1,),
        in_specs=[top, top, bottom, top],
        out_specs=[top, bottom],
        input_output_aliases={0: 0, 2: 1},
        cost_estimate=FREE,
        compiler_params=PARAMS,
        name="top_up",
    )(near, near_part, back, back_part)


def forward_product(out_proj, context, place, split, dtype=F32):
    rows, width = context.shape
    tile = width // 2

    def body(which, proj_ref, context_ref, *out_refs):
        value = lax.dot_general(
            proj_ref[...], context_ref[...], (((1,), (1,)), ((), ())), preferred_element_type=F32
        )
        if split:
            for half in (0, 1):

                @pl.when(pl.program_id(0) == half)
                def _(half=half):
                    out_refs[half][...] = value.astype(BF16)
        else:
            out_refs[0][...] = value.astype(dtype)

    half_spec = pl.BlockSpec((tile, rows), lambda i, which: (0, 0))
    out = pl.pallas_call(
        body,
        out_shape=[jax.ShapeDtypeStruct((tile, rows), BF16)] * 2
        if split
        else [jax.ShapeDtypeStruct((width, rows), dtype)],
        grid_spec=pltpu.PrefetchScalarGridSpec(
            num_scalar_prefetch=1,
            grid=(2,),
            in_specs=[
                pl.BlockSpec((tile, width), lambda i, which: (which[0] * 2 + i, 0)),
                pl.BlockSpec((rows, width), lambda i, which: (0, 0)),
            ],
            out_specs=[half_spec] * 2
            if split
            else [pl.BlockSpec((tile, rows), lambda i, which: (i, 0))],
        ),
        cost_estimate=FREE,
        compiler_params=PARAMS,
        name="forward_product",
    )(place.reshape(1), out_proj, context)
    return out if split else out[0]


def hidden_part(out_proj, context, residual, cotangent, norm_gain, place):
    rows, width = context.shape
    tile = width // 2

    def body(which, proj_ref, context_ref, residual_ref, cotangent_ref, gain_ref, hidden_ref, gained_ref):
        value = lax.dot_general(
            proj_ref[...], context_ref[...], (((1,), (1,)), ((), ())), preferred_element_type=F32
        )
        hidden_ref[...] = value + residual_ref[...].astype(F32).T
        gained_ref[...] = (gain_ref[...] * cotangent_ref[...].astype(F32)).T

    columns = pl.BlockSpec((rows, tile), lambda i, which: (0, i))
    return pl.pallas_call(
        body,
        out_shape=[jax.ShapeDtypeStruct((width, rows), F32)] * 2,
        grid_spec=pltpu.PrefetchScalarGridSpec(
            num_scalar_prefetch=1,
            grid=(2,),
            in_specs=[
                pl.BlockSpec((tile, width), lambda i, which: (which[0] * 2 + i, 0)),
                pl.BlockSpec((rows, width), lambda i, which: (0, 0)),
                columns,
                columns,
                pl.BlockSpec((1, tile), lambda i, which: (0, i)),
            ],
            out_specs=[pl.BlockSpec((tile, rows), lambda i, which: (i, 0))] * 2,
        ),
        cost_estimate=FREE,
        compiler_params=PARAMS,
        name="hidden_part",
    )(place.reshape(1), out_proj, context, residual, cotangent, norm_gain.reshape(1, width))


def lay_out(steps, chunks, siblings, x, y, c, z):
    block, rows = chunks[0][0].shape[-2:]
    arrays, places = [], []
    for value in [piece for pieces in chunks for piece in pieces] + [pieces[0][0] for pieces in siblings]:
        known = [i for i, other in enumerate(arrays) if other is value]
        places.append(known[0] if known else len(arrays))
        if not known:
            arrays.append(value)
    count_of = len(arrays)

    def body(where, *refs):
        ins, outs, sems = refs[:count_of], refs[count_of : count_of + len(steps)], refs[-1]
        wx, wy, wc, wz = (where[i] for i in range(4))

        def send(src, number, first, slots):
            pltpu.make_async_copy(
                src, outs[number].at[pl.ds(first, slots)], sems.at[number]
            ).start()

        position = 0
        for owner, group in enumerate((chunks, siblings)):
            for j, members in enumerate(group):
                per_piece = 4 // len(members)
                pieces = []
                for member in members:
                    ref = ins[places[position]]
                    position += 1
                    pieces.append(ref.at[:, wc] if owner == 0 else ref.at[pl.ds(member[1], 4)])
                for number, k in enumerate(steps):
                    wanted = lax.rem(wy + k, 4)

                    @pl.when((wc == 0) & (lax.rem(j + wz - wx + 4, 4) == k))
                    def _(pieces=pieces, per_piece=per_piece, number=number, owner=owner):
                        for i, piece in enumerate(pieces):
                            send(piece, number, owner * 4 + i * per_piece, per_piece)

                    for i, piece in enumerate(pieces):

                        @pl.when((wc == 1) & (wanted // per_piece == i))
                        def _(piece=piece, i=i, per_piece=per_piece, number=number, owner=owner,
                              j=j, wanted=wanted):
                            slot = wanted - i * per_piece
                            send(piece.at[pl.ds(slot, 1)], number, owner * 4 + j, 1)

        for number in range(len(steps)):
            pltpu.make_async_copy(outs[number], outs[number], sems.at[number]).wait()

    out = pl.pallas_call(
        body,
        out_shape=[jax.ShapeDtypeStruct((8, block, rows), BF16)] * len(steps),
        grid_spec=pltpu.PrefetchScalarGridSpec(
            num_scalar_prefetch=1,
            grid=(1,),
            in_specs=[pl.BlockSpec(memory_space=pl.ANY)] * count_of,
            out_specs=[pl.BlockSpec((8, block, rows), lambda i, where: (0, 0, 0))] * len(steps),
            scratch_shapes=[pltpu.SemaphoreType.DMA((len(steps),))],
        ),
        cost_estimate=FREE,
        compiler_params=pltpu.CompilerParams(vmem_limit_bytes=16 * 1024 * 1024),
        name="lay_out",
    )(jnp.stack([x, y, c, z]).astype(jnp.int32), *arrays)
    return [value.reshape(8 * block, rows) for value in out]


def weight_product(pieces, contexts, order, block):
    count, tile = len(pieces), 640
    height, rows = pieces[0].shape[0] // 2, pieces[0].shape[1]
    width = contexts[0].shape[1]

    def body(order_ref, *refs):
        outs, total = refs[2 * count : 2 * count + 4], refs[-1]
        total[...] = sum(
            jnp.dot(
                refs[i][core * height : (core + 1) * height, :],
                refs[count + i][core * rows : (core + 1) * rows, :],
                preferred_element_type=F32,
            )
            for i in range(count)
            for core in (0, 1)
        )
        for k in range(4):
            first = pl.multiple_of(order_ref[k] * block, block)
            outs[k][...] = total[pl.ds(first, block), :].astype(outs[k].dtype)

    return pl.pallas_call(
        body,
        out_shape=[jax.ShapeDtypeStruct((block, width), BF16 if k else F32) for k in range(4)],
        grid_spec=pltpu.PrefetchScalarGridSpec(
            num_scalar_prefetch=1,
            grid=(width // tile,),
            in_specs=[pl.BlockSpec((2 * height, rows), lambda n, order: (0, 0)) for _ in pieces]
            + [pl.BlockSpec((2 * rows, tile), lambda n, order: (0, n)) for _ in contexts],
            out_specs=[pl.BlockSpec((block, tile), lambda n, order: (0, n))] * 4,
            scratch_shapes=[pltpu.VMEM((height, tile), F32)],
        ),
        cost_estimate=FREE,
        compiler_params=pltpu.CompilerParams(vmem_limit_bytes=56 * 1024 * 1024),
        name="weight_product",
    )(order, *pieces, *contexts)


def per_device(
    context, residual, cotangent, out_proj, norm_gain, rewards, group_ids, lengths, destinations
):
    lanes = NX * NY * NC
    rows, width = residual.shape
    full = width * NZ
    x, y, c, z = (lax.axis_index(axis) for axis in ("x", "y", "c", "z"))

    top = width // 2
    far_top, far_bottom = forward_product(out_proj, context, (z + 2) % NZ, True)
    ready, _ = lax.optimization_barrier((context, far_top))
    pair = jnp.concatenate([context, shift(ready, "c", 1)], axis=0)
    sent_top, sent_bottom = shift(far_top, "z", 1), shift(far_bottom, "z", 3)
    near = forward_product(out_proj, context, (z + 1) % NZ, False, BF16)
    back = forward_product(out_proj, context, (z + 3) % NZ, False, BF16)
    sent_top, sent_bottom, near, back = lax.optimization_barrier(
        (sent_top, sent_bottom, near, back)
    )
    near, back = top_up(near, sent_top, back, sent_bottom)

    groups = rewards.shape[0] * lanes // GROUP
    member = (group_ids[:, None] == jnp.arange(groups)[None, :]).astype(F32)
    share, _ = lax.optimization_barrier((jnp.sum(member * rewards[:, None], axis=0), near))
    ready, _ = lax.optimization_barrier((context, share))
    own, gained_t = hidden_part(out_proj, ready, residual, cotangent, norm_gain, z)
    late_pair, _ = lax.optimization_barrier((pair, own))
    contexts = [pair] + [cross(late_pair, k, True) for k in (1, 2, 3)]
    hidden_t = own + shift(near, "z", 1).astype(F32) + shift(back, "z", 3).astype(F32)

    stats = jnp.stack(
        [jnp.sum(hidden_t * hidden_t, axis=0), jnp.sum(gained_t * hidden_t, axis=0)]
    )
    shares, _ = lax.optimization_barrier((all_shares(share), stats))
    group_total = jnp.sum(shares, axis=0)
    advantage = rewards - jnp.sum(member * group_total[None, :], axis=1) / GROUP
    scale = advantage * LMAX / (2.0 * lengths.astype(F32))
    live = jnp.arange(LMAX)[None, :] < lengths[:, None]
    row_weights = jnp.where(live, scale[:, None], F32(0.0)).reshape(-1).astype(BF16).astype(F32)

    stats = stats + shift(stats, "z", 1) + shift(stats, "z", 2) + shift(stats, "z", 3)
    inv_rms = lax.rsqrt(stats[0] / full + EPSILON)
    up_scale = inv_rms * row_weights
    hidden_scale = inv_rms**3 * (row_weights * stats[1]) / full
    grad_t = (up_scale[None, :] * gained_t - hidden_t * hidden_scale[None, :]).astype(BF16)
    grad_t, contexts[1], contexts[3] = lax.optimization_barrier((grad_t, contexts[1], contexts[3]))

    block = width // (NY * NC)

    def swap(*values):
        parted = [value.reshape(-1, NC, block, rows) for value in values]
        asked = [lax.dynamic_index_in_dim(value, 1 - c, 1, keepdims=False) for value in parted]
        return shift(jnp.concatenate(asked, axis=0).reshape(-1, rows), "c", 1)

    slots = slot_matrix(destinations[:, 0], lanes * PAIR, rows, 16)
    from_left, from_right = shift(grad_t, "z", 1), shift(grad_t, "z", 3)
    swapped = swap(grad_t)
    grad_rows, _ = lax.optimization_barrier((grad_t, swapped))
    d_residual = exchange(place_rows(slots, grad_rows), lanes)
    context_grad = context_product([grad_t], [z], out_proj)
    from_left, from_right, context_grad, swapped, contexts[2] = lax.optimization_barrier(
        (from_left, from_right, context_grad, swapped, contexts[2])
    )
    far_left, far_right = shift(from_left[:top], "z", 1), shift(from_right[top:], "z", 3)
    context_grad = context_product(
        [from_right, from_left], [(z + 1) % NZ, (z + 3) % NZ], out_proj, before=context_grad
    )
    far_left, far_right, context_grad = lax.optimization_barrier(
        (far_left, far_right, context_grad)
    )
    swapped_near = swap(from_right, from_left).reshape(8, block, rows)
    swapped_far = swap(far_left, far_right).reshape(4, block, rows)
    swapped_own = swapped.reshape(4, block, rows)

    def parted(*values):
        return [value.reshape(-1, NC, block, rows) for value in values]

    chunks = [parted(grad_t), parted(from_right), parted(far_left, far_right), parted(from_left)]
    siblings = [
        [(swapped_own, 0)], [(swapped_near[:4], 0)], [(swapped_far, 0)], [(swapped_near[4:], 0)]
    ]
    sends = lay_out((0, 1, 2, 3), chunks, siblings, x, y, c, z)
    far_left, far_right, sends = lax.optimization_barrier((far_left, far_right, sends))
    pieces = [sends[0]] + [cross(sends[k], k, True) for k in (1, 2, 3)]
    far_place = (z + 2) % NZ * 2
    placed = context_product(
        [far_left, far_right], [far_place, far_place + 1], out_proj, before=context_grad, slots=slots
    )
    placed, d_residual = lax.optimization_barrier((placed, d_residual))
    d_context = exchange(placed, lanes)
    order = [jnp.where(c == 0, (y + k) % NY, (x + k - z) % NZ) for k in range(4)]
    d_out_proj, *parts = weight_product(pieces, contexts, jnp.stack(order), block)
    parts = [cross(part, k, False) for k, part in zip((1, 2, 3), parts)]
    for part in parts:
        d_out_proj = d_out_proj + part.astype(F32)
    return (learner_rows(d_context), learner_rows(d_residual), d_out_proj / lanes)


def solution(mesh):
    wide = Mesh(mesh.devices.reshape(NX, NY, NC, NZ), DP + ("z",))
    placed = (
        P(DP, "z"),
        P(DP, "z"),
        P(DP, "z"),
        P(None, "z"),
        P("z"),
        P(DP),
        P(DP),
        P(DP),
        P(DP, None),
    )
    return jax.shard_map(
        per_device,
        mesh=wide,
        in_specs=placed,
        out_specs=(P(DP, "z"), P(DP, "z"), P(DP, "z")),
        check_vma=False,
    )
```

```python
import jax
import jax.numpy as jnp
from jax import lax
from jax.experimental import pallas as pl
from jax.experimental.pallas import tpu as pltpu
from jax.sharding import Mesh
from jax.sharding import PartitionSpec as P

LMAX = 64
GROUP = 16
PAIR = 3
BLOCK_ROWS = 4
EPSILON = 1e-06
NX, NY, NC, NZ = 4, 4, 2, 4
DP = ("x", "y", "c")
F32 = jnp.float32
BF16 = jnp.bfloat16


def shift(value, axis, step):
    size = lax.axis_size(axis)
    return lax.ppermute(value, axis, [(i, (i + step) % size) for i in range(size)])


def pick(values, index):
    return lax.dynamic_index_in_dim(values, index, 0, keepdims=False)


def cross(value, step, first):
    pairs = []
    for x in range(NX):
        for y in range(NY):
            for c in range(NC):
                along_x = (c == 0) == first
                to = ((x + step) % NX, y, c) if along_x else (x, (y + step) % NY, c)
                pairs.append(((x * NY + y) * NC + c, (to[0] * NY + to[1]) * NC + to[2]))
    return lax.ppermute(value, DP, pairs)


def all_shares(value):
    copies = jnp.broadcast_to(value, (NX * NY * NC,) + value.shape)
    return lax.all_to_all(copies, DP, split_axis=0, concat_axis=0, tiled=True)


def slot_matrix(owner_dest, slots, rows, padded):
    count = owner_dest.shape[0]
    per_block = rows // count
    same = owner_dest[:, None] == owner_dest[None, :]
    earlier = jnp.arange(count)[None, :] < jnp.arange(count)[:, None]
    rank = jnp.sum((same & earlier).astype(jnp.int32), axis=1)
    target = owner_dest * padded + rank * per_block
    row_target = jnp.repeat(target, per_block) + jnp.tile(jnp.arange(per_block), count)
    return (jnp.arange(slots // PAIR * padded)[:, None] == row_target[None, :]).astype(BF16)


def exchange(packed, lanes):
    blocks = packed.reshape((lanes, packed.shape[0] // lanes, packed.shape[1]))
    return lax.all_to_all(blocks, DP, split_axis=0, concat_axis=0, tiled=True)


def learner_rows(got):
    kept = PAIR * BLOCK_ROWS
    return got[:, :kept].reshape(got.shape[0] * kept, got.shape[2])


FREE = pl.CostEstimate(flops=0, bytes_accessed=0, transcendentals=0)
PARAMS = pltpu.CompilerParams(vmem_limit_bytes=48 * 1024 * 1024)


def context_product(chunks, places, out_proj, before=None, slots=None):
    width, rows = out_proj.shape[1], chunks[0].shape[1]
    count, tile = len(chunks), 640
    dtype = F32 if slots is None else BF16

    def body(which, *refs):
        refs = list(refs)
        out_ref = refs.pop()
        total = sum(
            lax.dot_general(
                refs[i][...], refs[count + i][...], (((0,), (0,)), ((), ())), preferred_element_type=F32
            )
            for i in range(count)
        )
        if before is not None:
            total = total + refs[2 * count][...]
        if slots is not None:
            total = jnp.dot(refs[-1][...], total.astype(BF16), preferred_element_type=F32)
        out_ref[...] = total.astype(dtype)

    in_specs = [pl.BlockSpec(chunk.shape, lambda n, which: (0, 0)) for chunk in chunks]
    in_specs += [
        pl.BlockSpec((chunk.shape[0], tile), lambda n, which, i=i: (which[i], n))
        for i, chunk in enumerate(chunks)
    ]
    operands = list(chunks) + [out_proj] * count
    out_rows = rows
    if before is not None:
        in_specs.append(pl.BlockSpec((rows, tile), lambda n, which: (0, n)))
        operands.append(before)
    if slots is not None:
        in_specs.append(pl.BlockSpec(slots.shape, lambda n, which: (0, 0)))
        operands.append(slots)
        out_rows = slots.shape[0]
    return pl.pallas_call(
        body,
        out_shape=jax.ShapeDtypeStruct((out_rows, width), dtype),
        grid_spec=pltpu.PrefetchScalarGridSpec(
            num_scalar_prefetch=1,
            grid=(width // tile,),
            in_specs=in_specs,
            out_specs=pl.BlockSpec((out_rows, tile), lambda n, which: (0, n)),
        ),
        cost_estimate=FREE,
        compiler_params=PARAMS,
        name="context_product",
    )(jnp.stack(places), *operands)


def place_rows(slots, grad_t):
    def body(slots_ref, grad_ref, out_ref):
        out_ref[...] = lax.dot_general(
            slots_ref[...], grad_ref[...], (((1,), (1,)), ((), ())), preferred_element_type=F32
        ).astype(BF16)

    return pl.pallas_call(
        body,
        out_shape=jax.ShapeDtypeStruct((slots.shape[0], grad_t.shape[0]), BF16),
        cost_estimate=FREE,
        compiler_params=PARAMS,
        name="place_rows",
    )(slots, grad_t)


def top_up(near, near_part, back, back_part):
    height, rows = near_part.shape

    def body(*refs):
        for i in (0, 1):
            value = refs[2 * i][...].astype(F32) + refs[2 * i + 1][...].astype(F32)
            refs[4 + i][...] = value.astype(BF16)

    top = pl.BlockSpec((height, rows), lambda i: (0, 0))
    bottom = pl.BlockSpec((height, rows), lambda i: (1, 0))
    return pl.pallas_call(
        body,
        out_shape=[jax.ShapeDtypeStruct(near.shape, BF16)] * 2,
        grid=(1,),
        in_specs=[top, top, bottom, top],
        out_specs=[top, bottom],
        input_output_aliases={0: 0, 2: 1},
        cost_estimate=FREE,
        compiler_params=PARAMS,
        name="top_up",
    )(near, near_part, back, back_part)


def forward_product(out_proj, context, place, split, dtype=F32):
    rows, width = context.shape
    tile = width // 2

    def body(which, proj_ref, context_ref, *out_refs):
        value = lax.dot_general(
            proj_ref[...], context_ref[...], (((1,), (1,)), ((), ())), preferred_element_type=F32
        )
        if split:
            for half in (0, 1):

                @pl.when(pl.program_id(0) == half)
                def _(half=half):
                    out_refs[half][...] = value.astype(BF16)
        else:
            out_refs[0][...] = value.astype(dtype)

    half_spec = pl.BlockSpec((tile, rows), lambda i, which: (0, 0))
    out = pl.pallas_call(
        body,
        out_shape=[jax.ShapeDtypeStruct((tile, rows), BF16)] * 2
        if split
        else [jax.ShapeDtypeStruct((width, rows), dtype)],
        grid_spec=pltpu.PrefetchScalarGridSpec(
            num_scalar_prefetch=1,
            grid=(2,),
            in_specs=[
                pl.BlockSpec((tile, width), lambda i, which: (which[0] * 2 + i, 0)),
                pl.BlockSpec((rows, width), lambda i, which: (0, 0)),
            ],
            out_specs=[half_spec] * 2
            if split
            else [pl.BlockSpec((tile, rows), lambda i, which: (i, 0))],
        ),
        cost_estimate=FREE,
        compiler_params=PARAMS,
        name="forward_product",
    )(place.reshape(1), out_proj, context)
    return out if split else out[0]


def hidden_part(out_proj, context, residual, cotangent, norm_gain, place):
    rows, width = context.shape
    tile = width // 2

    def body(which, proj_ref, context_ref, residual_ref, cotangent_ref, gain_ref, hidden_ref, gained_ref):
        value = lax.dot_general(
            proj_ref[...], context_ref[...], (((1,), (1,)), ((), ())), preferred_element_type=F32
        )
        hidden_ref[...] = value + residual_ref[...].astype(F32).T
        gained_ref[...] = (gain_ref[...] * cotangent_ref[...].astype(F32)).T

    columns = pl.BlockSpec((rows, tile), lambda i, which: (0, i))
    return pl.pallas_call(
        body,
        out_shape=[jax.ShapeDtypeStruct((width, rows), F32)] * 2,
        grid_spec=pltpu.PrefetchScalarGridSpec(
            num_scalar_prefetch=1,
            grid=(2,),
            in_specs=[
                pl.BlockSpec((tile, width), lambda i, which: (which[0] * 2 + i, 0)),
                pl.BlockSpec((rows, width), lambda i, which: (0, 0)),
                columns,
                columns,
                pl.BlockSpec((1, tile), lambda i, which: (0, i)),
            ],
            out_specs=[pl.BlockSpec((tile, rows), lambda i, which: (i, 0))] * 2,
        ),
        cost_estimate=FREE,
        compiler_params=PARAMS,
        name="hidden_part",
    )(place.reshape(1), out_proj, context, residual, cotangent, norm_gain.reshape(1, width))


def lay_out(steps, chunks, siblings, x, y, c, z):
    block, rows = chunks[0][0].shape[-2:]
    arrays, places = [], []
    for value in [piece for pieces in chunks for piece in pieces] + [pieces[0][0] for pieces in siblings]:
        known = [i for i, other in enumerate(arrays) if other is value]
        places.append(known[0] if known else len(arrays))
        if not known:
            arrays.append(value)
    count_of = len(arrays)

    def body(where, *refs):
        ins, outs, sems = refs[:count_of], refs[count_of : count_of + len(steps)], refs[-1]
        wx, wy, wc, wz = (where[i] for i in range(4))

        def send(src, number, first, slots):
            pltpu.make_async_copy(
                src, outs[number].at[pl.ds(first, slots)], sems.at[number]
            ).start()

        position = 0
        for owner, group in enumerate((chunks, siblings)):
            for j, members in enumerate(group):
                per_piece = 4 // len(members)
                pieces = []
                for member in members:
                    ref = ins[places[position]]
                    position += 1
                    pieces.append(ref.at[:, wc] if owner == 0 else ref.at[pl.ds(member[1], 4)])
                for number, k in enumerate(steps):
                    wanted = lax.rem(wy + k, 4)

                    @pl.when((wc == 0) & (lax.rem(j + wz - wx + 4, 4) == k))
                    def _(pieces=pieces, per_piece=per_piece, number=number, owner=owner):
                        for i, piece in enumerate(pieces):
                            send(piece, number, owner * 4 + i * per_piece, per_piece)

                    for i, piece in enumerate(pieces):

                        @pl.when((wc == 1) & (wanted // per_piece == i))
                        def _(piece=piece, i=i, per_piece=per_piece, number=number, owner=owner,
                              j=j, wanted=wanted):
                            slot = wanted - i * per_piece
                            send(piece.at[pl.ds(slot, 1)], number, owner * 4 + j, 1)

        for number in range(len(steps)):
            pltpu.make_async_copy(outs[number], outs[number], sems.at[number]).wait()

    out = pl.pallas_call(
        body,
        out_shape=[jax.ShapeDtypeStruct((8, block, rows), BF16)] * len(steps),
        grid_spec=pltpu.PrefetchScalarGridSpec(
            num_scalar_prefetch=1,
            grid=(1,),
            in_specs=[pl.BlockSpec(memory_space=pl.ANY)] * count_of,
            out_specs=[pl.BlockSpec((8, block, rows), lambda i, where: (0, 0, 0))] * len(steps),
            scratch_shapes=[pltpu.SemaphoreType.DMA((len(steps),))],
        ),
        cost_estimate=FREE,
        compiler_params=pltpu.CompilerParams(vmem_limit_bytes=16 * 1024 * 1024),
        name="lay_out",
    )(jnp.stack([x, y, c, z]).astype(jnp.int32), *arrays)
    return [value.reshape(8 * block, rows) for value in out]


def weight_product(pieces, contexts, order, block):
    count, tile = len(pieces), 640
    height, rows = pieces[0].shape[0] // 2, pieces[0].shape[1]
    width = contexts[0].shape[1]

    def body(order_ref, *refs):
        outs, total = refs[2 * count : 2 * count + 4], refs[-1]
        total[...] = sum(
            jnp.dot(
                refs[i][core * height : (core + 1) * height, :],
                refs[count + i][core * rows : (core + 1) * rows, :],
                preferred_element_type=F32,
            )
            for i in range(count)
            for core in (0, 1)
        )
        for k in range(4):
            first = pl.multiple_of(order_ref[k] * block, block)
            outs[k][...] = total[pl.ds(first, block), :].astype(outs[k].dtype)

    return pl.pallas_call(
        body,
        out_shape=[jax.ShapeDtypeStruct((block, width), BF16 if k else F32) for k in range(4)],
        grid_spec=pltpu.PrefetchScalarGridSpec(
            num_scalar_prefetch=1,
            grid=(width // tile,),
            in_specs=[pl.BlockSpec((2 * height, rows), lambda n, order: (0, 0)) for _ in pieces]
            + [pl.BlockSpec((2 * rows, tile), lambda n, order: (0, n)) for _ in contexts],
            out_specs=[pl.BlockSpec((block, tile), lambda n, order: (0, n))] * 4,
            scratch_shapes=[pltpu.VMEM((height, tile), F32)],
        ),
        cost_estimate=FREE,
        compiler_params=pltpu.CompilerParams(vmem_limit_bytes=56 * 1024 * 1024),
        name="weight_product",
    )(order, *pieces, *contexts)


def per_device(
    context, residual, cotangent, out_proj, norm_gain, rewards, group_ids, lengths, destinations
):
    lanes = NX * NY * NC
    rows, width = residual.shape
    full = width * NZ
    x, y, c, z = (lax.axis_index(axis) for axis in ("x", "y", "c", "z"))

    top = width // 2
    far_top, far_bottom = forward_product(out_proj, context, (z + 2) % NZ, True)
    ready, _ = lax.optimization_barrier((context, far_top))
    pair = jnp.concatenate([context, shift(ready, "c", 1)], axis=0)
    sent_top, sent_bottom = shift(far_top, "z", 1), shift(far_bottom, "z", 3)
    near = forward_product(out_proj, context, (z + 1) % NZ, False, BF16)
    back = forward_product(out_proj, context, (z + 3) % NZ, False, BF16)
    sent_top, sent_bottom, near, back, pair = lax.optimization_barrier(
        (sent_top, sent_bottom, near, back, pair)
    )
    near, back = top_up(near, sent_top, back, sent_bottom)

    ready, _, _ = lax.optimization_barrier((context, near, back))
    own, gained_t = hidden_part(out_proj, ready, residual, cotangent, norm_gain, z)
    late_pair, _ = lax.optimization_barrier((pair, near))
    contexts = [pair] + [cross(late_pair, k, True) for k in (1, 2, 3)]
    hidden_t = own + shift(near, "z", 1).astype(F32) + shift(back, "z", 3).astype(F32)

    stats = jnp.stack(
        [jnp.sum(hidden_t * hidden_t, axis=0), jnp.sum(gained_t * hidden_t, axis=0)]
    )
    groups = rewards.shape[0] * lanes // GROUP
    member = (group_ids[:, None] == jnp.arange(groups)[None, :]).astype(F32)
    share, _ = lax.optimization_barrier((jnp.sum(member * rewards[:, None], axis=0), own))
    shares, _ = lax.optimization_barrier((all_shares(share), stats))
    group_total = jnp.sum(shares, axis=0)
    advantage = rewards - jnp.sum(member * group_total[None, :], axis=1) / GROUP
    scale = advantage * LMAX / (2.0 * lengths.astype(F32))
    live = jnp.arange(LMAX)[None, :] < lengths[:, None]
    row_weights = jnp.where(live, scale[:, None], F32(0.0)).reshape(-1).astype(BF16).astype(F32)

    stats = stats + shift(stats, "z", 1) + shift(stats, "z", 2) + shift(stats, "z", 3)
    inv_rms = lax.rsqrt(stats[0] / full + EPSILON)
    up_scale = inv_rms * row_weights
    hidden_scale = inv_rms**3 * (row_weights * stats[1]) / full
    grad_t = (up_scale[None, :] * gained_t - hidden_t * hidden_scale[None, :]).astype(BF16)
    grad_t, contexts[1], contexts[3] = lax.optimization_barrier((grad_t, contexts[1], contexts[3]))

    block = width // (NY * NC)

    def swap(*values):
        parted = [value.reshape(-1, NC, block, rows) for value in values]
        asked = [lax.dynamic_index_in_dim(value, 1 - c, 1, keepdims=False) for value in parted]
        return shift(jnp.concatenate(asked, axis=0).reshape(-1, rows), "c", 1)

    slots = slot_matrix(destinations[:, 0], lanes * PAIR, rows, 16)
    from_left, from_right = shift(grad_t, "z", 1), shift(grad_t, "z", 3)
    swapped = swap(grad_t)
    grad_rows, _ = lax.optimization_barrier((grad_t, swapped))
    d_residual = exchange(place_rows(slots, grad_rows), lanes)
    context_grad = context_product([grad_t], [z], out_proj)
    from_left, from_right, context_grad, swapped, contexts[2] = lax.optimization_barrier(
        (from_left, from_right, context_grad, swapped, contexts[2])
    )
    far_left, far_right = shift(from_left[:top], "z", 1), shift(from_right[top:], "z", 3)
    context_grad = context_product(
        [from_right, from_left], [(z + 1) % NZ, (z + 3) % NZ], out_proj, before=context_grad
    )
    far_left, far_right, context_grad = lax.optimization_barrier(
        (far_left, far_right, context_grad)
    )
    swapped_near = swap(from_right, from_left).reshape(8, block, rows)
    swapped_far = swap(far_left, far_right).reshape(4, block, rows)
    swapped_own = swapped.reshape(4, block, rows)

    def parted(*values):
        return [value.reshape(-1, NC, block, rows) for value in values]

    chunks = [parted(grad_t), parted(from_right), parted(far_left, far_right), parted(from_left)]
    siblings = [
        [(swapped_own, 0)], [(swapped_near[:4], 0)], [(swapped_far, 0)], [(swapped_near[4:], 0)]
    ]
    sends = lay_out((0, 1, 2, 3), chunks, siblings, x, y, c, z)
    far_left, far_right, sends = lax.optimization_barrier((far_left, far_right, sends))
    pieces = [sends[0]] + [cross(sends[k], k, True) for k in (1, 2, 3)]
    far_place = (z + 2) % NZ * 2
    placed = context_product(
        [far_left, far_right], [far_place, far_place + 1], out_proj, before=context_grad, slots=slots
    )
    placed, d_residual = lax.optimization_barrier((placed, d_residual))
    d_context = exchange(placed, lanes)
    order = [jnp.where(c == 0, (y + k) % NY, (x + k - z) % NZ) for k in range(4)]
    d_out_proj, *parts = weight_product(pieces, contexts, jnp.stack(order), block)
    parts = [cross(part, k, False) for k, part in zip((1, 2, 3), parts)]
    for part in parts:
        d_out_proj = d_out_proj + part.astype(F32)
    return (learner_rows(d_context), learner_rows(d_residual), d_out_proj / lanes)


def solution(mesh):
    wide = Mesh(mesh.devices.reshape(NX, NY, NC, NZ), DP + ("z",))
    placed = (
        P(DP, "z"),
        P(DP, "z"),
        P(DP, "z"),
        P(None, "z"),
        P("z"),
        P(DP),
        P(DP),
        P(DP),
        P(DP, None),
    )
    return jax.shard_map(
        per_device,
        mesh=wide,
        in_specs=placed,
        out_specs=(P(DP, "z"), P(DP, "z"), P(DP, "z")),
        check_vma=False,
    )
```

```python
import jax
import jax.numpy as jnp
from jax import lax
from jax.experimental import pallas as pl
from jax.experimental.pallas import tpu as pltpu
from jax.sharding import Mesh
from jax.sharding import PartitionSpec as P

LMAX = 64
GROUP = 16
PAIR = 3
BLOCK_ROWS = 4
EPSILON = 1e-06
NX, NY, NC, NZ = 4, 4, 2, 4
DP = ("x", "y", "c")
F32 = jnp.float32
BF16 = jnp.bfloat16


def shift(value, axis, step):
    size = lax.axis_size(axis)
    return lax.ppermute(value, axis, [(i, (i + step) % size) for i in range(size)])


def pick(values, index):
    return lax.dynamic_index_in_dim(values, index, 0, keepdims=False)


def cross(value, step, first):
    pairs = []
    for x in range(NX):
        for y in range(NY):
            for c in range(NC):
                along_x = (c == 0) == first
                to = ((x + step) % NX, y, c) if along_x else (x, (y + step) % NY, c)
                pairs.append(((x * NY + y) * NC + c, (to[0] * NY + to[1]) * NC + to[2]))
    return lax.ppermute(value, DP, pairs)


def all_shares(value):
    copies = jnp.broadcast_to(value, (NX * NY * NC,) + value.shape)
    return lax.all_to_all(copies, DP, split_axis=0, concat_axis=0, tiled=True)


def slot_matrix(owner_dest, slots, rows, padded):
    count = owner_dest.shape[0]
    per_block = rows // count
    same = owner_dest[:, None] == owner_dest[None, :]
    earlier = jnp.arange(count)[None, :] < jnp.arange(count)[:, None]
    rank = jnp.sum((same & earlier).astype(jnp.int32), axis=1)
    target = owner_dest * padded + rank * per_block
    row_target = jnp.repeat(target, per_block) + jnp.tile(jnp.arange(per_block), count)
    return (jnp.arange(slots // PAIR * padded)[:, None] == row_target[None, :]).astype(BF16)


def exchange(packed, lanes):
    blocks = packed.reshape((lanes, packed.shape[0] // lanes, packed.shape[1]))
    return lax.all_to_all(blocks, DP, split_axis=0, concat_axis=0, tiled=True)


def learner_rows(got):
    kept = PAIR * BLOCK_ROWS
    return got[:, :kept].reshape(got.shape[0] * kept, got.shape[2])


FREE = pl.CostEstimate(flops=0, bytes_accessed=0, transcendentals=0)
PARAMS = pltpu.CompilerParams(vmem_limit_bytes=48 * 1024 * 1024)


def context_product(chunks, places, out_proj, before=None, slots=None):
    width, rows = out_proj.shape[1], chunks[0].shape[1]
    count, tile = len(chunks), 640
    dtype = F32 if slots is None else BF16

    def body(which, *refs):
        refs = list(refs)
        out_ref = refs.pop()
        total = sum(
            lax.dot_general(
                refs[i][...], refs[count + i][...], (((0,), (0,)), ((), ())), preferred_element_type=F32
            )
            for i in range(count)
        )
        if before is not None:
            total = total + refs[2 * count][...]
        if slots is not None:
            total = jnp.dot(refs[-1][...], total.astype(BF16), preferred_element_type=F32)
        out_ref[...] = total.astype(dtype)

    in_specs = [pl.BlockSpec(chunk.shape, lambda n, which: (0, 0)) for chunk in chunks]
    in_specs += [
        pl.BlockSpec((chunk.shape[0], tile), lambda n, which, i=i: (which[i], n))
        for i, chunk in enumerate(chunks)
    ]
    operands = list(chunks) + [out_proj] * count
    out_rows = rows
    if before is not None:
        in_specs.append(pl.BlockSpec((rows, tile), lambda n, which: (0, n)))
        operands.append(before)
    if slots is not None:
        in_specs.append(pl.BlockSpec(slots.shape, lambda n, which: (0, 0)))
        operands.append(slots)
        out_rows = slots.shape[0]
    return pl.pallas_call(
        body,
        out_shape=jax.ShapeDtypeStruct((out_rows, width), dtype),
        grid_spec=pltpu.PrefetchScalarGridSpec(
            num_scalar_prefetch=1,
            grid=(width // tile,),
            in_specs=in_specs,
            out_specs=pl.BlockSpec((out_rows, tile), lambda n, which: (0, n)),
        ),
        cost_estimate=FREE,
        compiler_params=PARAMS,
        name="context_product",
    )(jnp.stack(places), *operands)


def place_rows(slots, grad_t):
    def body(slots_ref, grad_ref, out_ref):
        out_ref[...] = lax.dot_general(
            slots_ref[...], grad_ref[...], (((1,), (1,)), ((), ())), preferred_element_type=F32
        ).astype(BF16)

    return pl.pallas_call(
        body,
        out_shape=jax.ShapeDtypeStruct((slots.shape[0], grad_t.shape[0]), BF16),
        cost_estimate=FREE,
        compiler_params=PARAMS,
        name="place_rows",
    )(slots, grad_t)


def top_up(near, near_part, back, back_part):
    height, rows = near_part.shape

    def body(*refs):
        for i in (0, 1):
            value = refs[2 * i][...].astype(F32) + refs[2 * i + 1][...].astype(F32)
            refs[4 + i][...] = value.astype(BF16)

    top = pl.BlockSpec((height, rows), lambda i: (0, 0))
    bottom = pl.BlockSpec((height, rows), lambda i: (1, 0))
    return pl.pallas_call(
        body,
        out_shape=[jax.ShapeDtypeStruct(near.shape, BF16)] * 2,
        grid=(1,),
        in_specs=[top, top, bottom, top],
        out_specs=[top, bottom],
        input_output_aliases={0: 0, 2: 1},
        cost_estimate=FREE,
        compiler_params=PARAMS,
        name="top_up",
    )(near, near_part, back, back_part)


def forward_product(out_proj, context, place, split, dtype=F32):
    rows, width = context.shape
    tile = width // 2

    def body(which, proj_ref, context_ref, *out_refs):
        value = lax.dot_general(
            proj_ref[...], context_ref[...], (((1,), (1,)), ((), ())), preferred_element_type=F32
        )
        if split:
            for half in (0, 1):

                @pl.when(pl.program_id(0) == half)
                def _(half=half):
                    out_refs[half][...] = value.astype(BF16)
        else:
            out_refs[0][...] = value.astype(dtype)

    half_spec = pl.BlockSpec((tile, rows), lambda i, which: (0, 0))
    out = pl.pallas_call(
        body,
        out_shape=[jax.ShapeDtypeStruct((tile, rows), BF16)] * 2
        if split
        else [jax.ShapeDtypeStruct((width, rows), dtype)],
        grid_spec=pltpu.PrefetchScalarGridSpec(
            num_scalar_prefetch=1,
            grid=(2,),
            in_specs=[
                pl.BlockSpec((tile, width), lambda i, which: (which[0] * 2 + i, 0)),
                pl.BlockSpec((rows, width), lambda i, which: (0, 0)),
            ],
            out_specs=[half_spec] * 2
            if split
            else [pl.BlockSpec((tile, rows), lambda i, which: (i, 0))],
        ),
        cost_estimate=FREE,
        compiler_params=PARAMS,
        name="forward_product",
    )(place.reshape(1), out_proj, context)
    return out if split else out[0]


def hidden_part(out_proj, context, residual, cotangent, norm_gain, place):
    rows, width = context.shape
    tile = width // 2

    def body(which, proj_ref, context_ref, residual_ref, cotangent_ref, gain_ref, hidden_ref, gained_ref):
        value = lax.dot_general(
            proj_ref[...], context_ref[...], (((1,), (1,)), ((), ())), preferred_element_type=F32
        )
        hidden_ref[...] = value + residual_ref[...].astype(F32).T
        gained_ref[...] = (gain_ref[...] * cotangent_ref[...].astype(F32)).T

    columns = pl.BlockSpec((rows, tile), lambda i, which: (0, i))
    return pl.pallas_call(
        body,
        out_shape=[jax.ShapeDtypeStruct((width, rows), F32)] * 2,
        grid_spec=pltpu.PrefetchScalarGridSpec(
            num_scalar_prefetch=1,
            grid=(2,),
            in_specs=[
                pl.BlockSpec((tile, width), lambda i, which: (which[0] * 2 + i, 0)),
                pl.BlockSpec((rows, width), lambda i, which: (0, 0)),
                columns,
                columns,
                pl.BlockSpec((1, tile), lambda i, which: (0, i)),
            ],
            out_specs=[pl.BlockSpec((tile, rows), lambda i, which: (i, 0))] * 2,
        ),
        cost_estimate=FREE,
        compiler_params=PARAMS,
        name="hidden_part",
    )(place.reshape(1), out_proj, context, residual, cotangent, norm_gain.reshape(1, width))


def lay_out(steps, chunks, siblings, x, y, c, z):
    block, rows = chunks[0][0].shape[-2:]
    arrays, places = [], []
    for value in [piece for pieces in chunks for piece in pieces] + [pieces[0][0] for pieces in siblings]:
        known = [i for i, other in enumerate(arrays) if other is value]
        places.append(known[0] if known else len(arrays))
        if not known:
            arrays.append(value)
    count_of = len(arrays)

    def body(where, *refs):
        ins, outs, sems = refs[:count_of], refs[count_of : count_of + len(steps)], refs[-1]
        wx, wy, wc, wz = (where[i] for i in range(4))

        def send(src, number, first, slots):
            pltpu.make_async_copy(
                src, outs[number].at[pl.ds(first, slots)], sems.at[number]
            ).start()

        position = 0
        for owner, group in enumerate((chunks, siblings)):
            for j, members in enumerate(group):
                per_piece = 4 // len(members)
                pieces = []
                for member in members:
                    ref = ins[places[position]]
                    position += 1
                    pieces.append(ref.at[:, wc] if owner == 0 else ref.at[pl.ds(member[1], 4)])
                for number, k in enumerate(steps):
                    wanted = lax.rem(wy + k, 4)

                    @pl.when((wc == 0) & (lax.rem(j + wz - wx + 4, 4) == k))
                    def _(pieces=pieces, per_piece=per_piece, number=number, owner=owner):
                        for i, piece in enumerate(pieces):
                            send(piece, number, owner * 4 + i * per_piece, per_piece)

                    for i, piece in enumerate(pieces):

                        @pl.when((wc == 1) & (wanted // per_piece == i))
                        def _(piece=piece, i=i, per_piece=per_piece, number=number, owner=owner,
                              j=j, wanted=wanted):
                            slot = wanted - i * per_piece
                            send(piece.at[pl.ds(slot, 1)], number, owner * 4 + j, 1)

        for number in range(len(steps)):
            pltpu.make_async_copy(outs[number], outs[number], sems.at[number]).wait()

    out = pl.pallas_call(
        body,
        out_shape=[jax.ShapeDtypeStruct((8, block, rows), BF16)] * len(steps),
        grid_spec=pltpu.PrefetchScalarGridSpec(
            num_scalar_prefetch=1,
            grid=(1,),
            in_specs=[pl.BlockSpec(memory_space=pl.ANY)] * count_of,
            out_specs=[pl.BlockSpec((8, block, rows), lambda i, where: (0, 0, 0))] * len(steps),
            scratch_shapes=[pltpu.SemaphoreType.DMA((len(steps),))],
        ),
        cost_estimate=FREE,
        compiler_params=pltpu.CompilerParams(vmem_limit_bytes=16 * 1024 * 1024),
        name="lay_out",
    )(jnp.stack([x, y, c, z]).astype(jnp.int32), *arrays)
    return [value.reshape(8 * block, rows) for value in out]


def weight_product(pieces, contexts, order, block):
    count, tile = len(pieces), 640
    height, rows = pieces[0].shape[0] // 2, pieces[0].shape[1]
    width = contexts[0].shape[1]

    def body(order_ref, *refs):
        outs, total = refs[2 * count : 2 * count + 4], refs[-1]
        total[...] = sum(
            jnp.dot(
                refs[i][core * height : (core + 1) * height, :],
                refs[count + i][core * rows : (core + 1) * rows, :],
                preferred_element_type=F32,
            )
            for i in range(count)
            for core in (0, 1)
        )
        for k in range(4):
            first = pl.multiple_of(order_ref[k] * block, block)
            outs[k][...] = total[pl.ds(first, block), :].astype(outs[k].dtype)

    return pl.pallas_call(
        body,
        out_shape=[jax.ShapeDtypeStruct((block, width), BF16 if k else F32) for k in range(4)],
        grid_spec=pltpu.PrefetchScalarGridSpec(
            num_scalar_prefetch=1,
            grid=(width // tile,),
            in_specs=[pl.BlockSpec((2 * height, rows), lambda n, order: (0, 0)) for _ in pieces]
            + [pl.BlockSpec((2 * rows, tile), lambda n, order: (0, n)) for _ in contexts],
            out_specs=[pl.BlockSpec((block, tile), lambda n, order: (0, n))] * 4,
            scratch_shapes=[pltpu.VMEM((height, tile), F32)],
        ),
        cost_estimate=FREE,
        compiler_params=pltpu.CompilerParams(vmem_limit_bytes=56 * 1024 * 1024),
        name="weight_product",
    )(order, *pieces, *contexts)


def per_device(
    context, residual, cotangent, out_proj, norm_gain, rewards, group_ids, lengths, destinations
):
    lanes = NX * NY * NC
    rows, width = residual.shape
    full = width * NZ
    x, y, c, z = (lax.axis_index(axis) for axis in ("x", "y", "c", "z"))

    top = width // 2
    far_top, far_bottom = forward_product(out_proj, context, (z + 2) % NZ, True)
    ready, _ = lax.optimization_barrier((context, far_top))
    pair = jnp.concatenate([context, shift(ready, "c", 1)], axis=0)
    sent_top, sent_bottom = shift(far_top, "z", 1), shift(far_bottom, "z", 3)
    near = forward_product(out_proj, context, (z + 1) % NZ, False, BF16)
    back = forward_product(out_proj, context, (z + 3) % NZ, False, BF16)
    sent_top, sent_bottom, near, back, pair = lax.optimization_barrier(
        (sent_top, sent_bottom, near, back, pair)
    )
    near, back = top_up(near, sent_top, back, sent_bottom)

    ready, _, _ = lax.optimization_barrier((context, near, back))
    own, gained_t = hidden_part(out_proj, ready, residual, cotangent, norm_gain, z)
    late_pair, _ = lax.optimization_barrier((pair, near))
    contexts = [pair] + [cross(late_pair, k, True) for k in (1, 2, 3)]
    hidden_t = own + shift(near, "z", 1).astype(F32) + shift(back, "z", 3).astype(F32)

    stats = jnp.stack(
        [jnp.sum(hidden_t * hidden_t, axis=0), jnp.sum(gained_t * hidden_t, axis=0)]
    )
    groups = rewards.shape[0] * lanes // GROUP
    member = (group_ids[:, None] == jnp.arange(groups)[None, :]).astype(F32)
    share, _ = lax.optimization_barrier((jnp.sum(member * rewards[:, None], axis=0), own))
    shares, _ = lax.optimization_barrier((all_shares(share), stats))
    group_total = jnp.sum(shares, axis=0)
    advantage = rewards - jnp.sum(member * group_total[None, :], axis=1) / GROUP
    scale = advantage * LMAX / (2.0 * lengths.astype(F32))
    live = jnp.arange(LMAX)[None, :] < lengths[:, None]
    row_weights = jnp.where(live, scale[:, None], F32(0.0)).reshape(-1).astype(BF16).astype(F32)

    stats = stats + shift(stats, "z", 1) + shift(stats, "z", 2) + shift(stats, "z", 3)
    inv_rms = lax.rsqrt(stats[0] / full + EPSILON)
    up_scale = inv_rms * row_weights
    hidden_scale = inv_rms**3 * (row_weights * stats[1]) / full
    grad_t = (up_scale[None, :] * gained_t - hidden_t * hidden_scale[None, :]).astype(BF16)
    grad_t, contexts[1], contexts[3] = lax.optimization_barrier((grad_t, contexts[1], contexts[3]))

    block = width // (NY * NC)

    def swap(*values):
        parted = [value.reshape(-1, NC, block, rows) for value in values]
        asked = [lax.dynamic_index_in_dim(value, 1 - c, 1, keepdims=False) for value in parted]
        return shift(jnp.concatenate(asked, axis=0).reshape(-1, rows), "c", 1)

    slots = slot_matrix(destinations[:, 0], lanes * PAIR, rows, 16)
    from_left, from_right = shift(grad_t, "z", 1), shift(grad_t, "z", 3)
    swapped = swap(grad_t)
    grad_rows, _ = lax.optimization_barrier((grad_t, swapped))
    d_residual = exchange(place_rows(slots, grad_rows), lanes)
    context_grad = context_product([grad_t], [z], out_proj)
    from_left, from_right, context_grad, swapped, contexts[2] = lax.optimization_barrier(
        (from_left, from_right, context_grad, swapped, contexts[2])
    )
    far_left, far_right = shift(from_left[:top], "z", 1), shift(from_right[top:], "z", 3)
    context_grad = context_product(
        [from_right, from_left], [(z + 1) % NZ, (z + 3) % NZ], out_proj, before=context_grad
    )
    far_left, far_right, context_grad = lax.optimization_barrier(
        (far_left, far_right, context_grad)
    )
    swapped_near = swap(from_right, from_left).reshape(8, block, rows)
    swapped_far = swap(far_left, far_right).reshape(4, block, rows)
    swapped_own = swapped.reshape(4, block, rows)

    def parted(*values):
        return [value.reshape(-1, NC, block, rows) for value in values]

    chunks = [parted(grad_t), parted(from_right), parted(far_left, far_right), parted(from_left)]
    siblings = [
        [(swapped_own, 0)], [(swapped_near[:4], 0)], [(swapped_far, 0)], [(swapped_near[4:], 0)]
    ]
    sends = lay_out((0, 1, 2, 3), chunks, siblings, x, y, c, z)
    far_left, far_right, sends = lax.optimization_barrier((far_left, far_right, sends))
    pieces = [sends[0]] + [cross(sends[k], k, True) for k in (1, 2, 3)]
    far_place = (z + 2) % NZ * 2
    placed = context_product(
        [far_left, far_right], [far_place, far_place + 1], out_proj, before=context_grad, slots=slots
    )
    placed, d_residual, pieces[3] = lax.optimization_barrier((placed, d_residual, pieces[3]))
    d_context = exchange(placed, lanes)
    order = [jnp.where(c == 0, (y + k) % NY, (x + k - z) % NZ) for k in range(4)]
    d_out_proj, *parts = weight_product(pieces, contexts, jnp.stack(order), block)
    parts = [cross(part, k, False) for k, part in zip((1, 2, 3), parts)]
    for part in parts:
        d_out_proj = d_out_proj + part.astype(F32)
    return (learner_rows(d_context), learner_rows(d_residual), d_out_proj / lanes)


def solution(mesh):
    wide = Mesh(mesh.devices.reshape(NX, NY, NC, NZ), DP + ("z",))
    placed = (
        P(DP, "z"),
        P(DP, "z"),
        P(DP, "z"),
        P(None, "z"),
        P("z"),
        P(DP),
        P(DP),
        P(DP),
        P(DP, None),
    )
    return jax.shard_map(
        per_device,
        mesh=wide,
        in_specs=placed,
        out_specs=(P(DP, "z"), P(DP, "z"), P(DP, "z")),
        check_vma=False,
    )
```

```python
import jax
import jax.numpy as jnp
from jax import lax
from jax.experimental import pallas as pl
from jax.experimental.pallas import tpu as pltpu
from jax.sharding import Mesh
from jax.sharding import PartitionSpec as P

LMAX = 64
GROUP = 16
PAIR = 3
BLOCK_ROWS = 4
EPSILON = 1e-06
NX, NY, NC, NZ = 4, 4, 2, 4
DP = ("x", "y", "c")
F32 = jnp.float32
BF16 = jnp.bfloat16


def shift(value, axis, step):
    size = lax.axis_size(axis)
    return lax.ppermute(value, axis, [(i, (i + step) % size) for i in range(size)])


def pick(values, index):
    return lax.dynamic_index_in_dim(values, index, 0, keepdims=False)


def cross(value, step, first):
    pairs = []
    for x in range(NX):
        for y in range(NY):
            for c in range(NC):
                along_x = (c == 0) == first
                to = ((x + step) % NX, y, c) if along_x else (x, (y + step) % NY, c)
                pairs.append(((x * NY + y) * NC + c, (to[0] * NY + to[1]) * NC + to[2]))
    return lax.ppermute(value, DP, pairs)


def all_shares(value):
    copies = jnp.broadcast_to(value, (NX * NY * NC,) + value.shape)
    return lax.all_to_all(copies, DP, split_axis=0, concat_axis=0, tiled=True)


def slot_matrix(owner_dest, slots, rows, padded):
    count = owner_dest.shape[0]
    per_block = rows // count
    same = owner_dest[:, None] == owner_dest[None, :]
    earlier = jnp.arange(count)[None, :] < jnp.arange(count)[:, None]
    rank = jnp.sum((same & earlier).astype(jnp.int32), axis=1)
    target = owner_dest * padded + rank * per_block
    row_target = jnp.repeat(target, per_block) + jnp.tile(jnp.arange(per_block), count)
    return (jnp.arange(slots // PAIR * padded)[:, None] == row_target[None, :]).astype(BF16)


def exchange(packed, lanes):
    blocks = packed.reshape((lanes, packed.shape[0] // lanes, packed.shape[1]))
    return lax.all_to_all(blocks, DP, split_axis=0, concat_axis=0, tiled=True)


def learner_rows(got):
    kept = PAIR * BLOCK_ROWS
    return got[:, :kept].reshape(got.shape[0] * kept, got.shape[2])


FREE = pl.CostEstimate(flops=0, bytes_accessed=0, transcendentals=0)
PARAMS = pltpu.CompilerParams(vmem_limit_bytes=48 * 1024 * 1024)


def context_product(chunks, places, out_proj, before=None, slots=None):
    width, rows = out_proj.shape[1], chunks[0].shape[1]
    count, tile = len(chunks), 640
    dtype = F32 if slots is None else BF16

    def body(which, *refs):
        refs = list(refs)
        out_ref = refs.pop()
        total = sum(
            lax.dot_general(
                refs[i][...], refs[count + i][...], (((0,), (0,)), ((), ())), preferred_element_type=F32
            )
            for i in range(count)
        )
        if before is not None:
            total = total + refs[2 * count][...]
        if slots is not None:
            total = jnp.dot(refs[-1][...], total.astype(BF16), preferred_element_type=F32)
        out_ref[...] = total.astype(dtype)

    in_specs = [pl.BlockSpec(chunk.shape, lambda n, which: (0, 0)) for chunk in chunks]
    in_specs += [
        pl.BlockSpec((chunk.shape[0], tile), lambda n, which, i=i: (which[i], n))
        for i, chunk in enumerate(chunks)
    ]
    operands = list(chunks) + [out_proj] * count
    out_rows = rows
    if before is not None:
        in_specs.append(pl.BlockSpec((rows, tile), lambda n, which: (0, n)))
        operands.append(before)
    if slots is not None:
        in_specs.append(pl.BlockSpec(slots.shape, lambda n, which: (0, 0)))
        operands.append(slots)
        out_rows = slots.shape[0]
    return pl.pallas_call(
        body,
        out_shape=jax.ShapeDtypeStruct((out_rows, width), dtype),
        grid_spec=pltpu.PrefetchScalarGridSpec(
            num_scalar_prefetch=1,
            grid=(width // tile,),
            in_specs=in_specs,
            out_specs=pl.BlockSpec((out_rows, tile), lambda n, which: (0, n)),
        ),
        cost_estimate=FREE,
        compiler_params=PARAMS,
        name="context_product",
    )(jnp.stack(places), *operands)


def place_rows(slots, grad_t):
    def body(slots_ref, grad_ref, out_ref):
        out_ref[...] = lax.dot_general(
            slots_ref[...], grad_ref[...], (((1,), (1,)), ((), ())), preferred_element_type=F32
        ).astype(BF16)

    return pl.pallas_call(
        body,
        out_shape=jax.ShapeDtypeStruct((slots.shape[0], grad_t.shape[0]), BF16),
        cost_estimate=FREE,
        compiler_params=PARAMS,
        name="place_rows",
    )(slots, grad_t)


def top_up(near, near_part, back, back_part):
    height, rows = near_part.shape

    def body(*refs):
        for i in (0, 1):
            value = refs[2 * i][...].astype(F32) + refs[2 * i + 1][...].astype(F32)
            refs[4 + i][...] = value.astype(BF16)

    top = pl.BlockSpec((height, rows), lambda i: (0, 0))
    bottom = pl.BlockSpec((height, rows), lambda i: (1, 0))
    return pl.pallas_call(
        body,
        out_shape=[jax.ShapeDtypeStruct(near.shape, BF16)] * 2,
        grid=(1,),
        in_specs=[top, top, bottom, top],
        out_specs=[top, bottom],
        input_output_aliases={0: 0, 2: 1},
        cost_estimate=FREE,
        compiler_params=PARAMS,
        name="top_up",
    )(near, near_part, back, back_part)


def forward_product(out_proj, context, place, split, dtype=F32):
    rows, width = context.shape
    tile = width // 2

    def body(which, proj_ref, context_ref, *out_refs):
        value = lax.dot_general(
            proj_ref[...], context_ref[...], (((1,), (1,)), ((), ())), preferred_element_type=F32
        )
        if split:
            for half in (0, 1):

                @pl.when(pl.program_id(0) == half)
                def _(half=half):
                    out_refs[half][...] = value.astype(BF16)
        else:
            out_refs[0][...] = value.astype(dtype)

    half_spec = pl.BlockSpec((tile, rows), lambda i, which: (0, 0))
    out = pl.pallas_call(
        body,
        out_shape=[jax.ShapeDtypeStruct((tile, rows), BF16)] * 2
        if split
        else [jax.ShapeDtypeStruct((width, rows), dtype)],
        grid_spec=pltpu.PrefetchScalarGridSpec(
            num_scalar_prefetch=1,
            grid=(2,),
            in_specs=[
                pl.BlockSpec((tile, width), lambda i, which: (which[0] * 2 + i, 0)),
                pl.BlockSpec((rows, width), lambda i, which: (0, 0)),
            ],
            out_specs=[half_spec] * 2
            if split
            else [pl.BlockSpec((tile, rows), lambda i, which: (i, 0))],
        ),
        cost_estimate=FREE,
        compiler_params=PARAMS,
        name="forward_product",
    )(place.reshape(1), out_proj, context)
    return out if split else out[0]


def hidden_part(out_proj, context, residual, cotangent, norm_gain, place):
    rows, width = context.shape
    tile = width // 2

    def body(which, proj_ref, context_ref, residual_ref, cotangent_ref, gain_ref, hidden_ref, gained_ref):
        value = lax.dot_general(
            proj_ref[...], context_ref[...], (((1,), (1,)), ((), ())), preferred_element_type=F32
        )
        hidden_ref[...] = value + residual_ref[...].astype(F32).T
        gained_ref[...] = (gain_ref[...] * cotangent_ref[...].astype(F32)).T

    columns = pl.BlockSpec((rows, tile), lambda i, which: (0, i))
    return pl.pallas_call(
        body,
        out_shape=[jax.ShapeDtypeStruct((width, rows), F32)] * 2,
        grid_spec=pltpu.PrefetchScalarGridSpec(
            num_scalar_prefetch=1,
            grid=(2,),
            in_specs=[
                pl.BlockSpec((tile, width), lambda i, which: (which[0] * 2 + i, 0)),
                pl.BlockSpec((rows, width), lambda i, which: (0, 0)),
                columns,
                columns,
                pl.BlockSpec((1, tile), lambda i, which: (0, i)),
            ],
            out_specs=[pl.BlockSpec((tile, rows), lambda i, which: (i, 0))] * 2,
        ),
        cost_estimate=FREE,
        compiler_params=PARAMS,
        name="hidden_part",
    )(place.reshape(1), out_proj, context, residual, cotangent, norm_gain.reshape(1, width))


def lay_out(steps, chunks, siblings, x, y, c, z):
    block, rows = chunks[0][0].shape[-2:]
    arrays, places = [], []
    for value in [piece for pieces in chunks for piece in pieces] + [pieces[0][0] for pieces in siblings]:
        known = [i for i, other in enumerate(arrays) if other is value]
        places.append(known[0] if known else len(arrays))
        if not known:
            arrays.append(value)
    count_of = len(arrays)

    def body(where, *refs):
        ins, outs, sems = refs[:count_of], refs[count_of : count_of + len(steps)], refs[-1]
        wx, wy, wc, wz = (where[i] for i in range(4))

        def send(src, number, first, slots):
            pltpu.make_async_copy(
                src, outs[number].at[pl.ds(first, slots)], sems.at[number]
            ).start()

        position = 0
        for owner, group in enumerate((chunks, siblings)):
            for j, members in enumerate(group):
                per_piece = 4 // len(members)
                pieces = []
                for member in members:
                    ref = ins[places[position]]
                    position += 1
                    pieces.append(ref.at[:, wc] if owner == 0 else ref.at[pl.ds(member[1], 4)])
                for number, k in enumerate(steps):
                    wanted = lax.rem(wy + k, 4)

                    @pl.when((wc == 0) & (lax.rem(j + wz - wx + 4, 4) == k))
                    def _(pieces=pieces, per_piece=per_piece, number=number, owner=owner):
                        for i, piece in enumerate(pieces):
                            send(piece, number, owner * 4 + i * per_piece, per_piece)

                    for i, piece in enumerate(pieces):

                        @pl.when((wc == 1) & (wanted // per_piece == i))
                        def _(piece=piece, i=i, per_piece=per_piece, number=number, owner=owner,
                              j=j, wanted=wanted):
                            slot = wanted - i * per_piece
                            send(piece.at[pl.ds(slot, 1)], number, owner * 4 + j, 1)

        for number in range(len(steps)):
            pltpu.make_async_copy(outs[number], outs[number], sems.at[number]).wait()

    out = pl.pallas_call(
        body,
        out_shape=[jax.ShapeDtypeStruct((8, block, rows), BF16)] * len(steps),
        grid_spec=pltpu.PrefetchScalarGridSpec(
            num_scalar_prefetch=1,
            grid=(1,),
            in_specs=[pl.BlockSpec(memory_space=pl.ANY)] * count_of,
            out_specs=[pl.BlockSpec((8, block, rows), lambda i, where: (0, 0, 0))] * len(steps),
            scratch_shapes=[pltpu.SemaphoreType.DMA((len(steps),))],
        ),
        cost_estimate=FREE,
        compiler_params=pltpu.CompilerParams(vmem_limit_bytes=16 * 1024 * 1024),
        name="lay_out",
    )(jnp.stack([x, y, c, z]).astype(jnp.int32), *arrays)
    return [value.reshape(8 * block, rows) for value in out]


def weight_product(pieces, contexts, order, block):
    count, tile = len(pieces), 640
    height, rows = pieces[0].shape[0] // 2, pieces[0].shape[1]
    width = contexts[0].shape[1]

    def body(order_ref, *refs):
        outs, total = refs[2 * count : 2 * count + 4], refs[-1]
        total[...] = sum(
            jnp.dot(
                refs[i][core * height : (core + 1) * height, :],
                refs[count + i][core * rows : (core + 1) * rows, :],
                preferred_element_type=F32,
            )
            for i in range(count)
            for core in (0, 1)
        )
        for k in range(4):
            first = pl.multiple_of(order_ref[k] * block, block)
            outs[k][...] = total[pl.ds(first, block), :].astype(outs[k].dtype)

    return pl.pallas_call(
        body,
        out_shape=[jax.ShapeDtypeStruct((block, width), BF16 if k else F32) for k in range(4)],
        grid_spec=pltpu.PrefetchScalarGridSpec(
            num_scalar_prefetch=1,
            grid=(width // tile,),
            in_specs=[pl.BlockSpec((2 * height, rows), lambda n, order: (0, 0)) for _ in pieces]
            + [pl.BlockSpec((2 * rows, tile), lambda n, order: (0, n)) for _ in contexts],
            out_specs=[pl.BlockSpec((block, tile), lambda n, order: (0, n))] * 4,
            scratch_shapes=[pltpu.VMEM((height, tile), F32)],
        ),
        cost_estimate=FREE,
        compiler_params=pltpu.CompilerParams(vmem_limit_bytes=56 * 1024 * 1024),
        name="weight_product",
    )(order, *pieces, *contexts)


def per_device(
    context, residual, cotangent, out_proj, norm_gain, rewards, group_ids, lengths, destinations
):
    lanes = NX * NY * NC
    rows, width = residual.shape
    full = width * NZ
    x, y, c, z = (lax.axis_index(axis) for axis in ("x", "y", "c", "z"))

    top = width // 2
    far_top, far_bottom = forward_product(out_proj, context, (z + 2) % NZ, True)
    ready, _ = lax.optimization_barrier((context, far_top))
    pair = jnp.concatenate([context, shift(ready, "c", 1)], axis=0)
    sent_top, sent_bottom = shift(far_top, "z", 1), shift(far_bottom, "z", 3)
    near = forward_product(out_proj, context, (z + 1) % NZ, False, BF16)
    back = forward_product(out_proj, context, (z + 3) % NZ, False, BF16)
    sent_top, sent_bottom, near, back, pair = lax.optimization_barrier(
        (sent_top, sent_bottom, near, back, pair)
    )
    near, back = top_up(near, sent_top, back, sent_bottom)

    ready, _, _ = lax.optimization_barrier((context, near, back))
    own, gained_t = hidden_part(out_proj, ready, residual, cotangent, norm_gain, z)
    late_pair, _ = lax.optimization_barrier((pair, near))
    contexts = [pair] + [cross(late_pair, k, True) for k in (1, 2, 3)]
    hidden_t = own + shift(near, "z", 1).astype(F32) + shift(back, "z", 3).astype(F32)

    stats = jnp.stack(
        [jnp.sum(hidden_t * hidden_t, axis=0), jnp.sum(gained_t * hidden_t, axis=0)]
    )
    groups = rewards.shape[0] * lanes // GROUP
    member = (group_ids[:, None] == jnp.arange(groups)[None, :]).astype(F32)
    share, _ = lax.optimization_barrier((jnp.sum(member * rewards[:, None], axis=0), own))
    shares, _ = lax.optimization_barrier((all_shares(share), stats))
    group_total = jnp.sum(shares, axis=0)
    advantage = rewards - jnp.sum(member * group_total[None, :], axis=1) / GROUP
    scale = advantage * LMAX / (2.0 * lengths.astype(F32))
    live = jnp.arange(LMAX)[None, :] < lengths[:, None]
    row_weights = jnp.where(live, scale[:, None], F32(0.0)).reshape(-1).astype(BF16).astype(F32)

    stats = stats + shift(stats, "z", 1) + shift(stats, "z", 2) + shift(stats, "z", 3)
    inv_rms = lax.rsqrt(stats[0] / full + EPSILON)
    up_scale = inv_rms * row_weights
    hidden_scale = inv_rms**3 * (row_weights * stats[1]) / full
    grad_t = (up_scale[None, :] * gained_t - hidden_t * hidden_scale[None, :]).astype(BF16)
    grad_t, contexts[1], contexts[3] = lax.optimization_barrier((grad_t, contexts[1], contexts[3]))

    block = width // (NY * NC)

    def swap(*values):
        parted = [value.reshape(-1, NC, block, rows) for value in values]
        asked = [lax.dynamic_index_in_dim(value, 1 - c, 1, keepdims=False) for value in parted]
        return shift(jnp.concatenate(asked, axis=0).reshape(-1, rows), "c", 1)

    slots = slot_matrix(destinations[:, 0], lanes * PAIR, rows, 16)
    from_left, from_right = shift(grad_t, "z", 1), shift(grad_t, "z", 3)
    swapped = swap(grad_t)
    grad_rows, _ = lax.optimization_barrier((grad_t, swapped))
    d_residual = exchange(place_rows(slots, grad_rows), lanes)
    context_grad = context_product([grad_t], [z], out_proj)
    from_left, from_right, context_grad, swapped, contexts[2] = lax.optimization_barrier(
        (from_left, from_right, context_grad, swapped, contexts[2])
    )
    far_left, far_right = shift(from_left[:top], "z", 1), shift(from_right[top:], "z", 3)
    context_grad = context_product(
        [from_right, from_left], [(z + 1) % NZ, (z + 3) % NZ], out_proj, before=context_grad
    )
    far_left, far_right, context_grad = lax.optimization_barrier(
        (far_left, far_right, context_grad)
    )
    swapped_near = swap(from_right, from_left).reshape(8, block, rows)
    swapped_far = swap(far_left, far_right).reshape(4, block, rows)
    swapped_own = swapped.reshape(4, block, rows)

    def parted(*values):
        return [value.reshape(-1, NC, block, rows) for value in values]

    chunks = [parted(grad_t), parted(from_right), parted(far_left, far_right), parted(from_left)]
    siblings = [
        [(swapped_own, 0)], [(swapped_near[:4], 0)], [(swapped_far, 0)], [(swapped_near[4:], 0)]
    ]
    sends = lay_out((0, 1, 2, 3), chunks, siblings, x, y, c, z)
    far_left, far_right, sends = lax.optimization_barrier((far_left, far_right, sends))
    pieces = [sends[0]] + [cross(sends[k], k, True) for k in (1, 2, 3)]
    far_place = (z + 2) % NZ * 2
    placed = context_product(
        [far_left, far_right], [far_place, far_place + 1], out_proj, before=context_grad, slots=slots
    )
    placed, d_residual = lax.optimization_barrier((placed, learner_rows(d_residual)))
    d_context = exchange(placed, lanes)
    order = [jnp.where(c == 0, (y + k) % NY, (x + k - z) % NZ) for k in range(4)]
    d_out_proj, *parts = weight_product(pieces, contexts, jnp.stack(order), block)
    parts = [cross(part, k, False) for k, part in zip((1, 2, 3), parts)]
    for part in parts:
        d_out_proj = d_out_proj + part.astype(F32)
    return (learner_rows(d_context), d_residual, d_out_proj / lanes)


def solution(mesh):
    wide = Mesh(mesh.devices.reshape(NX, NY, NC, NZ), DP + ("z",))
    placed = (
        P(DP, "z"),
        P(DP, "z"),
        P(DP, "z"),
        P(None, "z"),
        P("z"),
        P(DP),
        P(DP),
        P(DP),
        P(DP, None),
    )
    return jax.shard_map(
        per_device,
        mesh=wide,
        in_specs=placed,
        out_specs=(P(DP, "z"), P(DP, "z"), P(DP, "z")),
        check_vma=False,
    )
```

```python
import jax
import jax.numpy as jnp
from jax import lax
from jax.experimental import pallas as pl
from jax.experimental.pallas import tpu as pltpu
from jax.sharding import Mesh
from jax.sharding import PartitionSpec as P

LMAX = 64
GROUP = 16
PAIR = 3
BLOCK_ROWS = 4
EPSILON = 1e-06
NX, NY, NC, NZ = 4, 4, 2, 4
DP = ("x", "y", "c")
F32 = jnp.float32
BF16 = jnp.bfloat16


def shift(value, axis, step):
    size = lax.axis_size(axis)
    return lax.ppermute(value, axis, [(i, (i + step) % size) for i in range(size)])


def pick(values, index):
    return lax.dynamic_index_in_dim(values, index, 0, keepdims=False)


def cross(value, step, first):
    pairs = []
    for x in range(NX):
        for y in range(NY):
            for c in range(NC):
                along_x = (c == 0) == first
                to = ((x + step) % NX, y, c) if along_x else (x, (y + step) % NY, c)
                pairs.append(((x * NY + y) * NC + c, (to[0] * NY + to[1]) * NC + to[2]))
    return lax.ppermute(value, DP, pairs)


def all_shares(value):
    copies = jnp.broadcast_to(value, (NX * NY * NC,) + value.shape)
    return lax.all_to_all(copies, DP, split_axis=0, concat_axis=0, tiled=True)


def slot_matrix(owner_dest, slots, rows, padded):
    count = owner_dest.shape[0]
    per_block = rows // count
    same = owner_dest[:, None] == owner_dest[None, :]
    earlier = jnp.arange(count)[None, :] < jnp.arange(count)[:, None]
    rank = jnp.sum((same & earlier).astype(jnp.int32), axis=1)
    target = owner_dest * padded + rank * per_block
    row_target = jnp.repeat(target, per_block) + jnp.tile(jnp.arange(per_block), count)
    return (jnp.arange(slots // PAIR * padded)[:, None] == row_target[None, :]).astype(BF16)


def exchange(packed, lanes):
    blocks = packed.reshape((lanes, packed.shape[0] // lanes, packed.shape[1]))
    return lax.all_to_all(blocks, DP, split_axis=0, concat_axis=0, tiled=True)


def learner_rows(got):
    kept = PAIR * BLOCK_ROWS
    return got[:, :kept].reshape(got.shape[0] * kept, got.shape[2])


FREE = pl.CostEstimate(flops=0, bytes_accessed=0, transcendentals=0)
PARAMS = pltpu.CompilerParams(vmem_limit_bytes=48 * 1024 * 1024)


def context_product(chunks, places, out_proj, before=None, slots=None):
    width, rows = out_proj.shape[1], chunks[0].shape[1]
    count, tile = len(chunks), 640
    dtype = F32 if slots is None else BF16

    def body(which, *refs):
        refs = list(refs)
        out_ref = refs.pop()
        total = sum(
            lax.dot_general(
                refs[i][...], refs[count + i][...], (((0,), (0,)), ((), ())), preferred_element_type=F32
            )
            for i in range(count)
        )
        if before is not None:
            total = total + refs[2 * count][...]
        if slots is not None:
            total = jnp.dot(refs[-1][...], total.astype(BF16), preferred_element_type=F32)
        out_ref[...] = total.astype(dtype)

    in_specs = [pl.BlockSpec(chunk.shape, lambda n, which: (0, 0)) for chunk in chunks]
    in_specs += [
        pl.BlockSpec((chunk.shape[0], tile), lambda n, which, i=i: (which[i], n))
        for i, chunk in enumerate(chunks)
    ]
    operands = list(chunks) + [out_proj] * count
    out_rows = rows
    if before is not None:
        in_specs.append(pl.BlockSpec((rows, tile), lambda n, which: (0, n)))
        operands.append(before)
    if slots is not None:
        in_specs.append(pl.BlockSpec(slots.shape, lambda n, which: (0, 0)))
        operands.append(slots)
        out_rows = slots.shape[0]
    return pl.pallas_call(
        body,
        out_shape=jax.ShapeDtypeStruct((out_rows, width), dtype),
        grid_spec=pltpu.PrefetchScalarGridSpec(
            num_scalar_prefetch=1,
            grid=(width // tile,),
            in_specs=in_specs,
            out_specs=pl.BlockSpec((out_rows, tile), lambda n, which: (0, n)),
        ),
        cost_estimate=FREE,
        compiler_params=PARAMS,
        name="context_product",
    )(jnp.stack(places), *operands)


def place_rows(slots, grad_t):
    def body(slots_ref, grad_ref, out_ref):
        out_ref[...] = lax.dot_general(
            slots_ref[...], grad_ref[...], (((1,), (1,)), ((), ())), preferred_element_type=F32
        ).astype(BF16)

    return pl.pallas_call(
        body,
        out_shape=jax.ShapeDtypeStruct((slots.shape[0], grad_t.shape[0]), BF16),
        cost_estimate=FREE,
        compiler_params=PARAMS,
        name="place_rows",
    )(slots, grad_t)


def top_up(near, near_part, back, back_part):
    height, rows = near_part.shape

    def body(*refs):
        for i in (0, 1):
            value = refs[2 * i][...].astype(F32) + refs[2 * i + 1][...].astype(F32)
            refs[4 + i][...] = value.astype(BF16)

    top = pl.BlockSpec((height, rows), lambda i: (0, 0))
    bottom = pl.BlockSpec((height, rows), lambda i: (1, 0))
    return pl.pallas_call(
        body,
        out_shape=[jax.ShapeDtypeStruct(near.shape, BF16)] * 2,
        grid=(1,),
        in_specs=[top, top, bottom, top],
        out_specs=[top, bottom],
        input_output_aliases={0: 0, 2: 1},
        cost_estimate=FREE,
        compiler_params=PARAMS,
        name="top_up",
    )(near, near_part, back, back_part)


def forward_product(out_proj, context, place, split, dtype=F32):
    rows, width = context.shape
    tile = width // 2

    def body(which, proj_ref, context_ref, *out_refs):
        value = lax.dot_general(
            proj_ref[...], context_ref[...], (((1,), (1,)), ((), ())), preferred_element_type=F32
        )
        if split:
            for half in (0, 1):

                @pl.when(pl.program_id(0) == half)
                def _(half=half):
                    out_refs[half][...] = value.astype(BF16)
        else:
            out_refs[0][...] = value.astype(dtype)

    half_spec = pl.BlockSpec((tile, rows), lambda i, which: (0, 0))
    out = pl.pallas_call(
        body,
        out_shape=[jax.ShapeDtypeStruct((tile, rows), BF16)] * 2
        if split
        else [jax.ShapeDtypeStruct((width, rows), dtype)],
        grid_spec=pltpu.PrefetchScalarGridSpec(
            num_scalar_prefetch=1,
            grid=(2,),
            in_specs=[
                pl.BlockSpec((tile, width), lambda i, which: (which[0] * 2 + i, 0)),
                pl.BlockSpec((rows, width), lambda i, which: (0, 0)),
            ],
            out_specs=[half_spec] * 2
            if split
            else [pl.BlockSpec((tile, rows), lambda i, which: (i, 0))],
        ),
        cost_estimate=FREE,
        compiler_params=PARAMS,
        name="forward_product",
    )(place.reshape(1), out_proj, context)
    return out if split else out[0]


def hidden_part(out_proj, context, residual, cotangent, norm_gain, place):
    rows, width = context.shape
    tile = width // 2

    def body(which, proj_ref, context_ref, residual_ref, cotangent_ref, gain_ref, hidden_ref, gained_ref):
        value = lax.dot_general(
            proj_ref[...], context_ref[...], (((1,), (1,)), ((), ())), preferred_element_type=F32
        )
        hidden_ref[...] = value + residual_ref[...].astype(F32).T
        gained_ref[...] = (gain_ref[...] * cotangent_ref[...].astype(F32)).T

    columns = pl.BlockSpec((rows, tile), lambda i, which: (0, i))
    return pl.pallas_call(
        body,
        out_shape=[jax.ShapeDtypeStruct((width, rows), F32)] * 2,
        grid_spec=pltpu.PrefetchScalarGridSpec(
            num_scalar_prefetch=1,
            grid=(2,),
            in_specs=[
                pl.BlockSpec((tile, width), lambda i, which: (which[0] * 2 + i, 0)),
                pl.BlockSpec((rows, width), lambda i, which: (0, 0)),
                columns,
                columns,
                pl.BlockSpec((1, tile), lambda i, which: (0, i)),
            ],
            out_specs=[pl.BlockSpec((tile, rows), lambda i, which: (i, 0))] * 2,
        ),
        cost_estimate=FREE,
        compiler_params=PARAMS,
        name="hidden_part",
    )(place.reshape(1), out_proj, context, residual, cotangent, norm_gain.reshape(1, width))


def lay_out(steps, chunks, siblings, x, y, c, z):
    block, rows = chunks[0][0].shape[-2:]
    arrays, places = [], []
    for value in [piece for pieces in chunks for piece in pieces] + [pieces[0][0] for pieces in siblings]:
        known = [i for i, other in enumerate(arrays) if other is value]
        places.append(known[0] if known else len(arrays))
        if not known:
            arrays.append(value)
    count_of = len(arrays)

    def body(where, *refs):
        ins, outs, sems = refs[:count_of], refs[count_of : count_of + len(steps)], refs[-1]
        wx, wy, wc, wz = (where[i] for i in range(4))

        def send(src, number, first, slots):
            pltpu.make_async_copy(
                src, outs[number].at[pl.ds(first, slots)], sems.at[number]
            ).start()

        position = 0
        for owner, group in enumerate((chunks, siblings)):
            for j, members in enumerate(group):
                per_piece = 4 // len(members)
                pieces = []
                for member in members:
                    ref = ins[places[position]]
                    position += 1
                    pieces.append(ref.at[:, wc] if owner == 0 else ref.at[pl.ds(member[1], 4)])
                for number, k in enumerate(steps):
                    wanted = lax.rem(wy + k, 4)

                    @pl.when((wc == 0) & (lax.rem(j + wz - wx + 4, 4) == k))
                    def _(pieces=pieces, per_piece=per_piece, number=number, owner=owner):
                        for i, piece in enumerate(pieces):
                            send(piece, number, owner * 4 + i * per_piece, per_piece)

                    for i, piece in enumerate(pieces):

                        @pl.when((wc == 1) & (wanted // per_piece == i))
                        def _(piece=piece, i=i, per_piece=per_piece, number=number, owner=owner,
                              j=j, wanted=wanted):
                            slot = wanted - i * per_piece
                            send(piece.at[pl.ds(slot, 1)], number, owner * 4 + j, 1)

        for number in range(len(steps)):
            pltpu.make_async_copy(outs[number], outs[number], sems.at[number]).wait()

    out = pl.pallas_call(
        body,
        out_shape=[jax.ShapeDtypeStruct((8, block, rows), BF16)] * len(steps),
        grid_spec=pltpu.PrefetchScalarGridSpec(
            num_scalar_prefetch=1,
            grid=(1,),
            in_specs=[pl.BlockSpec(memory_space=pl.ANY)] * count_of,
            out_specs=[pl.BlockSpec((8, block, rows), lambda i, where: (0, 0, 0))] * len(steps),
            scratch_shapes=[pltpu.SemaphoreType.DMA((len(steps),))],
        ),
        cost_estimate=FREE,
        compiler_params=pltpu.CompilerParams(vmem_limit_bytes=16 * 1024 * 1024),
        name="lay_out",
    )(jnp.stack([x, y, c, z]).astype(jnp.int32), *arrays)
    return [value.reshape(8 * block, rows) for value in out]


def weight_product(pieces, contexts, order, block):
    count, tile = len(pieces), 640
    height, rows = pieces[0].shape[0] // 2, pieces[0].shape[1]
    width = contexts[0].shape[1]

    def body(order_ref, *refs):
        outs, total = refs[2 * count : 2 * count + 4], refs[-1]
        total[...] = sum(
            jnp.dot(
                refs[i][core * height : (core + 1) * height, :],
                refs[count + i][core * rows : (core + 1) * rows, :],
                preferred_element_type=F32,
            )
            for i in range(count)
            for core in (0, 1)
        )
        for k in range(4):
            first = pl.multiple_of(order_ref[k] * block, block)
            outs[k][...] = total[pl.ds(first, block), :].astype(outs[k].dtype)

    return pl.pallas_call(
        body,
        out_shape=[jax.ShapeDtypeStruct((block, width), BF16 if k else F32) for k in range(4)],
        grid_spec=pltpu.PrefetchScalarGridSpec(
            num_scalar_prefetch=1,
            grid=(width // tile,),
            in_specs=[pl.BlockSpec((2 * height, rows), lambda n, order: (0, 0)) for _ in pieces]
            + [pl.BlockSpec((2 * rows, tile), lambda n, order: (0, n)) for _ in contexts],
            out_specs=[pl.BlockSpec((block, tile), lambda n, order: (0, n))] * 4,
            scratch_shapes=[pltpu.VMEM((height, tile), F32)],
        ),
        cost_estimate=FREE,
        compiler_params=pltpu.CompilerParams(vmem_limit_bytes=56 * 1024 * 1024),
        name="weight_product",
    )(order, *pieces, *contexts)


def per_device(
    context, residual, cotangent, out_proj, norm_gain, rewards, group_ids, lengths, destinations
):
    lanes = NX * NY * NC
    rows, width = residual.shape
    full = width * NZ
    x, y, c, z = (lax.axis_index(axis) for axis in ("x", "y", "c", "z"))

    top = width // 2
    far_top, far_bottom = forward_product(out_proj, context, (z + 2) % NZ, True)
    ready, _ = lax.optimization_barrier((context, far_top))
    pair = jnp.concatenate([context, shift(ready, "c", 1)], axis=0)
    sent_top, sent_bottom = shift(far_top, "z", 1), shift(far_bottom, "z", 3)
    near = forward_product(out_proj, context, (z + 1) % NZ, False, BF16)
    back = forward_product(out_proj, context, (z + 3) % NZ, False, BF16)
    sent_top, sent_bottom, near, back, pair = lax.optimization_barrier(
        (sent_top, sent_bottom, near, back, pair)
    )
    near, back = top_up(near, sent_top, back, sent_bottom)

    ready, _, _ = lax.optimization_barrier((context, near, back))
    own, gained_t = hidden_part(out_proj, ready, residual, cotangent, norm_gain, z)
    late_pair, _ = lax.optimization_barrier((pair, near))
    contexts = [pair, cross(late_pair, 1, True), None, cross(late_pair, 3, True)]
    hidden_t = own + shift(near, "z", 1).astype(F32) + shift(back, "z", 3).astype(F32)

    stats = jnp.stack(
        [jnp.sum(hidden_t * hidden_t, axis=0), jnp.sum(gained_t * hidden_t, axis=0)]
    )
    groups = rewards.shape[0] * lanes // GROUP
    member = (group_ids[:, None] == jnp.arange(groups)[None, :]).astype(F32)
    share, _ = lax.optimization_barrier((jnp.sum(member * rewards[:, None], axis=0), own))
    shares, _ = lax.optimization_barrier((all_shares(share), stats))
    group_total = jnp.sum(shares, axis=0)
    advantage = rewards - jnp.sum(member * group_total[None, :], axis=1) / GROUP
    scale = advantage * LMAX / (2.0 * lengths.astype(F32))
    live = jnp.arange(LMAX)[None, :] < lengths[:, None]
    row_weights = jnp.where(live, scale[:, None], F32(0.0)).reshape(-1).astype(BF16).astype(F32)

    stats = stats + shift(stats, "z", 1) + shift(stats, "z", 2) + shift(stats, "z", 3)
    inv_rms = lax.rsqrt(stats[0] / full + EPSILON)
    up_scale = inv_rms * row_weights
    hidden_scale = inv_rms**3 * (row_weights * stats[1]) / full
    grad_t = (up_scale[None, :] * gained_t - hidden_t * hidden_scale[None, :]).astype(BF16)
    grad_t, contexts[1], contexts[3] = lax.optimization_barrier((grad_t, contexts[1], contexts[3]))

    block = width // (NY * NC)

    def swap(*values):
        parted = [value.reshape(-1, NC, block, rows) for value in values]
        asked = [lax.dynamic_index_in_dim(value, 1 - c, 1, keepdims=False) for value in parted]
        return shift(jnp.concatenate(asked, axis=0).reshape(-1, rows), "c", 1)

    slots = slot_matrix(destinations[:, 0], lanes * PAIR, rows, 16)
    contexts[2] = cross(lax.optimization_barrier((pair, grad_t))[0], 2, True)
    from_left, from_right = shift(grad_t, "z", 1), shift(grad_t, "z", 3)
    swapped = swap(grad_t)
    grad_rows, _ = lax.optimization_barrier((grad_t, swapped))
    d_residual = exchange(place_rows(slots, grad_rows), lanes)
    context_grad = context_product([grad_t], [z], out_proj)
    from_left, from_right, context_grad, swapped = lax.optimization_barrier(
        (from_left, from_right, context_grad, swapped)
    )
    far_left, far_right = shift(from_left[:top], "z", 1), shift(from_right[top:], "z", 3)
    context_grad = context_product(
        [from_right, from_left], [(z + 1) % NZ, (z + 3) % NZ], out_proj, before=context_grad
    )
    far_left, far_right, context_grad, contexts[2] = lax.optimization_barrier(
        (far_left, far_right, context_grad, contexts[2])
    )
    swapped_near = swap(from_right, from_left).reshape(8, block, rows)
    swapped_far = swap(far_left, far_right).reshape(4, block, rows)
    swapped_own = swapped.reshape(4, block, rows)

    def parted(*values):
        return [value.reshape(-1, NC, block, rows) for value in values]

    chunks = [parted(grad_t), parted(from_right), parted(far_left, far_right), parted(from_left)]
    siblings = [
        [(swapped_own, 0)], [(swapped_near[:4], 0)], [(swapped_far, 0)], [(swapped_near[4:], 0)]
    ]
    sends = lay_out((0, 1, 2, 3), chunks, siblings, x, y, c, z)
    far_left, far_right, sends = lax.optimization_barrier((far_left, far_right, sends))
    pieces = [sends[0]] + [cross(sends[k], k, True) for k in (1, 2, 3)]
    far_place = (z + 2) % NZ * 2
    placed = context_product(
        [far_left, far_right], [far_place, far_place + 1], out_proj, before=context_grad, slots=slots
    )
    placed, d_residual = lax.optimization_barrier((placed, learner_rows(d_residual)))
    d_context = exchange(placed, lanes)
    order = [jnp.where(c == 0, (y + k) % NY, (x + k - z) % NZ) for k in range(4)]
    d_out_proj, *parts = weight_product(pieces, contexts, jnp.stack(order), block)
    parts = [cross(part, k, False) for k, part in zip((1, 2, 3), parts)]
    for part in parts:
        d_out_proj = d_out_proj + part.astype(F32)
    return (learner_rows(d_context), d_residual, d_out_proj / lanes)


def solution(mesh):
    wide = Mesh(mesh.devices.reshape(NX, NY, NC, NZ), DP + ("z",))
    placed = (
        P(DP, "z"),
        P(DP, "z"),
        P(DP, "z"),
        P(None, "z"),
        P("z"),
        P(DP),
        P(DP),
        P(DP),
        P(DP, None),
    )
    return jax.shard_map(
        per_device,
        mesh=wide,
        in_specs=placed,
        out_specs=(P(DP, "z"), P(DP, "z"), P(DP, "z")),
        check_vma=False,
    )
```

```python
import jax
import jax.numpy as jnp
from jax import lax
from jax.experimental import pallas as pl
from jax.experimental.pallas import tpu as pltpu
from jax.sharding import Mesh
from jax.sharding import PartitionSpec as P

LMAX = 64
GROUP = 16
PAIR = 3
BLOCK_ROWS = 4
EPSILON = 1e-06
NX, NY, NC, NZ = 4, 4, 2, 4
DP = ("x", "y", "c")
F32 = jnp.float32
BF16 = jnp.bfloat16


def shift(value, axis, step):
    size = lax.axis_size(axis)
    return lax.ppermute(value, axis, [(i, (i + step) % size) for i in range(size)])


def pick(values, index):
    return lax.dynamic_index_in_dim(values, index, 0, keepdims=False)


def cross(value, step, first):
    pairs = []
    for x in range(NX):
        for y in range(NY):
            for c in range(NC):
                along_x = (c == 0) == first
                to = ((x + step) % NX, y, c) if along_x else (x, (y + step) % NY, c)
                pairs.append(((x * NY + y) * NC + c, (to[0] * NY + to[1]) * NC + to[2]))
    return lax.ppermute(value, DP, pairs)


def all_shares(value):
    copies = jnp.broadcast_to(value, (NX * NY * NC,) + value.shape)
    return lax.all_to_all(copies, DP, split_axis=0, concat_axis=0, tiled=True)


def slot_matrix(owner_dest, slots, rows, padded):
    count = owner_dest.shape[0]
    per_block = rows // count
    same = owner_dest[:, None] == owner_dest[None, :]
    earlier = jnp.arange(count)[None, :] < jnp.arange(count)[:, None]
    rank = jnp.sum((same & earlier).astype(jnp.int32), axis=1)
    target = owner_dest * padded + rank * per_block
    row_target = jnp.repeat(target, per_block) + jnp.tile(jnp.arange(per_block), count)
    return (jnp.arange(slots // PAIR * padded)[:, None] == row_target[None, :]).astype(BF16)


def exchange(packed, lanes):
    blocks = packed.reshape((lanes, packed.shape[0] // lanes, packed.shape[1]))
    return lax.all_to_all(blocks, DP, split_axis=0, concat_axis=0, tiled=True)


def learner_rows(got):
    kept = PAIR * BLOCK_ROWS
    return got[:, :kept].reshape(got.shape[0] * kept, got.shape[2])


FREE = pl.CostEstimate(flops=0, bytes_accessed=0, transcendentals=0)
PARAMS = pltpu.CompilerParams(vmem_limit_bytes=48 * 1024 * 1024)


def context_product(chunks, places, out_proj, before=None, slots=None):
    width, rows = out_proj.shape[1], chunks[0].shape[1]
    count, tile = len(chunks), 640
    dtype = F32 if slots is None else BF16

    def body(which, *refs):
        refs = list(refs)
        out_ref = refs.pop()
        total = sum(
            lax.dot_general(
                refs[i][...], refs[count + i][...], (((0,), (0,)), ((), ())), preferred_element_type=F32
            )
            for i in range(count)
        )
        if before is not None:
            total = total + refs[2 * count][...]
        if slots is not None:
            total = jnp.dot(refs[-1][...], total.astype(BF16), preferred_element_type=F32)
        out_ref[...] = total.astype(dtype)

    in_specs = [pl.BlockSpec(chunk.shape, lambda n, which: (0, 0)) for chunk in chunks]
    in_specs += [
        pl.BlockSpec((chunk.shape[0], tile), lambda n, which, i=i: (which[i], n))
        for i, chunk in enumerate(chunks)
    ]
    operands = list(chunks) + [out_proj] * count
    out_rows = rows
    if before is not None:
        in_specs.append(pl.BlockSpec((rows, tile), lambda n, which: (0, n)))
        operands.append(before)
    if slots is not None:
        in_specs.append(pl.BlockSpec(slots.shape, lambda n, which: (0, 0)))
        operands.append(slots)
        out_rows = slots.shape[0]
    return pl.pallas_call(
        body,
        out_shape=jax.ShapeDtypeStruct((out_rows, width), dtype),
        grid_spec=pltpu.PrefetchScalarGridSpec(
            num_scalar_prefetch=1,
            grid=(width // tile,),
            in_specs=in_specs,
            out_specs=pl.BlockSpec((out_rows, tile), lambda n, which: (0, n)),
        ),
        cost_estimate=FREE,
        compiler_params=pltpu.CompilerParams(vmem_limit_bytes=42 * 1024 * 1024),
        name="context_product",
    )(jnp.stack(places), *operands)


def place_rows(slots, grad_t):
    def body(slots_ref, grad_ref, out_ref):
        out_ref[...] = lax.dot_general(
            slots_ref[...], grad_ref[...], (((1,), (1,)), ((), ())), preferred_element_type=F32
        ).astype(BF16)

    return pl.pallas_call(
        body,
        out_shape=jax.ShapeDtypeStruct((slots.shape[0], grad_t.shape[0]), BF16),
        cost_estimate=FREE,
        compiler_params=PARAMS,
        name="place_rows",
    )(slots, grad_t)


def top_up(near, near_part, back, back_part):
    height, rows = near_part.shape

    def body(*refs):
        for i in (0, 1):
            value = refs[2 * i][...].astype(F32) + refs[2 * i + 1][...].astype(F32)
            refs[4 + i][...] = value.astype(BF16)

    top = pl.BlockSpec((height, rows), lambda i: (0, 0))
    bottom = pl.BlockSpec((height, rows), lambda i: (1, 0))
    return pl.pallas_call(
        body,
        out_shape=[jax.ShapeDtypeStruct(near.shape, BF16)] * 2,
        grid=(1,),
        in_specs=[top, top, bottom, top],
        out_specs=[top, bottom],
        input_output_aliases={0: 0, 2: 1},
        cost_estimate=FREE,
        compiler_params=PARAMS,
        name="top_up",
    )(near, near_part, back, back_part)


def forward_product(out_proj, context, place, split, dtype=F32):
    rows, width = context.shape
    tile = width // 2

    def body(which, proj_ref, context_ref, *out_refs):
        value = lax.dot_general(
            proj_ref[...], context_ref[...], (((1,), (1,)), ((), ())), preferred_element_type=F32
        )
        if split:
            for half in (0, 1):

                @pl.when(pl.program_id(0) == half)
                def _(half=half):
                    out_refs[half][...] = value.astype(BF16)
        else:
            out_refs[0][...] = value.astype(dtype)

    half_spec = pl.BlockSpec((tile, rows), lambda i, which: (0, 0))
    out = pl.pallas_call(
        body,
        out_shape=[jax.ShapeDtypeStruct((tile, rows), BF16)] * 2
        if split
        else [jax.ShapeDtypeStruct((width, rows), dtype)],
        grid_spec=pltpu.PrefetchScalarGridSpec(
            num_scalar_prefetch=1,
            grid=(2,),
            in_specs=[
                pl.BlockSpec((tile, width), lambda i, which: (which[0] * 2 + i, 0)),
                pl.BlockSpec((rows, width), lambda i, which: (0, 0)),
            ],
            out_specs=[half_spec] * 2
            if split
            else [pl.BlockSpec((tile, rows), lambda i, which: (i, 0))],
        ),
        cost_estimate=FREE,
        compiler_params=PARAMS,
        name="forward_product",
    )(place.reshape(1), out_proj, context)
    return out if split else out[0]


def hidden_part(out_proj, context, residual, cotangent, norm_gain, place):
    rows, width = context.shape
    tile = width // 2

    def body(which, proj_ref, context_ref, residual_ref, cotangent_ref, gain_ref, hidden_ref, gained_ref):
        value = lax.dot_general(
            proj_ref[...], context_ref[...], (((1,), (1,)), ((), ())), preferred_element_type=F32
        )
        hidden_ref[...] = value + residual_ref[...].astype(F32).T
        gained_ref[...] = (gain_ref[...] * cotangent_ref[...].astype(F32)).T

    columns = pl.BlockSpec((rows, tile), lambda i, which: (0, i))
    return pl.pallas_call(
        body,
        out_shape=[jax.ShapeDtypeStruct((width, rows), F32)] * 2,
        grid_spec=pltpu.PrefetchScalarGridSpec(
            num_scalar_prefetch=1,
            grid=(2,),
            in_specs=[
                pl.BlockSpec((tile, width), lambda i, which: (which[0] * 2 + i, 0)),
                pl.BlockSpec((rows, width), lambda i, which: (0, 0)),
                columns,
                columns,
                pl.BlockSpec((1, tile), lambda i, which: (0, i)),
            ],
            out_specs=[pl.BlockSpec((tile, rows), lambda i, which: (i, 0))] * 2,
        ),
        cost_estimate=FREE,
        compiler_params=PARAMS,
        name="hidden_part",
    )(place.reshape(1), out_proj, context, residual, cotangent, norm_gain.reshape(1, width))


def lay_out(steps, chunks, siblings, x, y, c, z):
    block, rows = chunks[0][0].shape[-2:]
    arrays, places = [], []
    for value in [piece for pieces in chunks for piece in pieces] + [pieces[0][0] for pieces in siblings]:
        known = [i for i, other in enumerate(arrays) if other is value]
        places.append(known[0] if known else len(arrays))
        if not known:
            arrays.append(value)
    count_of = len(arrays)

    def body(where, *refs):
        ins, outs, sems = refs[:count_of], refs[count_of : count_of + len(steps)], refs[-1]
        wx, wy, wc, wz = (where[i] for i in range(4))

        def send(src, number, first, slots):
            pltpu.make_async_copy(
                src, outs[number].at[pl.ds(first, slots)], sems.at[number]
            ).start()

        position = 0
        for owner, group in enumerate((chunks, siblings)):
            for j, members in enumerate(group):
                per_piece = 4 // len(members)
                pieces = []
                for member in members:
                    ref = ins[places[position]]
                    position += 1
                    pieces.append(ref.at[:, wc] if owner == 0 else ref.at[pl.ds(member[1], 4)])
                for number, k in enumerate(steps):
                    wanted = lax.rem(wy + k, 4)

                    @pl.when((wc == 0) & (lax.rem(j + wz - wx + 4, 4) == k))
                    def _(pieces=pieces, per_piece=per_piece, number=number, owner=owner):
                        for i, piece in enumerate(pieces):
                            send(piece, number, owner * 4 + i * per_piece, per_piece)

                    for i, piece in enumerate(pieces):

                        @pl.when((wc == 1) & (wanted // per_piece == i))
                        def _(piece=piece, i=i, per_piece=per_piece, number=number, owner=owner,
                              j=j, wanted=wanted):
                            slot = wanted - i * per_piece
                            send(piece.at[pl.ds(slot, 1)], number, owner * 4 + j, 1)

        for number in range(len(steps)):
            pltpu.make_async_copy(outs[number], outs[number], sems.at[number]).wait()

    out = pl.pallas_call(
        body,
        out_shape=[jax.ShapeDtypeStruct((8, block, rows), BF16)] * len(steps),
        grid_spec=pltpu.PrefetchScalarGridSpec(
            num_scalar_prefetch=1,
            grid=(1,),
            in_specs=[pl.BlockSpec(memory_space=pl.ANY)] * count_of,
            out_specs=[pl.BlockSpec((8, block, rows), lambda i, where: (0, 0, 0))] * len(steps),
            scratch_shapes=[pltpu.SemaphoreType.DMA((len(steps),))],
        ),
        cost_estimate=FREE,
        compiler_params=pltpu.CompilerParams(vmem_limit_bytes=16 * 1024 * 1024),
        name="lay_out",
    )(jnp.stack([x, y, c, z]).astype(jnp.int32), *arrays)
    return [value.reshape(8 * block, rows) for value in out]


def weight_product(pieces, contexts, order, block):
    count, tile = len(pieces), 640
    height, rows = pieces[0].shape[0] // 2, pieces[0].shape[1]
    width = contexts[0].shape[1]

    def body(order_ref, *refs):
        outs, total = refs[2 * count : 2 * count + 4], refs[-1]
        total[...] = sum(
            jnp.dot(
                refs[i][core * height : (core + 1) * height, :],
                refs[count + i][core * rows : (core + 1) * rows, :],
                preferred_element_type=F32,
            )
            for i in range(count)
            for core in (0, 1)
        )
        for k in range(4):
            first = pl.multiple_of(order_ref[k] * block, block)
            outs[k][...] = total[pl.ds(first, block), :].astype(outs[k].dtype)

    return pl.pallas_call(
        body,
        out_shape=[jax.ShapeDtypeStruct((block, width), BF16 if k else F32) for k in range(4)],
        grid_spec=pltpu.PrefetchScalarGridSpec(
            num_scalar_prefetch=1,
            grid=(width // tile,),
            in_specs=[pl.BlockSpec((2 * height, rows), lambda n, order: (0, 0)) for _ in pieces]
            + [pl.BlockSpec((2 * rows, tile), lambda n, order: (0, n)) for _ in contexts],
            out_specs=[pl.BlockSpec((block, tile), lambda n, order: (0, n))] * 4,
            scratch_shapes=[pltpu.VMEM((height, tile), F32)],
        ),
        cost_estimate=FREE,
        compiler_params=pltpu.CompilerParams(vmem_limit_bytes=42 * 1024 * 1024),
        name="weight_product",
    )(order, *pieces, *contexts)


def per_device(
    context, residual, cotangent, out_proj, norm_gain, rewards, group_ids, lengths, destinations
):
    lanes = NX * NY * NC
    rows, width = residual.shape
    full = width * NZ
    x, y, c, z = (lax.axis_index(axis) for axis in ("x", "y", "c", "z"))

    top = width // 2
    far_top, far_bottom = forward_product(out_proj, context, (z + 2) % NZ, True)
    ready, _ = lax.optimization_barrier((context, far_top))
    pair = jnp.concatenate([context, shift(ready, "c", 1)], axis=0)
    sent_top, sent_bottom = shift(far_top, "z", 1), shift(far_bottom, "z", 3)
    near = forward_product(out_proj, context, (z + 1) % NZ, False, BF16)
    back = forward_product(out_proj, context, (z + 3) % NZ, False, BF16)
    sent_top, sent_bottom, near, back, pair = lax.optimization_barrier(
        (sent_top, sent_bottom, near, back, pair)
    )
    near, back = top_up(near, sent_top, back, sent_bottom)

    ready, _, _ = lax.optimization_barrier((context, near, back))
    own, gained_t = hidden_part(out_proj, ready, residual, cotangent, norm_gain, z)
    late_pair, _ = lax.optimization_barrier((pair, near))
    contexts = [pair] + [cross(late_pair, k, True) for k in (1, 2, 3)]
    hidden_t = own + shift(near, "z", 1).astype(F32) + shift(back, "z", 3).astype(F32)

    stats = jnp.stack(
        [jnp.sum(hidden_t * hidden_t, axis=0), jnp.sum(gained_t * hidden_t, axis=0)]
    )
    groups = rewards.shape[0] * lanes // GROUP
    member = (group_ids[:, None] == jnp.arange(groups)[None, :]).astype(F32)
    share, _ = lax.optimization_barrier((jnp.sum(member * rewards[:, None], axis=0), own))
    shares, _ = lax.optimization_barrier((all_shares(share), stats))
    group_total = jnp.sum(shares, axis=0)
    advantage = rewards - jnp.sum(member * group_total[None, :], axis=1) / GROUP
    scale = advantage * LMAX / (2.0 * lengths.astype(F32))
    live = jnp.arange(LMAX)[None, :] < lengths[:, None]
    row_weights = jnp.where(live, scale[:, None], F32(0.0)).reshape(-1).astype(BF16).astype(F32)

    stats = stats + shift(stats, "z", 1) + shift(stats, "z", 2) + shift(stats, "z", 3)
    inv_rms = lax.rsqrt(stats[0] / full + EPSILON)
    up_scale = inv_rms * row_weights
    hidden_scale = inv_rms**3 * (row_weights * stats[1]) / full
    grad_t = (up_scale[None, :] * gained_t - hidden_t * hidden_scale[None, :]).astype(BF16)
    grad_t, contexts[1], contexts[3] = lax.optimization_barrier((grad_t, contexts[1], contexts[3]))

    block = width // (NY * NC)

    def swap(*values):
        parted = [value.reshape(-1, NC, block, rows) for value in values]
        asked = [lax.dynamic_index_in_dim(value, 1 - c, 1, keepdims=False) for value in parted]
        return shift(jnp.concatenate(asked, axis=0).reshape(-1, rows), "c", 1)

    slots = slot_matrix(destinations[:, 0], lanes * PAIR, rows, 16)
    from_left, from_right = shift(grad_t, "z", 1), shift(grad_t, "z", 3)
    swapped = swap(grad_t)
    grad_rows, _ = lax.optimization_barrier((grad_t, swapped))
    d_residual = exchange(place_rows(slots, grad_rows), lanes)
    context_grad = context_product([grad_t], [z], out_proj)
    from_left, from_right, context_grad, swapped, contexts[2] = lax.optimization_barrier(
        (from_left, from_right, context_grad, swapped, contexts[2])
    )
    far_left, far_right = shift(from_left[:top], "z", 1), shift(from_right[top:], "z", 3)
    context_grad = context_product(
        [from_right, from_left], [(z + 1) % NZ, (z + 3) % NZ], out_proj, before=context_grad
    )
    far_left, far_right, context_grad = lax.optimization_barrier(
        (far_left, far_right, context_grad)
    )
    swapped_near = swap(from_right, from_left).reshape(8, block, rows)
    swapped_far = swap(far_left, far_right).reshape(4, block, rows)
    swapped_own = swapped.reshape(4, block, rows)

    def parted(*values):
        return [value.reshape(-1, NC, block, rows) for value in values]

    chunks = [parted(grad_t), parted(from_right), parted(far_left, far_right), parted(from_left)]
    siblings = [
        [(swapped_own, 0)], [(swapped_near[:4], 0)], [(swapped_far, 0)], [(swapped_near[4:], 0)]
    ]
    sends = lay_out((0, 1, 2, 3), chunks, siblings, x, y, c, z)
    far_left, far_right, sends = lax.optimization_barrier((far_left, far_right, sends))
    pieces = [sends[0]] + [cross(sends[k], k, True) for k in (1, 2, 3)]
    far_place = (z + 2) % NZ * 2
    placed = context_product(
        [far_left, far_right], [far_place, far_place + 1], out_proj, before=context_grad, slots=slots
    )
    placed, d_residual = lax.optimization_barrier((placed, learner_rows(d_residual)))
    d_context = exchange(placed, lanes)
    order = [jnp.where(c == 0, (y + k) % NY, (x + k - z) % NZ) for k in range(4)]
    d_out_proj, *parts = weight_product(pieces, contexts, jnp.stack(order), block)
    parts = [cross(part, k, False) for k, part in zip((1, 2, 3), parts)]
    for part in parts:
        d_out_proj = d_out_proj + part.astype(F32)
    return (learner_rows(d_context), d_residual, d_out_proj / lanes)


def solution(mesh):
    wide = Mesh(mesh.devices.reshape(NX, NY, NC, NZ), DP + ("z",))
    placed = (
        P(DP, "z"),
        P(DP, "z"),
        P(DP, "z"),
        P(None, "z"),
        P("z"),
        P(DP),
        P(DP),
        P(DP),
        P(DP, None),
    )
    return jax.shard_map(
        per_device,
        mesh=wide,
        in_specs=placed,
        out_specs=(P(DP, "z"), P(DP, "z"), P(DP, "z")),
        check_vma=False,
    )
```

```python
import jax
import jax.numpy as jnp
from jax import lax
from jax.experimental import pallas as pl
from jax.experimental.pallas import tpu as pltpu
from jax.sharding import Mesh
from jax.sharding import PartitionSpec as P

LMAX = 64
GROUP = 16
PAIR = 3
BLOCK_ROWS = 4
EPSILON = 1e-06
NX, NY, NC, NZ = 4, 4, 2, 4
DP = ("x", "y", "c")
F32 = jnp.float32
BF16 = jnp.bfloat16


def shift(value, axis, step):
    size = lax.axis_size(axis)
    return lax.ppermute(value, axis, [(i, (i + step) % size) for i in range(size)])


def pick(values, index):
    return lax.dynamic_index_in_dim(values, index, 0, keepdims=False)


def cross(value, step, first):
    pairs = []
    for x in range(NX):
        for y in range(NY):
            for c in range(NC):
                along_x = (c == 0) == first
                to = ((x + step) % NX, y, c) if along_x else (x, (y + step) % NY, c)
                pairs.append(((x * NY + y) * NC + c, (to[0] * NY + to[1]) * NC + to[2]))
    return lax.ppermute(value, DP, pairs)


def all_shares(value):
    copies = jnp.broadcast_to(value, (NX * NY * NC,) + value.shape)
    return lax.all_to_all(copies, DP, split_axis=0, concat_axis=0, tiled=True)


def slot_matrix(owner_dest, slots, rows, padded):
    count = owner_dest.shape[0]
    per_block = rows // count
    same = owner_dest[:, None] == owner_dest[None, :]
    earlier = jnp.arange(count)[None, :] < jnp.arange(count)[:, None]
    rank = jnp.sum((same & earlier).astype(jnp.int32), axis=1)
    target = owner_dest * padded + rank * per_block
    row_target = jnp.repeat(target, per_block) + jnp.tile(jnp.arange(per_block), count)
    return (jnp.arange(slots // PAIR * padded)[:, None] == row_target[None, :]).astype(BF16)


def exchange(packed, lanes):
    blocks = packed.reshape((lanes, packed.shape[0] // lanes, packed.shape[1]))
    return lax.all_to_all(blocks, DP, split_axis=0, concat_axis=0, tiled=True)


def learner_rows(got):
    kept = PAIR * BLOCK_ROWS
    return got[:, :kept].reshape(got.shape[0] * kept, got.shape[2])


FREE = pl.CostEstimate(flops=0, bytes_accessed=0, transcendentals=0)
PARAMS = pltpu.CompilerParams(vmem_limit_bytes=48 * 1024 * 1024)


def context_product(chunks, places, out_proj, before=None, slots=None):
    width, rows = out_proj.shape[1], chunks[0].shape[1]
    count, tile = len(chunks), 640
    dtype = F32 if slots is None else BF16

    def body(which, *refs):
        refs = list(refs)
        out_ref = refs.pop()
        total = sum(
            lax.dot_general(
                refs[i][...], refs[count + i][...], (((0,), (0,)), ((), ())), preferred_element_type=F32
            )
            for i in range(count)
        )
        if before is not None:
            total = total + refs[2 * count][...]
        if slots is not None:
            total = jnp.dot(refs[-1][...], total.astype(BF16), preferred_element_type=F32)
        out_ref[...] = total.astype(dtype)

    in_specs = [pl.BlockSpec(chunk.shape, lambda n, which: (0, 0)) for chunk in chunks]
    in_specs += [
        pl.BlockSpec((chunk.shape[0], tile), lambda n, which, i=i: (which[i], n))
        for i, chunk in enumerate(chunks)
    ]
    operands = list(chunks) + [out_proj] * count
    out_rows = rows
    if before is not None:
        in_specs.append(pl.BlockSpec((rows, tile), lambda n, which: (0, n)))
        operands.append(before)
    if slots is not None:
        in_specs.append(pl.BlockSpec(slots.shape, lambda n, which: (0, 0)))
        operands.append(slots)
        out_rows = slots.shape[0]
    return pl.pallas_call(
        body,
        out_shape=jax.ShapeDtypeStruct((out_rows, width), dtype),
        grid_spec=pltpu.PrefetchScalarGridSpec(
            num_scalar_prefetch=1,
            grid=(width // tile,),
            in_specs=in_specs,
            out_specs=pl.BlockSpec((out_rows, tile), lambda n, which: (0, n)),
        ),
        cost_estimate=FREE,
        compiler_params=pltpu.CompilerParams(vmem_limit_bytes=42 * 1024 * 1024),
        name="context_product",
    )(jnp.stack(places), *operands)


def place_rows(slots, grad_t):
    def body(slots_ref, grad_ref, out_ref):
        out_ref[...] = lax.dot_general(
            slots_ref[...], grad_ref[...], (((1,), (1,)), ((), ())), preferred_element_type=F32
        ).astype(BF16)

    return pl.pallas_call(
        body,
        out_shape=jax.ShapeDtypeStruct((slots.shape[0], grad_t.shape[0]), BF16),
        cost_estimate=FREE,
        compiler_params=PARAMS,
        name="place_rows",
    )(slots, grad_t)


def top_up(near, near_part, back, back_part):
    height, rows = near_part.shape

    def body(*refs):
        for i in (0, 1):
            value = refs[2 * i][...].astype(F32) + refs[2 * i + 1][...].astype(F32)
            refs[4 + i][...] = value.astype(BF16)

    top = pl.BlockSpec((height, rows), lambda i: (0, 0))
    bottom = pl.BlockSpec((height, rows), lambda i: (1, 0))
    return pl.pallas_call(
        body,
        out_shape=[jax.ShapeDtypeStruct(near.shape, BF16)] * 2,
        grid=(1,),
        in_specs=[top, top, bottom, top],
        out_specs=[top, bottom],
        input_output_aliases={0: 0, 2: 1},
        cost_estimate=FREE,
        compiler_params=PARAMS,
        name="top_up",
    )(near, near_part, back, back_part)


def forward_product(out_proj, context, place, split, dtype=F32):
    rows, width = context.shape
    tile = width // 2

    def body(which, proj_ref, context_ref, *out_refs):
        value = lax.dot_general(
            proj_ref[...], context_ref[...], (((1,), (1,)), ((), ())), preferred_element_type=F32
        )
        if split:
            for half in (0, 1):

                @pl.when(pl.program_id(0) == half)
                def _(half=half):
                    out_refs[half][...] = value.astype(BF16)
        else:
            out_refs[0][...] = value.astype(dtype)

    half_spec = pl.BlockSpec((tile, rows), lambda i, which: (0, 0))
    out = pl.pallas_call(
        body,
        out_shape=[jax.ShapeDtypeStruct((tile, rows), BF16)] * 2
        if split
        else [jax.ShapeDtypeStruct((width, rows), dtype)],
        grid_spec=pltpu.PrefetchScalarGridSpec(
            num_scalar_prefetch=1,
            grid=(2,),
            in_specs=[
                pl.BlockSpec((tile, width), lambda i, which: (which[0] * 2 + i, 0)),
                pl.BlockSpec((rows, width), lambda i, which: (0, 0)),
            ],
            out_specs=[half_spec] * 2
            if split
            else [pl.BlockSpec((tile, rows), lambda i, which: (i, 0))],
        ),
        cost_estimate=FREE,
        compiler_params=PARAMS,
        name="forward_product",
    )(place.reshape(1), out_proj, context)
    return out if split else out[0]


def hidden_part(out_proj, context, residual, cotangent, norm_gain, place):
    rows, width = context.shape
    tile = width // 2

    def body(which, proj_ref, context_ref, residual_ref, cotangent_ref, gain_ref, hidden_ref, gained_ref):
        value = lax.dot_general(
            proj_ref[...], context_ref[...], (((1,), (1,)), ((), ())), preferred_element_type=F32
        )
        hidden_ref[...] = value + residual_ref[...].astype(F32).T
        gained_ref[...] = (gain_ref[...] * cotangent_ref[...].astype(F32)).T

    columns = pl.BlockSpec((rows, tile), lambda i, which: (0, i))
    return pl.pallas_call(
        body,
        out_shape=[jax.ShapeDtypeStruct((width, rows), F32)] * 2,
        grid_spec=pltpu.PrefetchScalarGridSpec(
            num_scalar_prefetch=1,
            grid=(2,),
            in_specs=[
                pl.BlockSpec((tile, width), lambda i, which: (which[0] * 2 + i, 0)),
                pl.BlockSpec((rows, width), lambda i, which: (0, 0)),
                columns,
                columns,
                pl.BlockSpec((1, tile), lambda i, which: (0, i)),
            ],
            out_specs=[pl.BlockSpec((tile, rows), lambda i, which: (i, 0))] * 2,
        ),
        cost_estimate=FREE,
        compiler_params=PARAMS,
        name="hidden_part",
    )(place.reshape(1), out_proj, context, residual, cotangent, norm_gain.reshape(1, width))


def lay_out(steps, chunks, siblings, x, y, c, z):
    block, rows = chunks[0][0].shape[-2:]
    arrays, places = [], []
    for value in [piece for pieces in chunks for piece in pieces] + [pieces[0][0] for pieces in siblings]:
        known = [i for i, other in enumerate(arrays) if other is value]
        places.append(known[0] if known else len(arrays))
        if not known:
            arrays.append(value)
    count_of = len(arrays)

    def body(where, *refs):
        ins, outs, sems = refs[:count_of], refs[count_of : count_of + len(steps)], refs[-1]
        wx, wy, wc, wz = (where[i] for i in range(4))

        def send(src, number, first, slots):
            pltpu.make_async_copy(
                src, outs[number].at[pl.ds(first, slots)], sems.at[number]
            ).start()

        position = 0
        for owner, group in enumerate((chunks, siblings)):
            for j, members in enumerate(group):
                per_piece = 4 // len(members)
                pieces = []
                for member in members:
                    ref = ins[places[position]]
                    position += 1
                    pieces.append(ref.at[:, wc] if owner == 0 else ref.at[pl.ds(member[1], 4)])
                for number, k in enumerate(steps):
                    wanted = lax.rem(wy + k, 4)

                    @pl.when((wc == 0) & (lax.rem(j + wz - wx + 4, 4) == k))
                    def _(pieces=pieces, per_piece=per_piece, number=number, owner=owner):
                        for i, piece in enumerate(pieces):
                            send(piece, number, owner * 4 + i * per_piece, per_piece)

                    for i, piece in enumerate(pieces):

                        @pl.when((wc == 1) & (wanted // per_piece == i))
                        def _(piece=piece, i=i, per_piece=per_piece, number=number, owner=owner,
                              j=j, wanted=wanted):
                            slot = wanted - i * per_piece
                            send(piece.at[pl.ds(slot, 1)], number, owner * 4 + j, 1)

        for number in range(len(steps)):
            pltpu.make_async_copy(outs[number], outs[number], sems.at[number]).wait()

    out = pl.pallas_call(
        body,
        out_shape=[jax.ShapeDtypeStruct((8, block, rows), BF16)] * len(steps),
        grid_spec=pltpu.PrefetchScalarGridSpec(
            num_scalar_prefetch=1,
            grid=(1,),
            in_specs=[pl.BlockSpec(memory_space=pl.ANY)] * count_of,
            out_specs=[pl.BlockSpec((8, block, rows), lambda i, where: (0, 0, 0))] * len(steps),
            scratch_shapes=[pltpu.SemaphoreType.DMA((len(steps),))],
        ),
        cost_estimate=FREE,
        compiler_params=pltpu.CompilerParams(vmem_limit_bytes=16 * 1024 * 1024),
        name="lay_out",
    )(jnp.stack([x, y, c, z]).astype(jnp.int32), *arrays)
    return [value.reshape(8 * block, rows) for value in out]


def weight_product(pieces, contexts, order, block):
    count, tile = len(pieces), 640
    height, rows = pieces[0].shape[0] // 2, pieces[0].shape[1]
    width = contexts[0].shape[1]

    def body(order_ref, *refs):
        outs, total = refs[2 * count : 2 * count + 4], refs[-1]
        total[...] = sum(
            jnp.dot(
                refs[i][core * height : (core + 1) * height, :],
                refs[count + i][core * rows : (core + 1) * rows, :],
                preferred_element_type=F32,
            )
            for i in range(count)
            for core in (0, 1)
        )
        for k in range(4):
            first = pl.multiple_of(order_ref[k] * block, block)
            outs[k][...] = total[pl.ds(first, block), :].astype(outs[k].dtype)

    return pl.pallas_call(
        body,
        out_shape=[jax.ShapeDtypeStruct((block, width), BF16 if k else F32) for k in range(4)],
        grid_spec=pltpu.PrefetchScalarGridSpec(
            num_scalar_prefetch=1,
            grid=(width // tile,),
            in_specs=[pl.BlockSpec((2 * height, rows), lambda n, order: (0, 0)) for _ in pieces]
            + [pl.BlockSpec((2 * rows, tile), lambda n, order: (0, n)) for _ in contexts],
            out_specs=[pl.BlockSpec((block, tile), lambda n, order: (0, n))] * 4,
            scratch_shapes=[pltpu.VMEM((height, tile), F32)],
        ),
        cost_estimate=FREE,
        compiler_params=pltpu.CompilerParams(vmem_limit_bytes=42 * 1024 * 1024),
        name="weight_product",
    )(order, *pieces, *contexts)


def per_device(
    context, residual, cotangent, out_proj, norm_gain, rewards, group_ids, lengths, destinations
):
    lanes = NX * NY * NC
    rows, width = residual.shape
    full = width * NZ
    x, y, c, z = (lax.axis_index(axis) for axis in ("x", "y", "c", "z"))

    top = width // 2
    far_top, far_bottom = forward_product(out_proj, context, (z + 2) % NZ, True)
    ready, _ = lax.optimization_barrier((context, far_top))
    pair = jnp.concatenate([context, shift(ready, "c", 1)], axis=0)
    sent_top, sent_bottom = shift(far_top, "z", 1), shift(far_bottom, "z", 3)
    near = forward_product(out_proj, context, (z + 1) % NZ, False, BF16)
    back = forward_product(out_proj, context, (z + 3) % NZ, False, BF16)
    sent_top, sent_bottom, near, back, pair = lax.optimization_barrier(
        (sent_top, sent_bottom, near, back, pair)
    )
    near, back = top_up(near, sent_top, back, sent_bottom)

    ready, _, _ = lax.optimization_barrier((context, near, back))
    own, gained_t = hidden_part(out_proj, ready, residual, cotangent, norm_gain, z)
    late_pair, _ = lax.optimization_barrier((pair, near))
    contexts = [pair] + [cross(late_pair, k, True) for k in (1, 2, 3)]
    hidden_t = own + shift(near, "z", 1).astype(F32) + shift(back, "z", 3).astype(F32)

    stats = jnp.stack(
        [jnp.sum(hidden_t * hidden_t, axis=0), jnp.sum(gained_t * hidden_t, axis=0)]
    )
    groups = rewards.shape[0] * lanes // GROUP
    member = (group_ids[:, None] == jnp.arange(groups)[None, :]).astype(F32)
    share, _ = lax.optimization_barrier((jnp.sum(member * rewards[:, None], axis=0), own))
    shares, _ = lax.optimization_barrier((all_shares(share), stats))
    group_total = jnp.sum(shares, axis=0)
    advantage = rewards - jnp.sum(member * group_total[None, :], axis=1) / GROUP
    scale = advantage * LMAX / (2.0 * lengths.astype(F32))
    live = jnp.arange(LMAX)[None, :] < lengths[:, None]
    row_weights = jnp.where(live, scale[:, None], F32(0.0)).reshape(-1).astype(BF16).astype(F32)

    stats = stats + shift(stats, "z", 1) + shift(stats, "z", 2) + shift(stats, "z", 3)
    inv_rms = lax.rsqrt(stats[0] / full + EPSILON)
    up_scale = inv_rms * row_weights
    hidden_scale = inv_rms**3 * (row_weights * stats[1]) / full
    grad_t = (up_scale[None, :] * gained_t - hidden_t * hidden_scale[None, :]).astype(BF16)
    grad_t, contexts[1], contexts[3] = lax.optimization_barrier((grad_t, contexts[1], contexts[3]))

    block = width // (NY * NC)

    def swap(*values):
        parted = [value.reshape(-1, NC, block, rows) for value in values]
        asked = [lax.dynamic_index_in_dim(value, 1 - c, 1, keepdims=False) for value in parted]
        return shift(jnp.concatenate(asked, axis=0).reshape(-1, rows), "c", 1)

    slots = slot_matrix(destinations[:, 0], lanes * PAIR, rows, 16)
    from_left, from_right = shift(grad_t, "z", 1), shift(grad_t, "z", 3)
    swapped = swap(grad_t)
    grad_rows, _ = lax.optimization_barrier((grad_t, swapped))
    d_residual = exchange(place_rows(slots, grad_rows), lanes)
    context_grad = context_product([grad_t], [z], out_proj)
    from_left, from_right, context_grad, swapped, contexts[2] = lax.optimization_barrier(
        (from_left, from_right, context_grad, swapped, contexts[2])
    )
    far_left, far_right = shift(from_left[:top], "z", 1), shift(from_right[top:], "z", 3)
    context_grad = context_product(
        [from_right, from_left], [(z + 1) % NZ, (z + 3) % NZ], out_proj, before=context_grad
    )
    far_left, far_right, context_grad = lax.optimization_barrier(
        (far_left, far_right, context_grad)
    )
    swapped_near = swap(from_right, from_left).reshape(8, block, rows)
    swapped_far = swap(far_left, far_right).reshape(4, block, rows)
    swapped_own = swapped.reshape(4, block, rows)

    def parted(*values):
        return [value.reshape(-1, NC, block, rows) for value in values]

    chunks = [parted(grad_t), parted(from_right), parted(far_left, far_right), parted(from_left)]
    siblings = [
        [(swapped_own, 0)], [(swapped_near[:4], 0)], [(swapped_far, 0)], [(swapped_near[4:], 0)]
    ]
    sends = lay_out((0, 1, 2, 3), chunks, siblings, x, y, c, z)
    far_left, far_right, sends = lax.optimization_barrier((far_left, far_right, sends))
    pieces = [sends[0], None, None, None]
    for k in (2, 1, 3):
        pieces[k] = cross(sends[k], k, True)
    far_place = (z + 2) % NZ * 2
    placed = context_product(
        [far_left, far_right], [far_place, far_place + 1], out_proj, before=context_grad, slots=slots
    )
    placed, d_residual = lax.optimization_barrier((placed, learner_rows(d_residual)))
    d_context = exchange(placed, lanes)
    order = [jnp.where(c == 0, (y + k) % NY, (x + k - z) % NZ) for k in range(4)]
    d_out_proj, *parts = weight_product(pieces, contexts, jnp.stack(order), block)
    parts = [cross(parts[k - 1], k, False) for k in (2, 1, 3)]
    for part in parts:
        d_out_proj = d_out_proj + part.astype(F32)
    return (learner_rows(d_context), d_residual, d_out_proj / lanes)


def solution(mesh):
    wide = Mesh(mesh.devices.reshape(NX, NY, NC, NZ), DP + ("z",))
    placed = (
        P(DP, "z"),
        P(DP, "z"),
        P(DP, "z"),
        P(None, "z"),
        P("z"),
        P(DP),
        P(DP),
        P(DP),
        P(DP, None),
    )
    return jax.shard_map(
        per_device,
        mesh=wide,
        in_specs=placed,
        out_specs=(P(DP, "z"), P(DP, "z"), P(DP, "z")),
        check_vma=False,
    )
```

```python
import jax
import jax.numpy as jnp
from jax import lax
from jax.experimental import pallas as pl
from jax.experimental.pallas import tpu as pltpu
from jax.sharding import Mesh
from jax.sharding import PartitionSpec as P

LMAX = 64
GROUP = 16
PAIR = 3
BLOCK_ROWS = 4
EPSILON = 1e-06
NX, NY, NC, NZ = 4, 4, 2, 4
DP = ("x", "y", "c")
F32 = jnp.float32
BF16 = jnp.bfloat16


def shift(value, axis, step):
    size = lax.axis_size(axis)
    return lax.ppermute(value, axis, [(i, (i + step) % size) for i in range(size)])


def pick(values, index):
    return lax.dynamic_index_in_dim(values, index, 0, keepdims=False)


def cross(value, step, first):
    pairs = []
    for x in range(NX):
        for y in range(NY):
            for c in range(NC):
                along_x = (c == 0) == first
                to = ((x + step) % NX, y, c) if along_x else (x, (y + step) % NY, c)
                pairs.append(((x * NY + y) * NC + c, (to[0] * NY + to[1]) * NC + to[2]))
    return lax.ppermute(value, DP, pairs)


def all_shares(value):
    copies = jnp.broadcast_to(value, (NX * NY * NC,) + value.shape)
    return lax.all_to_all(copies, DP, split_axis=0, concat_axis=0, tiled=True)


def slot_matrix(owner_dest, slots, rows, padded):
    count = owner_dest.shape[0]
    per_block = rows // count
    same = owner_dest[:, None] == owner_dest[None, :]
    earlier = jnp.arange(count)[None, :] < jnp.arange(count)[:, None]
    rank = jnp.sum((same & earlier).astype(jnp.int32), axis=1)
    target = owner_dest * padded + rank * per_block
    row_target = jnp.repeat(target, per_block) + jnp.tile(jnp.arange(per_block), count)
    return (jnp.arange(slots // PAIR * padded)[:, None] == row_target[None, :]).astype(BF16)


def half_slot_matrix(owner_dest, lanes, rows):
    count = owner_dest.shape[0]
    per_block = rows // count
    kept = PAIR * per_block
    same = owner_dest[:, None] == owner_dest[None, :]
    earlier = jnp.arange(count)[None, :] < jnp.arange(count)[:, None]
    rank = jnp.sum((same & earlier).astype(jnp.int32), axis=1)
    target = owner_dest * 2 * kept + rank * per_block
    row_target = jnp.repeat(target, per_block) + jnp.tile(jnp.arange(per_block), count)
    row_target = row_target[None, None, :] + kept * jnp.arange(2)[:, None, None]
    return (jnp.arange(lanes * 2 * kept)[None, :, None] == row_target).astype(BF16)


def exchange(packed, lanes):
    blocks = packed.reshape((lanes, packed.shape[0] // lanes, packed.shape[1]))
    return lax.all_to_all(blocks, DP, split_axis=0, concat_axis=0, tiled=True)


def learner_rows(got):
    kept = PAIR * BLOCK_ROWS
    return got[:, :kept].reshape(got.shape[0] * kept, got.shape[2])


FREE = pl.CostEstimate(flops=0, bytes_accessed=0, transcendentals=0)
PARAMS = pltpu.CompilerParams(vmem_limit_bytes=48 * 1024 * 1024)


def context_product(chunks, places, out_proj, before=None, slots=None):
    width, rows = out_proj.shape[1], chunks[0].shape[1]
    count, tile = len(chunks), 640
    dtype = F32 if slots is None else BF16

    def body(which, *refs):
        refs = list(refs)
        out_ref = refs.pop()
        total = sum(
            lax.dot_general(
                refs[i][...], refs[count + i][...], (((0,), (0,)), ((), ())), preferred_element_type=F32
            )
            for i in range(count)
        )
        if before is not None:
            total = total + refs[2 * count][...]
        if slots is None:
            out_ref[...] = total
            return
        total = jnp.dot(refs[-1][0], total.astype(BF16), preferred_element_type=F32)

        @pl.when(pl.program_id(0) == 0)
        def _():
            out_ref[...] = total.astype(BF16)

        @pl.when(pl.program_id(0) == 1)
        def _():
            out_ref[...] += total.astype(BF16)

    in_specs = [pl.BlockSpec(chunk.shape, lambda n, which: (0, 0)) for chunk in chunks]
    in_specs += [
        pl.BlockSpec((chunk.shape[0], tile), lambda n, which, i=i: (which[i], n))
        for i, chunk in enumerate(chunks)
    ]
    operands = list(chunks) + [out_proj] * count
    out_rows = rows
    if before is not None:
        in_specs.append(pl.BlockSpec((rows, tile), lambda n, which: (0, n)))
        operands.append(before)
    if slots is not None:
        in_specs.append(pl.BlockSpec((1,) + slots.shape[1:], lambda n, which: (n, 0, 0)))
        operands.append(slots)
        out_rows = slots.shape[1]
    return pl.pallas_call(
        body,
        out_shape=jax.ShapeDtypeStruct((out_rows, width if slots is None else tile), dtype),
        grid_spec=pltpu.PrefetchScalarGridSpec(
            num_scalar_prefetch=1,
            grid=(width // tile,),
            in_specs=in_specs,
            out_specs=pl.BlockSpec(
                (out_rows, tile), lambda n, which: (0, n if slots is None else 0)
            ),
        ),
        cost_estimate=FREE,
        compiler_params=pltpu.CompilerParams(vmem_limit_bytes=42 * 1024 * 1024),
        name="context_product",
    )(jnp.stack(places), *operands)


def unfold(got):
    lanes, folded, half = got.shape
    kept = folded // 2

    def body(got_ref, out_ref):
        shape = (lanes * kept, lanes * folded)
        row = lax.broadcasted_iota(jnp.int32, shape, 0)
        column = lax.broadcasted_iota(jnp.int32, shape, 1)
        for h in (0, 1):
            wanted = row + kept * (((row * 5462) >> 16) + h)
            taken = jnp.where(column == wanted, F32(1.0), F32(0.0)).astype(BF16)
            out_ref[:, h * half : (h + 1) * half] = jnp.dot(
                taken, got_ref[...], preferred_element_type=F32
            ).astype(BF16)

    return pl.pallas_call(
        body,
        out_shape=jax.ShapeDtypeStruct((lanes * kept, 2 * half), BF16),
        cost_estimate=FREE,
        compiler_params=pltpu.CompilerParams(vmem_limit_bytes=16 * 1024 * 1024),
        name="unfold",
    )(got.reshape(lanes * folded, half))


def place_rows(slots, grad_t):
    def body(slots_ref, grad_ref, out_ref):
        out_ref[...] = lax.dot_general(
            slots_ref[...], grad_ref[...], (((1,), (1,)), ((), ())), preferred_element_type=F32
        ).astype(BF16)

    return pl.pallas_call(
        body,
        out_shape=jax.ShapeDtypeStruct((slots.shape[0], grad_t.shape[0]), BF16),
        cost_estimate=FREE,
        compiler_params=PARAMS,
        name="place_rows",
    )(slots, grad_t)


def top_up(near, near_part, back, back_part):
    height, rows = near_part.shape

    def body(*refs):
        for i in (0, 1):
            value = refs[2 * i][...].astype(F32) + refs[2 * i + 1][...].astype(F32)
            refs[4 + i][...] = value.astype(BF16)

    top = pl.BlockSpec((height, rows), lambda i: (0, 0))
    bottom = pl.BlockSpec((height, rows), lambda i: (1, 0))
    return pl.pallas_call(
        body,
        out_shape=[jax.ShapeDtypeStruct(near.shape, BF16)] * 2,
        grid=(1,),
        in_specs=[top, top, bottom, top],
        out_specs=[top, bottom],
        input_output_aliases={0: 0, 2: 1},
        cost_estimate=FREE,
        compiler_params=PARAMS,
        name="top_up",
    )(near, near_part, back, back_part)


def forward_product(out_proj, context, place, split, dtype=F32):
    rows, width = context.shape
    tile = width // 2

    def body(which, proj_ref, context_ref, *out_refs):
        value = lax.dot_general(
            proj_ref[...], context_ref[...], (((1,), (1,)), ((), ())), preferred_element_type=F32
        )
        if split:
            for half in (0, 1):

                @pl.when(pl.program_id(0) == half)
                def _(half=half):
                    out_refs[half][...] = value.astype(BF16)
        else:
            out_refs[0][...] = value.astype(dtype)

    half_spec = pl.BlockSpec((tile, rows), lambda i, which: (0, 0))
    out = pl.pallas_call(
        body,
        out_shape=[jax.ShapeDtypeStruct((tile, rows), BF16)] * 2
        if split
        else [jax.ShapeDtypeStruct((width, rows), dtype)],
        grid_spec=pltpu.PrefetchScalarGridSpec(
            num_scalar_prefetch=1,
            grid=(2,),
            in_specs=[
                pl.BlockSpec((tile, width), lambda i, which: (which[0] * 2 + i, 0)),
                pl.BlockSpec((rows, width), lambda i, which: (0, 0)),
            ],
            out_specs=[half_spec] * 2
            if split
            else [pl.BlockSpec((tile, rows), lambda i, which: (i, 0))],
        ),
        cost_estimate=FREE,
        compiler_params=PARAMS,
        name="forward_product",
    )(place.reshape(1), out_proj, context)
    return out if split else out[0]


def hidden_part(out_proj, context, residual, cotangent, norm_gain, place):
    rows, width = context.shape
    tile = width // 2

    def body(which, proj_ref, context_ref, residual_ref, cotangent_ref, gain_ref, hidden_ref, gained_ref):
        value = lax.dot_general(
            proj_ref[...], context_ref[...], (((1,), (1,)), ((), ())), preferred_element_type=F32
        )
        hidden_ref[...] = value + residual_ref[...].astype(F32).T
        gained_ref[...] = (gain_ref[...] * cotangent_ref[...].astype(F32)).T

    columns = pl.BlockSpec((rows, tile), lambda i, which: (0, i))
    return pl.pallas_call(
        body,
        out_shape=[jax.ShapeDtypeStruct((width, rows), F32)] * 2,
        grid_spec=pltpu.PrefetchScalarGridSpec(
            num_scalar_prefetch=1,
            grid=(2,),
            in_specs=[
                pl.BlockSpec((tile, width), lambda i, which: (which[0] * 2 + i, 0)),
                pl.BlockSpec((rows, width), lambda i, which: (0, 0)),
                columns,
                columns,
                pl.BlockSpec((1, tile), lambda i, which: (0, i)),
            ],
            out_specs=[pl.BlockSpec((tile, rows), lambda i, which: (i, 0))] * 2,
        ),
        cost_estimate=FREE,
        compiler_params=PARAMS,
        name="hidden_part",
    )(place.reshape(1), out_proj, context, residual, cotangent, norm_gain.reshape(1, width))


def lay_out(steps, chunks, siblings, x, y, c, z):
    block, rows = chunks[0][0].shape[-2:]
    arrays, places = [], []
    for value in [piece for pieces in chunks for piece in pieces] + [pieces[0][0] for pieces in siblings]:
        known = [i for i, other in enumerate(arrays) if other is value]
        places.append(known[0] if known else len(arrays))
        if not known:
            arrays.append(value)
    count_of = len(arrays)

    def body(where, *refs):
        ins, outs, sems = refs[:count_of], refs[count_of : count_of + len(steps)], refs[-1]
        wx, wy, wc, wz = (where[i] for i in range(4))

        def send(src, number, first, slots):
            pltpu.make_async_copy(
                src, outs[number].at[pl.ds(first, slots)], sems.at[number]
            ).start()

        position = 0
        for owner, group in enumerate((chunks, siblings)):
            for j, members in enumerate(group):
                per_piece = 4 // len(members)
                pieces = []
                for member in members:
                    ref = ins[places[position]]
                    position += 1
                    pieces.append(ref.at[:, wc] if owner == 0 else ref.at[pl.ds(member[1], 4)])
                for number, k in enumerate(steps):
                    wanted = lax.rem(wy + k, 4)

                    @pl.when((wc == 0) & (lax.rem(j + wz - wx + 4, 4) == k))
                    def _(pieces=pieces, per_piece=per_piece, number=number, owner=owner):
                        for i, piece in enumerate(pieces):
                            send(piece, number, owner * 4 + i * per_piece, per_piece)

                    for i, piece in enumerate(pieces):

                        @pl.when((wc == 1) & (wanted // per_piece == i))
                        def _(piece=piece, i=i, per_piece=per_piece, number=number, owner=owner,
                              j=j, wanted=wanted):
                            slot = wanted - i * per_piece
                            send(piece.at[pl.ds(slot, 1)], number, owner * 4 + j, 1)

        for number in range(len(steps)):
            pltpu.make_async_copy(outs[number], outs[number], sems.at[number]).wait()

    out = pl.pallas_call(
        body,
        out_shape=[jax.ShapeDtypeStruct((8, block, rows), BF16)] * len(steps),
        grid_spec=pltpu.PrefetchScalarGridSpec(
            num_scalar_prefetch=1,
            grid=(1,),
            in_specs=[pl.BlockSpec(memory_space=pl.ANY)] * count_of,
            out_specs=[pl.BlockSpec((8, block, rows), lambda i, where: (0, 0, 0))] * len(steps),
            scratch_shapes=[pltpu.SemaphoreType.DMA((len(steps),))],
        ),
        cost_estimate=FREE,
        compiler_params=pltpu.CompilerParams(vmem_limit_bytes=16 * 1024 * 1024),
        name="lay_out",
    )(jnp.stack([x, y, c, z]).astype(jnp.int32), *arrays)
    return [value.reshape(8 * block, rows) for value in out]


def weight_product(pieces, contexts, order, block):
    count, tile = len(pieces), 640
    height, rows = pieces[0].shape[0] // 2, pieces[0].shape[1]
    width = contexts[0].shape[1]

    def body(order_ref, *refs):
        outs, total = refs[2 * count : 2 * count + 4], refs[-1]
        total[...] = sum(
            jnp.dot(
                refs[i][core * height : (core + 1) * height, :],
                refs[count + i][core * rows : (core + 1) * rows, :],
                preferred_element_type=F32,
            )
            for i in range(count)
            for core in (0, 1)
        )
        for k in range(4):
            first = pl.multiple_of(order_ref[k] * block, block)
            outs[k][...] = total[pl.ds(first, block), :].astype(outs[k].dtype)

    return pl.pallas_call(
        body,
        out_shape=[jax.ShapeDtypeStruct((block, width), BF16 if k else F32) for k in range(4)],
        grid_spec=pltpu.PrefetchScalarGridSpec(
            num_scalar_prefetch=1,
            grid=(width // tile,),
            in_specs=[pl.BlockSpec((2 * height, rows), lambda n, order: (0, 0)) for _ in pieces]
            + [pl.BlockSpec((2 * rows, tile), lambda n, order: (0, n)) for _ in contexts],
            out_specs=[pl.BlockSpec((block, tile), lambda n, order: (0, n))] * 4,
            scratch_shapes=[pltpu.VMEM((height, tile), F32)],
        ),
        cost_estimate=FREE,
        compiler_params=pltpu.CompilerParams(vmem_limit_bytes=42 * 1024 * 1024),
        name="weight_product",
    )(order, *pieces, *contexts)


def per_device(
    context, residual, cotangent, out_proj, norm_gain, rewards, group_ids, lengths, destinations
):
    lanes = NX * NY * NC
    rows, width = residual.shape
    full = width * NZ
    x, y, c, z = (lax.axis_index(axis) for axis in ("x", "y", "c", "z"))

    top = width // 2
    far_top, far_bottom = forward_product(out_proj, context, (z + 2) % NZ, True)
    ready, _ = lax.optimization_barrier((context, far_top))
    pair = jnp.concatenate([context, shift(ready, "c", 1)], axis=0)
    sent_top, sent_bottom = shift(far_top, "z", 1), shift(far_bottom, "z", 3)
    near = forward_product(out_proj, context, (z + 1) % NZ, False, BF16)
    back = forward_product(out_proj, context, (z + 3) % NZ, False, BF16)
    sent_top, sent_bottom, near, back, pair = lax.optimization_barrier(
        (sent_top, sent_bottom, near, back, pair)
    )
    near, back = top_up(near, sent_top, back, sent_bottom)

    ready, _, _ = lax.optimization_barrier((context, near, back))
    own, gained_t = hidden_part(out_proj, ready, residual, cotangent, norm_gain, z)
    late_pair, _ = lax.optimization_barrier((pair, near))
    contexts = [pair] + [cross(late_pair, k, True) for k in (1, 2, 3)]
    hidden_t = own + shift(near, "z", 1).astype(F32) + shift(back, "z", 3).astype(F32)

    stats = jnp.stack(
        [jnp.sum(hidden_t * hidden_t, axis=0), jnp.sum(gained_t * hidden_t, axis=0)]
    )
    groups = rewards.shape[0] * lanes // GROUP
    member = (group_ids[:, None] == jnp.arange(groups)[None, :]).astype(F32)
    share, _ = lax.optimization_barrier((jnp.sum(member * rewards[:, None], axis=0), own))
    shares, _ = lax.optimization_barrier((all_shares(share), stats))
    group_total = jnp.sum(shares, axis=0)
    advantage = rewards - jnp.sum(member * group_total[None, :], axis=1) / GROUP
    scale = advantage * LMAX / (2.0 * lengths.astype(F32))
    live = jnp.arange(LMAX)[None, :] < lengths[:, None]
    row_weights = jnp.where(live, scale[:, None], F32(0.0)).reshape(-1).astype(BF16).astype(F32)

    stats = stats + shift(stats, "z", 1) + shift(stats, "z", 2) + shift(stats, "z", 3)
    inv_rms = lax.rsqrt(stats[0] / full + EPSILON)
    up_scale = inv_rms * row_weights
    hidden_scale = inv_rms**3 * (row_weights * stats[1]) / full
    grad_t = (up_scale[None, :] * gained_t - hidden_t * hidden_scale[None, :]).astype(BF16)
    grad_t, contexts[1], contexts[3] = lax.optimization_barrier((grad_t, contexts[1], contexts[3]))

    block = width // (NY * NC)

    def swap(*values):
        parted = [value.reshape(-1, NC, block, rows) for value in values]
        asked = [lax.dynamic_index_in_dim(value, 1 - c, 1, keepdims=False) for value in parted]
        return shift(jnp.concatenate(asked, axis=0).reshape(-1, rows), "c", 1)

    half_slots = half_slot_matrix(destinations[:, 0], lanes, rows)
    slots = slot_matrix(destinations[:, 0], lanes * PAIR, rows, 16)
    from_left, from_right = shift(grad_t, "z", 1), shift(grad_t, "z", 3)
    swapped = swap(grad_t)
    grad_rows, _ = lax.optimization_barrier((grad_t, swapped))
    d_residual = exchange(place_rows(slots, grad_rows), lanes)
    context_grad = context_product([grad_t], [z], out_proj)
    from_left, from_right, context_grad, swapped, contexts[2] = lax.optimization_barrier(
        (from_left, from_right, context_grad, swapped, contexts[2])
    )
    far_left, far_right = shift(from_left[:top], "z", 1), shift(from_right[top:], "z", 3)
    context_grad = context_product(
        [from_right, from_left], [(z + 1) % NZ, (z + 3) % NZ], out_proj, before=context_grad
    )
    far_left, far_right, context_grad = lax.optimization_barrier(
        (far_left, far_right, context_grad)
    )
    swapped_near = swap(from_right, from_left).reshape(8, block, rows)
    swapped_far = swap(far_left, far_right).reshape(4, block, rows)
    swapped_own = swapped.reshape(4, block, rows)

    def parted(*values):
        return [value.reshape(-1, NC, block, rows) for value in values]

    chunks = [parted(grad_t), parted(from_right), parted(far_left, far_right), parted(from_left)]
    siblings = [
        [(swapped_own, 0)], [(swapped_near[:4], 0)], [(swapped_far, 0)], [(swapped_near[4:], 0)]
    ]
    sends = lay_out((0, 1, 2, 3), chunks, siblings, x, y, c, z)
    far_left, far_right, sends = lax.optimization_barrier((far_left, far_right, sends))
    pieces = [sends[0], None, None, None]
    for k in (2, 1, 3):
        pieces[k] = cross(sends[k], k, True)
    far_place = (z + 2) % NZ * 2
    placed = context_product(
        [far_left, far_right], [far_place, far_place + 1], out_proj, before=context_grad, slots=half_slots
    )
    placed, d_residual = lax.optimization_barrier((placed, learner_rows(d_residual)))
    d_context = exchange(placed, lanes)
    order = [jnp.where(c == 0, (y + k) % NY, (x + k - z) % NZ) for k in range(4)]
    d_out_proj, *parts = weight_product(pieces, contexts, jnp.stack(order), block)
    parts = [cross(parts[k - 1], k, False) for k in (2, 1, 3)]
    parts, d_context = lax.optimization_barrier((parts, unfold(d_context)))
    for part in parts:
        d_out_proj = d_out_proj + part.astype(F32)
    return (d_context, d_residual, d_out_proj / lanes)


def solution(mesh):
    wide = Mesh(mesh.devices.reshape(NX, NY, NC, NZ), DP + ("z",))
    placed = (
        P(DP, "z"),
        P(DP, "z"),
        P(DP, "z"),
        P(None, "z"),
        P("z"),
        P(DP),
        P(DP),
        P(DP),
        P(DP, None),
    )
    return jax.shard_map(
        per_device,
        mesh=wide,
        in_specs=placed,
        out_specs=(P(DP, "z"), P(DP, "z"), P(DP, "z")),
        check_vma=False,
    )
```

```python
import jax
import jax.numpy as jnp
from jax import lax
from jax.experimental import pallas as pl
from jax.experimental.pallas import tpu as pltpu
from jax.sharding import Mesh
from jax.sharding import PartitionSpec as P

LMAX = 64
GROUP = 16
PAIR = 3
BLOCK_ROWS = 4
EPSILON = 1e-06
NX, NY, NC, NZ = 4, 4, 2, 4
DP = ("x", "y", "c")
F32 = jnp.float32
BF16 = jnp.bfloat16


def shift(value, axis, step):
    size = lax.axis_size(axis)
    return lax.ppermute(value, axis, [(i, (i + step) % size) for i in range(size)])


def pick(values, index):
    return lax.dynamic_index_in_dim(values, index, 0, keepdims=False)


def cross(value, step, first):
    pairs = []
    for x in range(NX):
        for y in range(NY):
            for c in range(NC):
                along_x = (c == 0) == first
                to = ((x + step) % NX, y, c) if along_x else (x, (y + step) % NY, c)
                pairs.append(((x * NY + y) * NC + c, (to[0] * NY + to[1]) * NC + to[2]))
    return lax.ppermute(value, DP, pairs)


def all_shares(value):
    copies = jnp.broadcast_to(value, (NX * NY * NC,) + value.shape)
    return lax.all_to_all(copies, DP, split_axis=0, concat_axis=0, tiled=True)


def slot_matrix(owner_dest, slots, rows, padded):
    count = owner_dest.shape[0]
    per_block = rows // count
    same = owner_dest[:, None] == owner_dest[None, :]
    earlier = jnp.arange(count)[None, :] < jnp.arange(count)[:, None]
    rank = jnp.sum((same & earlier).astype(jnp.int32), axis=1)
    target = owner_dest * padded + rank * per_block
    row_target = jnp.repeat(target, per_block) + jnp.tile(jnp.arange(per_block), count)
    return (jnp.arange(slots // PAIR * padded)[:, None] == row_target[None, :]).astype(BF16)


def half_slot_matrix(owner_dest, lanes, rows):
    count = owner_dest.shape[0]
    per_block = rows // count
    kept = PAIR * per_block
    same = owner_dest[:, None] == owner_dest[None, :]
    earlier = jnp.arange(count)[None, :] < jnp.arange(count)[:, None]
    rank = jnp.sum((same & earlier).astype(jnp.int32), axis=1)
    target = owner_dest * 2 * kept + rank * per_block
    row_target = jnp.repeat(target, per_block) + jnp.tile(jnp.arange(per_block), count)
    row_target = row_target[None, None, :] + kept * jnp.arange(2)[:, None, None]
    return (jnp.arange(lanes * 2 * kept)[None, :, None] == row_target).astype(BF16)


def exchange(packed, lanes):
    blocks = packed.reshape((lanes, packed.shape[0] // lanes, packed.shape[1]))
    return lax.all_to_all(blocks, DP, split_axis=0, concat_axis=0, tiled=True)


def learner_rows(got):
    kept = PAIR * BLOCK_ROWS
    return got[:, :kept].reshape(got.shape[0] * kept, got.shape[2])


FREE = pl.CostEstimate(flops=0, bytes_accessed=0, transcendentals=0)
PARAMS = pltpu.CompilerParams(vmem_limit_bytes=48 * 1024 * 1024)


def context_product(chunks, places, out_proj, before=None, slots=None):
    width, rows = out_proj.shape[1], chunks[0].shape[1]
    count, tile = len(chunks), 640
    dtype = F32 if slots is None else BF16

    def body(which, *refs):
        refs = list(refs)
        out_ref = refs.pop()
        total = sum(
            lax.dot_general(
                refs[i][...], refs[count + i][...], (((0,), (0,)), ((), ())), preferred_element_type=F32
            )
            for i in range(count)
        )
        if before is not None:
            total = total + refs[2 * count][...]
        if slots is None:
            out_ref[...] = total
            return
        total = jnp.dot(refs[-1][0], total.astype(BF16), preferred_element_type=F32)

        @pl.when(pl.program_id(0) == 0)
        def _():
            out_ref[...] = total.astype(BF16)

        @pl.when(pl.program_id(0) == 1)
        def _():
            out_ref[...] += total.astype(BF16)

    in_specs = [pl.BlockSpec(chunk.shape, lambda n, which: (0, 0)) for chunk in chunks]
    in_specs += [
        pl.BlockSpec((chunk.shape[0], tile), lambda n, which, i=i: (which[i], n))
        for i, chunk in enumerate(chunks)
    ]
    operands = list(chunks) + [out_proj] * count
    out_rows = rows
    if before is not None:
        in_specs.append(pl.BlockSpec((rows, tile), lambda n, which: (0, n)))
        operands.append(before)
    if slots is not None:
        in_specs.append(pl.BlockSpec((1,) + slots.shape[1:], lambda n, which: (n, 0, 0)))
        operands.append(slots)
        out_rows = slots.shape[1]
    return pl.pallas_call(
        body,
        out_shape=jax.ShapeDtypeStruct((out_rows, width if slots is None else tile), dtype),
        grid_spec=pltpu.PrefetchScalarGridSpec(
            num_scalar_prefetch=1,
            grid=(width // tile,),
            in_specs=in_specs,
            out_specs=pl.BlockSpec(
                (out_rows, tile), lambda n, which: (0, n if slots is None else 0)
            ),
        ),
        cost_estimate=FREE,
        compiler_params=pltpu.CompilerParams(vmem_limit_bytes=42 * 1024 * 1024),
        name="context_product",
    )(jnp.stack(places), *operands)


def unfold(got):
    lanes, folded, half = got.shape
    kept = folded // 2

    def body(got_ref, out_ref):
        shape = (lanes * kept, lanes * folded)
        row = lax.broadcasted_iota(jnp.int32, shape, 0)
        column = lax.broadcasted_iota(jnp.int32, shape, 1)
        for h in (0, 1):
            wanted = row + kept * (((row * 5462) >> 16) + h)
            taken = jnp.where(column == wanted, F32(1.0), F32(0.0)).astype(BF16)
            out_ref[:, h * half : (h + 1) * half] = jnp.dot(
                taken, got_ref[...], preferred_element_type=F32
            ).astype(BF16)

    return pl.pallas_call(
        body,
        out_shape=jax.ShapeDtypeStruct((lanes * kept, 2 * half), BF16),
        cost_estimate=FREE,
        compiler_params=pltpu.CompilerParams(vmem_limit_bytes=16 * 1024 * 1024),
        name="unfold",
    )(got.reshape(lanes * folded, half))


def place_rows(slots, grad_t):
    def body(slots_ref, grad_ref, out_ref):
        out_ref[...] = lax.dot_general(
            slots_ref[...], grad_ref[...], (((1,), (1,)), ((), ())), preferred_element_type=F32
        ).astype(BF16)

    return pl.pallas_call(
        body,
        out_shape=jax.ShapeDtypeStruct((slots.shape[0], grad_t.shape[0]), BF16),
        cost_estimate=FREE,
        compiler_params=PARAMS,
        name="place_rows",
    )(slots, grad_t)


def top_up(near, near_part, back, back_part):
    height, rows = near_part.shape

    def body(*refs):
        for i in (0, 1):
            value = refs[2 * i][...].astype(F32) + refs[2 * i + 1][...].astype(F32)
            refs[4 + i][...] = value.astype(BF16)

    top = pl.BlockSpec((height, rows), lambda i: (0, 0))
    bottom = pl.BlockSpec((height, rows), lambda i: (1, 0))
    return pl.pallas_call(
        body,
        out_shape=[jax.ShapeDtypeStruct(near.shape, BF16)] * 2,
        grid=(1,),
        in_specs=[top, top, bottom, top],
        out_specs=[top, bottom],
        input_output_aliases={0: 0, 2: 1},
        cost_estimate=FREE,
        compiler_params=PARAMS,
        name="top_up",
    )(near, near_part, back, back_part)


def forward_product(out_proj, context, place, split, dtype=F32):
    rows, width = context.shape
    tile = width // 2

    def body(which, proj_ref, context_ref, *out_refs):
        value = lax.dot_general(
            proj_ref[...], context_ref[...], (((1,), (1,)), ((), ())), preferred_element_type=F32
        )
        if split:
            for half in (0, 1):

                @pl.when(pl.program_id(0) == half)
                def _(half=half):
                    out_refs[half][...] = value.astype(BF16)
        else:
            out_refs[0][...] = value.astype(dtype)

    half_spec = pl.BlockSpec((tile, rows), lambda i, which: (0, 0))
    out = pl.pallas_call(
        body,
        out_shape=[jax.ShapeDtypeStruct((tile, rows), BF16)] * 2
        if split
        else [jax.ShapeDtypeStruct((width, rows), dtype)],
        grid_spec=pltpu.PrefetchScalarGridSpec(
            num_scalar_prefetch=1,
            grid=(2,),
            in_specs=[
                pl.BlockSpec((tile, width), lambda i, which: (which[0] * 2 + i, 0)),
                pl.BlockSpec((rows, width), lambda i, which: (0, 0)),
            ],
            out_specs=[half_spec] * 2
            if split
            else [pl.BlockSpec((tile, rows), lambda i, which: (i, 0))],
        ),
        cost_estimate=FREE,
        compiler_params=PARAMS,
        name="forward_product",
    )(place.reshape(1), out_proj, context)
    return out if split else out[0]


def hidden_part(out_proj, context, residual, cotangent, norm_gain, place):
    rows, width = context.shape
    tile = width // 2

    def body(which, proj_ref, context_ref, residual_ref, cotangent_ref, gain_ref, hidden_ref, gained_ref):
        value = lax.dot_general(
            proj_ref[...], context_ref[...], (((1,), (1,)), ((), ())), preferred_element_type=F32
        )
        hidden_ref[...] = value + residual_ref[...].astype(F32).T
        gained_ref[...] = (gain_ref[...] * cotangent_ref[...].astype(F32)).T

    columns = pl.BlockSpec((rows, tile), lambda i, which: (0, i))
    return pl.pallas_call(
        body,
        out_shape=[jax.ShapeDtypeStruct((width, rows), F32)] * 2,
        grid_spec=pltpu.PrefetchScalarGridSpec(
            num_scalar_prefetch=1,
            grid=(2,),
            in_specs=[
                pl.BlockSpec((tile, width), lambda i, which: (which[0] * 2 + i, 0)),
                pl.BlockSpec((rows, width), lambda i, which: (0, 0)),
                columns,
                columns,
                pl.BlockSpec((1, tile), lambda i, which: (0, i)),
            ],
            out_specs=[pl.BlockSpec((tile, rows), lambda i, which: (i, 0))] * 2,
        ),
        cost_estimate=FREE,
        compiler_params=PARAMS,
        name="hidden_part",
    )(place.reshape(1), out_proj, context, residual, cotangent, norm_gain.reshape(1, width))


def lay_out(steps, chunks, siblings, x, y, c, z):
    block, rows = chunks[0][0].shape[-2:]
    arrays, places = [], []
    for value in [piece for pieces in chunks for piece in pieces] + [pieces[0][0] for pieces in siblings]:
        known = [i for i, other in enumerate(arrays) if other is value]
        places.append(known[0] if known else len(arrays))
        if not known:
            arrays.append(value)
    count_of = len(arrays)

    def body(where, *refs):
        ins, outs, sems = refs[:count_of], refs[count_of : count_of + len(steps)], refs[-1]
        wx, wy, wc, wz = (where[i] for i in range(4))

        def send(src, number, first, slots):
            pltpu.make_async_copy(
                src, outs[number].at[pl.ds(first, slots)], sems.at[number]
            ).start()

        position = 0
        for owner, group in enumerate((chunks, siblings)):
            for j, members in enumerate(group):
                per_piece = 4 // len(members)
                pieces = []
                for member in members:
                    ref = ins[places[position]]
                    position += 1
                    pieces.append(ref.at[:, wc] if owner == 0 else ref.at[pl.ds(member[1], 4)])
                for number, k in enumerate(steps):
                    wanted = lax.rem(wy + k, 4)

                    @pl.when((wc == 0) & (lax.rem(j + wz - wx + 4, 4) == k))
                    def _(pieces=pieces, per_piece=per_piece, number=number, owner=owner):
                        for i, piece in enumerate(pieces):
                            send(piece, number, owner * 4 + i * per_piece, per_piece)

                    for i, piece in enumerate(pieces):

                        @pl.when((wc == 1) & (wanted // per_piece == i))
                        def _(piece=piece, i=i, per_piece=per_piece, number=number, owner=owner,
                              j=j, wanted=wanted):
                            slot = wanted - i * per_piece
                            send(piece.at[pl.ds(slot, 1)], number, owner * 4 + j, 1)

        for number in range(len(steps)):
            pltpu.make_async_copy(outs[number], outs[number], sems.at[number]).wait()

    out = pl.pallas_call(
        body,
        out_shape=[jax.ShapeDtypeStruct((8, block, rows), BF16)] * len(steps),
        grid_spec=pltpu.PrefetchScalarGridSpec(
            num_scalar_prefetch=1,
            grid=(1,),
            in_specs=[pl.BlockSpec(memory_space=pl.ANY)] * count_of,
            out_specs=[pl.BlockSpec((8, block, rows), lambda i, where: (0, 0, 0))] * len(steps),
            scratch_shapes=[pltpu.SemaphoreType.DMA((len(steps),))],
        ),
        cost_estimate=FREE,
        compiler_params=pltpu.CompilerParams(vmem_limit_bytes=16 * 1024 * 1024),
        name="lay_out",
    )(jnp.stack([x, y, c, z]).astype(jnp.int32), *arrays)
    return [value.reshape(8 * block, rows) for value in out]


def weight_product(pieces, contexts, order, block):
    count, tile = len(pieces), 640
    height, rows = pieces[0].shape[0] // 2, pieces[0].shape[1]
    width = contexts[0].shape[1]

    def body(order_ref, *refs):
        outs, total = refs[2 * count : 2 * count + 4], refs[-1]
        total[...] = sum(
            jnp.dot(
                refs[i][core * height : (core + 1) * height, :],
                refs[count + i][core * rows : (core + 1) * rows, :],
                preferred_element_type=F32,
            )
            for i in range(count)
            for core in (0, 1)
        )
        for k in range(4):
            first = pl.multiple_of(order_ref[k] * block, block)
            outs[k][...] = total[pl.ds(first, block), :].astype(outs[k].dtype)

    return pl.pallas_call(
        body,
        out_shape=[jax.ShapeDtypeStruct((block, width), BF16 if k else F32) for k in range(4)],
        grid_spec=pltpu.PrefetchScalarGridSpec(
            num_scalar_prefetch=1,
            grid=(width // tile,),
            in_specs=[pl.BlockSpec((2 * height, rows), lambda n, order: (0, 0)) for _ in pieces]
            + [pl.BlockSpec((2 * rows, tile), lambda n, order: (0, n)) for _ in contexts],
            out_specs=[pl.BlockSpec((block, tile), lambda n, order: (0, n))] * 4,
            scratch_shapes=[pltpu.VMEM((height, tile), F32)],
        ),
        cost_estimate=FREE,
        compiler_params=pltpu.CompilerParams(vmem_limit_bytes=56 * 1024 * 1024),
        name="weight_product",
    )(order, *pieces, *contexts)


def per_device(
    context, residual, cotangent, out_proj, norm_gain, rewards, group_ids, lengths, destinations
):
    lanes = NX * NY * NC
    rows, width = residual.shape
    full = width * NZ
    x, y, c, z = (lax.axis_index(axis) for axis in ("x", "y", "c", "z"))

    top = width // 2
    far_top, far_bottom = forward_product(out_proj, context, (z + 2) % NZ, True)
    ready, _ = lax.optimization_barrier((context, far_top))
    pair = jnp.concatenate([context, shift(ready, "c", 1)], axis=0)
    sent_top, sent_bottom = shift(far_top, "z", 1), shift(far_bottom, "z", 3)
    near = forward_product(out_proj, context, (z + 1) % NZ, False, BF16)
    back = forward_product(out_proj, context, (z + 3) % NZ, False, BF16)
    sent_top, sent_bottom, near, back, pair = lax.optimization_barrier(
        (sent_top, sent_bottom, near, back, pair)
    )
    near, back = top_up(near, sent_top, back, sent_bottom)

    ready, _, _ = lax.optimization_barrier((context, near, back))
    own, gained_t = hidden_part(out_proj, ready, residual, cotangent, norm_gain, z)
    late_pair, _ = lax.optimization_barrier((pair, near))
    contexts = [pair] + [cross(late_pair, k, True) for k in (1, 2, 3)]
    hidden_t = own + shift(near, "z", 1).astype(F32) + shift(back, "z", 3).astype(F32)

    stats = jnp.stack(
        [jnp.sum(hidden_t * hidden_t, axis=0), jnp.sum(gained_t * hidden_t, axis=0)]
    )
    groups = rewards.shape[0] * lanes // GROUP
    member = (group_ids[:, None] == jnp.arange(groups)[None, :]).astype(F32)
    share, _ = lax.optimization_barrier((jnp.sum(member * rewards[:, None], axis=0), own))
    shares, _ = lax.optimization_barrier((all_shares(share), stats))
    group_total = jnp.sum(shares, axis=0)
    advantage = rewards - jnp.sum(member * group_total[None, :], axis=1) / GROUP
    scale = advantage * LMAX / (2.0 * lengths.astype(F32))
    live = jnp.arange(LMAX)[None, :] < lengths[:, None]
    row_weights = jnp.where(live, scale[:, None], F32(0.0)).reshape(-1).astype(BF16).astype(F32)

    stats = stats + shift(stats, "z", 1) + shift(stats, "z", 2) + shift(stats, "z", 3)
    inv_rms = lax.rsqrt(stats[0] / full + EPSILON)
    up_scale = inv_rms * row_weights
    hidden_scale = inv_rms**3 * (row_weights * stats[1]) / full
    grad_t = (up_scale[None, :] * gained_t - hidden_t * hidden_scale[None, :]).astype(BF16)
    grad_t, contexts[1], contexts[3] = lax.optimization_barrier((grad_t, contexts[1], contexts[3]))

    block = width // (NY * NC)

    def swap(*values):
        parted = [value.reshape(-1, NC, block, rows) for value in values]
        asked = [lax.dynamic_index_in_dim(value, 1 - c, 1, keepdims=False) for value in parted]
        return shift(jnp.concatenate(asked, axis=0).reshape(-1, rows), "c", 1)

    half_slots = half_slot_matrix(destinations[:, 0], lanes, rows)
    slots = slot_matrix(destinations[:, 0], lanes * PAIR, rows, 16)
    from_left, from_right = shift(grad_t, "z", 1), shift(grad_t, "z", 3)
    swapped = swap(grad_t)
    grad_rows, _ = lax.optimization_barrier((grad_t, swapped))
    d_residual = exchange(place_rows(slots, grad_rows), lanes)
    context_grad = context_product([grad_t], [z], out_proj)
    from_left, from_right, context_grad, swapped, contexts[2] = lax.optimization_barrier(
        (from_left, from_right, context_grad, swapped, contexts[2])
    )
    far_left, far_right = shift(from_left[:top], "z", 1), shift(from_right[top:], "z", 3)
    context_grad = context_product(
        [from_right, from_left], [(z + 1) % NZ, (z + 3) % NZ], out_proj, before=context_grad
    )
    far_left, far_right, context_grad = lax.optimization_barrier(
        (far_left, far_right, context_grad)
    )
    swapped_near = swap(from_right, from_left).reshape(8, block, rows)
    swapped_far = swap(far_left, far_right).reshape(4, block, rows)
    swapped_own = swapped.reshape(4, block, rows)

    def parted(*values):
        return [value.reshape(-1, NC, block, rows) for value in values]

    chunks = [parted(grad_t), parted(from_right), parted(far_left, far_right), parted(from_left)]
    siblings = [
        [(swapped_own, 0)], [(swapped_near[:4], 0)], [(swapped_far, 0)], [(swapped_near[4:], 0)]
    ]
    sends = lay_out((0, 1, 2, 3), chunks, siblings, x, y, c, z)
    far_left, far_right, sends = lax.optimization_barrier((far_left, far_right, sends))
    pieces = [sends[0], None, None, None]
    for k in (2, 1, 3):
        pieces[k] = cross(sends[k], k, True)
    far_place = (z + 2) % NZ * 2
    placed = context_product(
        [far_left, far_right], [far_place, far_place + 1], out_proj, before=context_grad, slots=half_slots
    )
    placed, d_residual = lax.optimization_barrier((placed, learner_rows(d_residual)))
    d_context = exchange(placed, lanes)
    order = [jnp.where(c == 0, (y + k) % NY, (x + k - z) % NZ) for k in range(4)]
    d_out_proj, *parts = weight_product(pieces, contexts, jnp.stack(order), block)
    parts = [cross(parts[k - 1], k, False) for k in (2, 1, 3)]
    parts, d_context = lax.optimization_barrier((parts, unfold(d_context)))
    for part in parts:
        d_out_proj = d_out_proj + part.astype(F32)
    return (d_context, d_residual, d_out_proj / lanes)


def solution(mesh):
    wide = Mesh(mesh.devices.reshape(NX, NY, NC, NZ), DP + ("z",))
    placed = (
        P(DP, "z"),
        P(DP, "z"),
        P(DP, "z"),
        P(None, "z"),
        P("z"),
        P(DP),
        P(DP),
        P(DP),
        P(DP, None),
    )
    return jax.shard_map(
        per_device,
        mesh=wide,
        in_specs=placed,
        out_specs=(P(DP, "z"), P(DP, "z"), P(DP, "z")),
        check_vma=False,
    )
```
